32 devices in a mesh: leaf: 8 (over z, y), vec: 4 (over x, core).
Axes of the slice: x: 2, y: 2, z: 4, core: 2. Of those that a mesh axis runs over, the one named last changes fastest.
Arguments:
- values: bfloat16 [64, 65536], P('vec', 'leaf'), may hold values from -6 to 6
- coords: float32 [3, 65536], P(None, 'leaf'), may hold values from 0 to 16, as said below
- basis: bfloat16 [512, 64, 128], P(('leaf', 'vec')), may hold values from -0.5 to 0.5
- transfer: bfloat16 [1016, 4096], P('leaf'), may hold values from -0.625 to 0.625
- coupling: bfloat16 [24, 4096], replicated, may hold values from -0.15625 to 0.15625
- near_src: int32 [512, 27], P('leaf'), may hold values from -1 to 511, as said below
- far_src: int32 [1016, 24], P('leaf'), may hold values from -1 to 1015, as said below
- far_cls: int32 [1016, 24], P('leaf'), may hold values from 0 to 23
- top_src: int32 [12, 24], replicated, may hold values from -1 to 7, as said below
- top_cls: int32 [12, 24], replicated, may hold values from 0 to 23
Outputs:
- result: bfloat16 [64, 65536], P('vec', 'leaf')
The draws below stay inside these ranges and needn't reach their ends.
Inputs may be any that keep to these rules, and one draw needn't show every extreme that they name: `coords`: leaf box t owns the unit cube with corner (t % 16, (t % 64) // 16, t // 64), and its points lie in that cube. `near_src`: slot 9 (c + 1) + 3 (b + 1) + (a + 1) of row t names the leaf box whose cube lies at offset (a, b, c) from the cube of t, for a, b, c in -1, 0, 1, or holds -1 where no such box exists or the pair is left out; slot 13 always holds t; the first leaf box of every subtree keeps every neighbour that exists. `far_src`: row p * 127 + s belongs to slot s of subtree p. At most 24 entries of a row are live, the rest are -1, and the row of the first leaf box of every subtree but the first has 24. A live entry p * 127 + s names slot s of subtree p: a node of the row's level, on the row's subtree or one beside it, two to 13 nodes away along that level. The rows of the roots are all -1. `top_src`: rows 0 to 7 belong to the roots and name roots; row 8 + q belongs to top node q and names top nodes. At most 24 entries of a row are live, -1 marks the rest, and a live entry lies two or more places from the row's own node.
All inputs are finite; a program needn't handle non-finite values.
Results may differ from the reference program's by a relative error of at most 0.02125.
Values may be sent and summed in bfloat16 or wider, within the bound.
No kernel may reach another device: no remote copies, remote signals or barrier semaphores. Data moves between devices by JAX's collectives and lax.ppermute only.
A program may use at most 64 MiB of HBM per device.

```python
import jax
import jax.numpy as jnp
from jax import lax

M = 128
K = 64
NV = 64
NS = 27
FS = 24
NCLASS = 24
LB = 64
ROW = 16
REACH = 13
TB = 127
SUBTREES = 8
TOPS = 12
NB = 512
NPTS = 65536
N_LEAF = 8


def pick_sources(key, target, usable, slots):
    row_total = target.shape[0]
    span_width = target.shape[1]
    candidate = jnp.arange(span_width, dtype=jnp.int32)[None, :]
    score = jax.random.randint(key, (row_total, span_width), 0, 1 << 20, dtype=jnp.int32) * span_width + candidate
    score = jnp.where(usable, score, (1 << 20) * span_width + candidate)
    unused, chosen = lax.top_k(-score, slots)
    return (jnp.take_along_axis(target, chosen, axis=1), jnp.take_along_axis(usable, chosen, axis=1))


def draw_coords(key, part):
    key = jax.random.fold_in(key, 11)
    box_index = jnp.arange(NB * M, dtype=jnp.int32) // M
    first_axis = box_index % ROW
    second_axis = box_index % LB // ROW
    layer_index = box_index // LB
    centers = jnp.stack([first_axis, second_axis, layer_index]).astype(jnp.float32)
    offsets = jax.random.uniform(key, (3, NB * M), jnp.float32)
    return centers + offsets


def draw_near_src(key, part):
    key = jax.random.fold_in(key, 23)
    target = jnp.arange(NB, dtype=jnp.int32)
    first_axis = target % ROW
    second_axis = target % LB // ROW
    layer_index = target // LB
    slot_index = jnp.arange(27, dtype=jnp.int32)
    step_a = slot_index % 3 - 1
    step_b = slot_index // 3 % 3 - 1
    step_c = slot_index // 9 - 1
    new_a = first_axis[:, None] + step_a[None, :]
    new_b = second_axis[:, None] + step_b[None, :]
    new_c = layer_index[:, None] + step_c[None, :]
    inside = (new_a >= 0) & (new_a < ROW) & (new_b >= 0) & (new_b < LB // ROW) & (new_c >= 0) & (new_c < NB // LB)
    keep_flags = jax.random.randint(key, (NB, 27), 0, 4, dtype=jnp.int32) > 0
    keep_flags = keep_flags | (slot_index == 13)[None, :] | (target % LB == 0)[:, None]
    neighbour = new_c * LB + new_b * ROW + new_a
    return jnp.where(inside & keep_flags, neighbour, -1)


def draw_far_src(key, part):
    key = jax.random.fold_in(key, 37)
    pick_key, count_key = jax.random.split(key)
    subtree_total = NB // LB
    row_total = subtree_total * TB
    row_index = jnp.arange(row_total, dtype=jnp.int32)
    device_index = row_index // TB
    heap_index = row_index % TB + 1
    level_size = jnp.ones_like(heap_index)
    for bit_index in range(1, LB.bit_length()):
        level_size = jnp.where(heap_index >= 2 ** bit_index, 2 ** bit_index, level_size)
    place_index = device_index * level_size + heap_index - level_size
    span_width = 2 * (REACH - 1)
    candidate = jnp.arange(span_width, dtype=jnp.int32)
    step_size = candidate // 2 + 2
    signed_step = jnp.where(candidate % 2 == 0, step_size, -step_size)
    target = place_index[:, None] + signed_step[None, :]
    usable = (step_size[None, :] <= level_size[:, None]) & (target >= 0) & (target < subtree_total * level_size[:, None])
    picked, good = pick_sources(pick_key, target, usable, FS)
    live_count = jax.random.randint(count_key, (row_total, 1), FS // 2, FS + 1, dtype=jnp.int32)
    live_count = jnp.where((heap_index == LB)[:, None], FS, live_count)
    good = good & (jnp.arange(FS, dtype=jnp.int32)[None, :] < live_count)
    safe_pick = jnp.where(good, picked, 0)
    source_device = safe_pick // level_size[:, None]
    source_slot = safe_pick % level_size[:, None] + level_size[:, None] - 1
    return jnp.where(good, source_device * TB + source_slot, -1)


def draw_top_src(key, part):
    key = jax.random.fold_in(key, 53)
    subtree_total = NB // LB
    row_total = subtree_total + subtree_total // 2
    row_index = jnp.arange(row_total, dtype=jnp.int32)
    lower_rows = row_index < subtree_total
    level_count = jnp.where(lower_rows, subtree_total, subtree_total // 2)
    place_index = jnp.where(lower_rows, row_index, row_index - subtree_total)
    span_width = max(2 * subtree_total, FS)
    candidate = jnp.arange(span_width, dtype=jnp.int32)
    step_size = candidate // 2 + 2
    signed_step = jnp.where(candidate % 2 == 0, step_size, -step_size)
    target = place_index[:, None] + signed_step[None, :]
    usable = (target >= 0) & (target < level_count[:, None])
    picked, good = pick_sources(key, target, usable, FS)
    return jnp.where(good, picked, -1)


def plant(result, stream_key, least, top_value):
    longest = result.shape.index(max(result.shape))
    spots = []
    for shift in (0, 1):
        where = [jax.random.randint(jax.random.fold_in(stream_key, axis), (), 0, length) for axis, length in enumerate(result.shape)]
        where[longest] = (where[longest] + shift) % result.shape[longest]
        spots.append(tuple(where))
    return result.at[spots[0]].set(least).at[spots[1]].set(top_value)


def block_scale(key, extent, cuts, low, high):
    level, own = 1.0, jax.random.fold_in(key, 6)
    for position, shards_of in cuts:
        steps = jnp.exp(jax.random.uniform(jax.random.fold_in(own, position), (shards_of,), jnp.float32, low / len(cuts), high / len(cuts)))
        level = level * jnp.repeat(steps, extent[position] // shards_of).reshape([-1 if axis == position else 1 for axis in range(len(extent))])
    return level


def gaussian(key, dims, spread, reach, cuts=(), held_as=jnp.bfloat16):
    values = spread * jax.random.normal(key, dims, jnp.float32)
    if cuts:
        values = values * block_scale(key, dims, cuts, -0.22, 0.18)
    return jnp.clip(values, -reach, reach).astype(held_as)


def setup_inputs(seed: int = 0) -> dict:
    seeds = jax.random.split(jax.random.key(seed), 11)
    values = gaussian(seeds[0], (NV, NPTS), 1.0, 6.0, ((0, 4), (1, 8)))
    coords = draw_coords(jax.random.fold_in(seeds[10], 71), 0)
    basis = gaussian(seeds[2], (NB, K, M), M ** -0.5, 0.5, ((0, 32),))
    transfer = gaussian(seeds[3], (SUBTREES * TB, K * K), (K + K // 2) ** -0.5, 0.625, ((0, 8),))
    coupling = gaussian(seeds[4], (NCLASS, K * K), (K * FS) ** -0.5, 0.15625)
    near_src = draw_near_src(jax.random.fold_in(seeds[10], 71), 0)
    far_src = draw_far_src(jax.random.fold_in(seeds[10], 71), 0)
    far_cls = plant(jax.random.randint(seeds[7], (SUBTREES * TB, FS), 0, NCLASS), jax.random.fold_in(seeds[7], 1), 0, NCLASS - 1).astype(jnp.int32)
    top_src = draw_top_src(jax.random.fold_in(seeds[10], 71), 0)
    top_cls = plant(jax.random.randint(seeds[9], (TOPS, FS), 0, NCLASS), jax.random.fold_in(seeds[9], 1), 0, NCLASS - 1).astype(jnp.int32)
    return dict(values=values, coords=coords, basis=basis, transfer=transfer, coupling=coupling, near_src=near_src, far_src=far_src, far_cls=far_cls, top_src=top_src, top_cls=top_cls)


kernel_spread = 0.2
kernel_amplitude = 0.3


def group_couple(gathered, classes, live_mask, coupling):
    class_picks = ((classes[:, :, None] == jnp.arange(NCLASS, dtype=jnp.int32)[None, None, :]) & live_mask[:, :, None]).astype(jnp.float32)
    grouped = jnp.einsum('rsc,rsx->rcx', class_picks, gathered.astype(jnp.float32)).astype(jnp.bfloat16)
    row_total = grouped.shape[0]
    grouped = grouped.reshape(row_total, NCLASS, NV, K)
    matrices = coupling.reshape(NCLASS, K, K).astype(jnp.float32)
    return jnp.einsum('ckl,rcnl->rnk', matrices, grouped.astype(jnp.float32))


def table_terms(source_rows, classes, coef_table, coupling):
    live_mask = source_rows >= 0
    gathered = jnp.take(coef_table, jnp.where(live_mask, source_rows, 0), axis=0)
    return group_couple(gathered, classes, live_mask, coupling)


def reference(values, coords, basis, transfer, coupling, near_src, far_src, far_cls, top_src, top_cls):
    value_boxes = values.reshape(NV, NB, M)
    point_boxes = coords.reshape(3, NB, M)
    group_size = min(16, LB)

    def near_block(block_index):
        first_box = block_index * group_size
        sources = lax.dynamic_slice_in_dim(near_src, first_box, group_size, 0)
        live_mask = sources >= 0
        safe_rows = jnp.where(live_mask, sources, 0)
        target_here = lax.dynamic_slice_in_dim(point_boxes, first_box, group_size, 1)
        source_points = jnp.take(point_boxes, safe_rows, axis=1)
        distance = jnp.zeros((group_size, NS, M, M), jnp.float32)
        for axis_index in range(3):
            offset = target_here[axis_index][:, None, :, None] - source_points[axis_index][:, :, None, :]
            distance = distance + offset * offset
        kernel = (kernel_amplitude * jnp.exp(-distance / kernel_spread) * live_mask[:, :, None, None].astype(jnp.float32)).astype(jnp.bfloat16)
        source_values = jnp.take(value_boxes, safe_rows, axis=1)
        return jnp.einsum('bsij,nbsj->nbi', kernel.astype(jnp.float32), source_values.astype(jnp.float32))

    near_values = lax.map(near_block, jnp.arange(NB // group_size, dtype=jnp.int32))
    near_values = jnp.transpose(near_values, (1, 0, 2, 3)).reshape(NV, NB * M)

    leaf_coef = jnp.einsum('bkm,nbm->bnk', basis.astype(jnp.float32), value_boxes.astype(jnp.float32)).astype(jnp.bfloat16)
    tree_mats = transfer.reshape(N_LEAF, TB, K, K)
    levels = [leaf_coef.reshape(N_LEAF, LB, NV, K)]
    node_count = LB
    while node_count > 1:
        matrices = tree_mats[:, node_count - 1:2 * node_count - 1].astype(jnp.float32)
        lifted = jnp.einsum('pckl,pcnl->pcnk', matrices, levels[-1].astype(jnp.float32))
        levels.append(lifted.reshape(N_LEAF, node_count // 2, 2, NV, K).sum(axis=2).astype(jnp.bfloat16))
        node_count = node_count // 2

    fields = []
    for level_depth in range(len(levels) - 1):
        node_count = LB >> level_depth
        flat_coef = levels[level_depth].reshape(N_LEAF * node_count, NV * K)

        def device_terms(device_index):
            first_row = device_index * TB + node_count - 1
            source_rows = lax.dynamic_slice_in_dim(far_src, first_row, node_count, 0)
            classes = lax.dynamic_slice_in_dim(far_cls, first_row, node_count, 0)
            live_mask = source_rows >= 0
            safe_rows = jnp.where(live_mask, source_rows, 0)
            place_index = jnp.where(live_mask, (safe_rows // TB) * node_count + safe_rows % TB - (node_count - 1), 0)
            gathered = jnp.take(flat_coef, place_index, axis=0)
            return group_couple(gathered, classes, live_mask, coupling)

        fields.append(lax.map(device_terms, jnp.arange(N_LEAF, dtype=jnp.int32)))

    root_coef = levels[-1].reshape(N_LEAF, NV, K)
    root_mats = tree_mats[:, 0].astype(jnp.float32)
    lifts = jnp.einsum('pkl,pnl->pnk', root_mats, root_coef.astype(jnp.float32))
    top_coef = lifts.reshape(N_LEAF // 2, 2, NV, K).sum(axis=1).astype(jnp.bfloat16)

    root_field = table_terms(top_src[:N_LEAF], top_cls[:N_LEAF], root_coef.reshape(N_LEAF, NV * K), coupling)
    top_down = table_terms(top_src[N_LEAF:], top_cls[N_LEAF:], top_coef.reshape(N_LEAF // 2, NV * K), coupling).astype(jnp.bfloat16)
    pushed_root = jnp.einsum('pkl,pnk->pnl', root_mats, jnp.repeat(top_down, 2, axis=0).astype(jnp.float32))
    down_coef = (root_field + pushed_root).astype(jnp.bfloat16).reshape(N_LEAF, 1, NV, K)
    for level_depth in reversed(range(len(levels) - 1)):
        node_count = LB >> level_depth
        matrices = tree_mats[:, node_count - 1:2 * node_count - 1].astype(jnp.float32)
        pushed = jnp.einsum('pckl,pcnk->pcnl', matrices, jnp.repeat(down_coef, 2, axis=1).astype(jnp.float32))
        down_coef = (fields[level_depth] + pushed).astype(jnp.bfloat16)
    far_values = jnp.einsum('bkm,bnk->nbm', basis.astype(jnp.float32), down_coef.reshape(NB, NV, K).astype(jnp.float32))
    return (near_values + far_values.reshape(NV, NB * M)).astype(jnp.bfloat16)
```

```python
import math

import jax
import jax.numpy as jnp
import numpy as np
from jax import lax
from jax.experimental import pallas as pl
from jax.experimental.pallas import tpu as pltpu
from jax.sharding import PartitionSpec as P

M = 128
K = 64
REACH = 13
TB = 127
ROW = 16
N = 16
B = 64
PAIRS = 64
RIM = 28

SCALE = math.log2(math.e) / 0.2
SHIFT = math.log2(0.3)
DEAD = -1000.0

NN = (((1,), (0,)), ((), ()))
NT = (((1,), (1,)), ((), ()))
TN = (((0,), (0,)), ((), ()))


def dot(a, b, dims=NN):
    return lax.dot_general(a, b, dims, preferred_element_type=jnp.float32)


def vmem():
    return pl.BlockSpec(memory_space=pltpu.VMEM)


def rounded(x):
    return lax.reduce_precision(x, 8, 7)


def near_kernel(near_ref, x_ref, low_ref, own_ref, high_ref, sel_ref, mask_ref, out_ref, yp_ref):
    layers = (low_ref, own_ref, high_ref)
    for l, src in enumerate(layers):

        def features(u, carry, l=l, src=src):
            first = pl.multiple_of(jnp.maximum(u - 1, 0) * M, M)
            second = pl.multiple_of(jnp.minimum(u, B - 1) * M, M)
            both = jnp.concatenate(
                [src[16:32, pl.ds(first, M)], src[16:32, pl.ds(second, M)]], axis=0
            )
            yp_ref[l, u] = dot(both, sel_ref[...], TN).astype(jnp.bfloat16)
            return carry

        lax.fori_loop(0, B + 1, features, 0, unroll=5)

    zero = jnp.zeros((64, M), jnp.bfloat16)

    def weights(t, a, b, c, slot):
        live = jnp.where(near_ref[t, slot] >= 0, 1, 0)
        return jnp.concatenate(
            [x_ref[t, a], x_ref[t, 3 + b], x_ref[t, 6 + c], mask_ref[live]], axis=0
        )

    for row in range(B // ROW):
        steps = [b for b in range(3) if 0 <= row + b - 1 < B // ROW]

        def pair(q, carry, row=row, steps=steps):
            t = row * ROW + 2 * q
            kernels, vectors = [], []
            for c in range(3):
                for b in steps:
                    for a in range(3):
                        slot = 9 * c + 3 * b + a
                        u = t + (b - 1) * ROW + a - 1
                        w = jnp.concatenate(
                            [
                                jnp.concatenate([weights(t, a, b, c, slot), zero], axis=1),
                                jnp.concatenate([zero, weights(t + 1, a, b, c, slot)], axis=1),
                            ],
                            axis=0,
                        )
                        e = dot(yp_ref[c, u + 1], w)
                        kernels.append(jnp.exp2(e).astype(jnp.bfloat16))
                        first = pl.multiple_of(jnp.maximum(u, 0) * M, M)
                        second = pl.multiple_of(jnp.minimum(u + 1, B - 1) * M, M)
                        src = layers[c]
                        vectors.append(
                            jnp.concatenate(
                                [src[0:16, pl.ds(first, M)], src[0:16, pl.ds(second, M)]], axis=0
                            )
                        )
            total = dot(jnp.concatenate(vectors, axis=1), jnp.concatenate(kernels, axis=0))
            here = pl.multiple_of(t * M, M)
            out_ref[:, pl.ds(here, M)] = total[0:16, 0:M]
            out_ref[:, pl.ds(here + M, M)] = total[16:32, M : 2 * M]
            return carry

        lax.fori_loop(0, ROW // 2, pair, 0)


def near_field(near_src, x_tiles, low, own, high):
    sel = np.zeros((32, 128), np.float32)
    for half in range(2):
        for k in range(3):
            for r, source in enumerate((2 * k, 2 * k + 1, 2 * k, 2 * k + 1, 9, 9, 9)):
                sel[16 * half + source, 64 * half + 16 * k + r] = 1
        for r, source in enumerate((9, 6, 7, 8)):
            sel[16 * half + source, 64 * half + 48 + r] = 1
    mask = np.zeros((2, 16, 128), np.float32)
    mask[:, 1:4] = 1
    mask[0, 0] = DEAD
    return pl.pallas_call(
        near_kernel,
        name="near_field",
        out_shape=jax.ShapeDtypeStruct((N, B * M), jnp.float32),
        in_specs=[pl.BlockSpec(memory_space=pltpu.SMEM)] + [vmem()] * 6,
        out_specs=vmem(),
        scratch_shapes=[pltpu.VMEM((3, B + 1, M, M), jnp.bfloat16)],
        compiler_params=pltpu.CompilerParams(vmem_limit_bytes=40 << 20),
        cost_estimate=pl.CostEstimate(
            flops=20_000_000_000, bytes_accessed=5_000_000, transcendentals=28_000_000
        ),
    )(
        near_src,
        x_tiles,
        low,
        own,
        high,
        jnp.asarray(sel, jnp.bfloat16),
        jnp.asarray(mask, jnp.bfloat16),
    )


def counts_kernel(col_ref, cls_ref, a_ref):
    classes = a_ref.shape[0]
    width = a_ref.shape[2]
    slots = col_ref.shape[1]
    spread = slots * 8
    lane = lax.broadcasted_iota(jnp.int32, (slots, spread), 1)
    copies = (lane // 8 == lax.broadcasted_iota(jnp.int32, (slots, spread), 0)).astype(jnp.float32)
    columns = lax.broadcasted_iota(jnp.int32, (8, width), 1)
    match = (
        lax.broadcasted_iota(jnp.int32, (8, spread), 1) % 8
        == lax.broadcasted_iota(jnp.int32, (8, spread), 0)
    )

    def block(g, carry):
        halves = []
        for h in range(2):
            rows = pl.ds(pl.multiple_of(g * 16 + h * 8, 8), 8)
            col = col_ref[rows, :]
            wide = dot(cls_ref[rows, :].astype(jnp.float32), copies).astype(jnp.int32)
            wide = jnp.where(match, wide, -1)
            left = jnp.concatenate(
                [jnp.where(wide == c, 1.0, 0.0) for c in range(classes)], axis=0
            ).astype(jnp.bfloat16)
            right = jnp.concatenate(
                [jnp.where(col[:, e : e + 1] == columns, 1.0, 0.0) for e in range(slots)], axis=0
            ).astype(jnp.bfloat16)
            halves.append(dot(left, right))
        for c in range(classes):
            both = jnp.concatenate([half[8 * c : 8 * c + 8] for half in halves], axis=0)
            a_ref[c, pl.ds(pl.multiple_of(g * 16, 16), 16), :] = both.astype(jnp.bfloat16)
        return carry

    lax.fori_loop(0, 2 * PAIRS // 16, block, 0)


def class_counts(columns, classes, class_count, width):
    return pl.pallas_call(
        counts_kernel,
        name="class_counts",
        out_shape=jax.ShapeDtypeStruct((class_count, 2 * PAIRS, width), jnp.bfloat16),
        in_specs=[vmem()] * 2,
        out_specs=vmem(),
        compiler_params=pltpu.CompilerParams(vmem_limit_bytes=20 << 20),
        cost_estimate=pl.CostEstimate(
            flops=2_000_000_000, bytes_accessed=1_600_000, transcendentals=0
        ),
    )(columns, classes)


def up_kernel(values_ref, basis_ref, links_ref, first_ref, root_ref, out_ref, cs_ref):
    lower = lax.broadcasted_iota(jnp.int32, (N, 2 * K), 1) < K

    def keep(pair_index, tile):
        cs_ref[pl.ds(pair_index, N, stride=PAIRS), :] = tile
        return tile

    def lift(stacked, matrix):
        both = dot(stacked, matrix, NT)
        return jnp.where(lower, both[:N], both[N:]).astype(jnp.bfloat16)

    tiles = {}
    for i in range(B // 2):
        stacked = jnp.concatenate(
            [values_ref[:, 2 * i * M : (2 * i + 1) * M], values_ref[:, (2 * i + 1) * M : (2 * i + 2) * M]],
            axis=0,
        )
        tiles[B // 2 - 1 + i] = lift(stacked, basis_ref[i])
        keep(B // 2 - 1 + i, tiles[B // 2 - 1 + i].astype(jnp.float32))
    for j in reversed(range(B // 2 - 1)):
        stacked = jnp.concatenate([tiles[2 * j + 1], tiles[2 * j + 2]], axis=0)
        tiles[j] = lift(stacked, links_ref[j])
        keep(j, tiles[j].astype(jnp.float32))
    root = dot(tiles[0], first_ref[...], NT).astype(jnp.bfloat16)
    up = dot(root, root_ref[...], NT)
    last = jnp.concatenate([root.astype(jnp.float32), up], axis=1)
    keep(PAIRS - 1, last)
    for n in range(N):
        out_ref[n] = cs_ref[n * PAIRS : (n + 1) * PAIRS, :].astype(jnp.bfloat16)
    out_ref[N, 0:N, :] = last.astype(jnp.bfloat16)
    out_ref[N, N:PAIRS, :] = jnp.zeros((PAIRS - N, 2 * K), jnp.bfloat16)


def upward(values, basis, links, first, root):
    return pl.pallas_call(
        up_kernel,
        name="upward",
        out_shape=jax.ShapeDtypeStruct((N + 1, PAIRS, 2 * K), jnp.bfloat16),
        in_specs=[vmem()] * 5,
        out_specs=vmem(),
        scratch_shapes=[pltpu.VMEM((N * PAIRS, 2 * K), jnp.float32)],
        compiler_params=pltpu.CompilerParams(vmem_limit_bytes=20 << 20),
        cost_estimate=pl.CostEstimate(
            flops=300_000_000, bytes_accessed=3_000_000, transcendentals=0
        ),
    )(values, basis, links, first, root)


def down_kernel(
    place_ref,
    low_ref,
    own_ref,
    high_ref,
    tops_ref,
    a_ref,
    coupling_ref,
    links_ref,
    first_ref,
    root_ref,
    basis_ref,
    near_ref,
    out_ref,
    cf_ref,
    side_ref,
    call_ref,
    bd_ref,
    lhs_ref,
    fs_ref,
):
    classes = a_ref.shape[0]
    height = a_ref.shape[2] // 2
    subtrees = tops_ref.shape[0]
    lower = lax.broadcasted_iota(jnp.int32, (N, 2 * K), 1) < K

    used = PAIRS + 2 * RIM + subtrees
    for n in range(N):
        base = n * height
        cf_ref[base : base + PAIRS, :] = own_ref[0, n].astype(jnp.float32)
        side_ref[...] = low_ref[0, n].astype(jnp.float32)
        at = base + PAIRS
        for start, size in ((0, 7), (8, 7), (24, 7), (56, 7)):
            cf_ref[at : at + size, :] = side_ref[start : start + size, :]
            at += size
        side_ref[...] = high_ref[0, n].astype(jnp.float32)
        for start, size in ((0, 14), (15, 7), (31, 7)):
            cf_ref[at : at + size, :] = side_ref[start : start + size, :]
            at += size
        if used < height:
            cf_ref[base + used : base + height, :] = jnp.zeros((height - used, 2 * K), jnp.float32)
    for q in range(subtrees // 2):
        even = tops_ref[2 * q, 0].astype(jnp.float32)
        odd = tops_ref[2 * q + 1, 0].astype(jnp.float32)
        at = PAIRS + 2 * RIM + 2 * q
        cf_ref[pl.ds(at, N, stride=height), :] = jnp.where(lower, even, even + odd)
        cf_ref[pl.ds(at + 1, N, stride=height), :] = odd
    wide_lower = lax.broadcasted_iota(jnp.int32, (height, 2 * K), 1) < K
    for m in range(N // 2):
        one = cf_ref[2 * m * height : (2 * m + 1) * height, :]
        two = cf_ref[(2 * m + 1) * height : (2 * m + 2) * height, :]
        lanes = slice(m * 2 * K, (m + 1) * 2 * K)
        call_ref[0:height, lanes] = jnp.where(
            wide_lower, one, pltpu.roll(two, K, 1)
        ).astype(jnp.bfloat16)
        call_ref[height : 2 * height, lanes] = jnp.where(
            wide_lower, pltpu.roll(one, K, 1), two
        ).astype(jnp.bfloat16)

    def spread(c, carry):
        s = coupling_ref[c]
        z = jnp.zeros((K, K), jnp.bfloat16)
        at = pl.multiple_of(c * 4 * K, 4 * K)
        for block in range(4):
            place = (0, 2, 1, 3)[block]
            bd_ref[pl.ds(at + block * K, K), :] = jnp.concatenate(
                [s if place == i else z for i in range(4)], axis=1
            )
        return carry

    lax.fori_loop(0, classes, spread, 0)

    for c in range(classes):
        grouped = dot(a_ref[c], call_ref[...]).astype(jnp.bfloat16)
        for m in range(N // 2):
            for parity in range(2):
                lhs_ref[
                    m * PAIRS : (m + 1) * PAIRS,
                    (2 * c + parity) * 2 * K : (2 * c + parity + 1) * 2 * K,
                ] = grouped[parity * PAIRS : (parity + 1) * PAIRS, m * 2 * K : (m + 1) * 2 * K]
    for m in range(N // 2):
        field = dot(lhs_ref[m * PAIRS : (m + 1) * PAIRS, :], bd_ref[...])
        fs_ref[2 * m * PAIRS : (2 * m + 1) * PAIRS, :] = field[:, 0 : 2 * K]
        fs_ref[(2 * m + 1) * PAIRS : (2 * m + 2) * PAIRS, :] = field[:, 2 * K : 4 * K]

    def field_of(pair_index):
        return fs_ref[pl.ds(pair_index, N, stride=PAIRS), :]

    def push(tile, matrix):
        none = jnp.zeros_like(tile)
        stacked = jnp.concatenate(
            [jnp.where(lower, tile, none), jnp.where(lower, none, tile)], axis=0
        ).astype(jnp.bfloat16)
        return dot(stacked, matrix)

    last = field_of(PAIRS - 1)
    top = last[:, K : 2 * K].astype(jnp.bfloat16)
    root = (last[:, 0:K] + dot(top, root_ref[...])).astype(jnp.bfloat16)
    tiles = {0: field_of(0) + dot(root, first_ref[...])}
    for j in range(B // 2 - 1):
        both = push(tiles[j], links_ref[j])
        tiles[2 * j + 1] = field_of(2 * j + 1) + both[:N]
        tiles[2 * j + 2] = field_of(2 * j + 2) + both[N:]
    for i in range(B // 2):
        both = push(tiles[B // 2 - 1 + i], basis_ref[i])
        for h in range(2):
            lanes = slice((2 * i + h) * M, (2 * i + h + 1) * M)
            out_ref[:, lanes] = (near_ref[:, lanes] + both[h * N : (h + 1) * N]).astype(jnp.bfloat16)


def downward(place, gathered, counts, coupling, links, first, root, basis, near):
    subtrees = gathered.shape[0]
    classes = counts.shape[0]
    height = counts.shape[2] // 2
    block = (1, N + 1, PAIRS, 2 * K)

    def whole(x):
        return pl.BlockSpec(x.shape, lambda i, p: (0,) * x.ndim)

    grid_spec = pltpu.PrefetchScalarGridSpec(
        num_scalar_prefetch=1,
        grid=(1,),
        in_specs=[
            pl.BlockSpec(block, lambda i, p: (jnp.maximum(p[0] - 1, 0), 0, 0, 0)),
            pl.BlockSpec(block, lambda i, p: (p[0], 0, 0, 0)),
            pl.BlockSpec(block, lambda i, p: (jnp.minimum(p[0] + 1, subtrees - 1), 0, 0, 0)),
            pl.BlockSpec((subtrees, 1, N, 2 * K), lambda i, p: (0, N, 0, 0)),
        ]
        + [whole(x) for x in (counts, coupling, links, first, root, basis, near)],
        out_specs=pl.BlockSpec((N, B * M), lambda i, p: (0, 0)),
        scratch_shapes=[
            pltpu.VMEM((N * height, 2 * K), jnp.float32),
            pltpu.VMEM((PAIRS, 2 * K), jnp.float32),
            pltpu.VMEM((2 * height, N * K), jnp.bfloat16),
            pltpu.VMEM((classes * 4 * K, 4 * K), jnp.bfloat16),
            pltpu.VMEM((N // 2 * PAIRS, classes * 4 * K), jnp.bfloat16),
            pltpu.VMEM((N * PAIRS, 2 * K), jnp.float32),
        ],
    )
    return pl.pallas_call(
        down_kernel,
        name="downward",
        out_shape=jax.ShapeDtypeStruct((N, B * M), jnp.bfloat16),
        grid_spec=grid_spec,
        compiler_params=pltpu.CompilerParams(vmem_limit_bytes=48 << 20),
        cost_estimate=pl.CostEstimate(
            flops=4_000_000_000, bytes_accessed=6_000_000, transcendentals=0
        ),
    )(place, gathered, gathered, gathered, gathered, counts, coupling, links, first, root, basis, near)


def source_columns(far_src, top_src, position, subtrees, height):
    owner = far_src // TB
    slot = far_src % TB
    count = jnp.ones_like(slot)
    for bit in range(1, 7):
        count = jnp.where(slot + 1 >= 2**bit, 2**bit, count)
    first = (count - 2) // 2
    inside = (slot - (count - 1)) // 2
    pairs = count // 2
    width = jnp.minimum(pairs, 7)
    rim_first = jnp.where(count <= 16, first, jnp.where(count == 32, 14, 21))
    side = owner - position
    row = jnp.where(
        side == 0,
        first + inside,
        jnp.where(
            side < 0,
            PAIRS + rim_first + inside - (pairs - width),
            PAIRS + RIM + rim_first + inside,
        ),
    )
    column = jnp.where(far_src >= 0, row + ((slot - 1) % 2) * height, -1)
    base = PAIRS + 2 * RIM
    roots = lax.dynamic_slice_in_dim(top_src, position, 1, 0)
    tops = lax.dynamic_slice_in_dim(top_src, subtrees + position // 2, 1, 0)
    roots = jnp.where(roots >= 0, base + roots, -1)
    tops = jnp.where(tops >= 0, height + base + 2 * tops, -1)
    return by_parity(column, roots, tops)


def by_parity(rows, root, top):
    paired = rows[1:].reshape(PAIRS - 1, 2, rows.shape[1])
    return jnp.concatenate([paired[:, 0], root, paired[:, 1], top], axis=0)


def per_device(
    values, coords, basis, transfer, coupling, near_src, far_src, far_cls, top_src, top_cls
):
    position = lax.axis_index("leaf")
    subtrees = lax.axis_size("leaf")
    class_count = coupling.shape[0]
    height = -(-(PAIRS + 2 * RIM + subtrees) // 64) * 64

    whole_basis = lax.all_gather(basis, "vec", axis=0, tiled=True)

    box = jnp.arange(B, dtype=jnp.int32)
    centre = jnp.stack(
        [box % ROW, box // ROW, jnp.full((B,), 0, jnp.int32) + position]
    ).astype(jnp.float32) + 0.5
    local = coords.reshape(3, B, M) - centre[:, :, None]
    flat = coords - jnp.repeat(centre, M, axis=1)
    high = rounded(flat)
    rest = rounded(flat - high)
    held = high + rest
    size = -SCALE * (held[0] ** 2 + held[1] ** 2 + held[2] ** 2)
    size_a = rounded(size)
    size_b = rounded(size - size_a)
    size_c = size - size_a - size_b
    rows = []
    for k in range(3):
        rows += [high[k], rest[k]]
    rows += [size_a, size_b, size_c, jnp.ones_like(size)]
    rows += [jnp.zeros_like(size)] * 6
    packed = jnp.concatenate([values, jnp.stack(rows).astype(jnp.bfloat16)], axis=0)
    forward = [(i, i + 1) for i in range(subtrees - 1)]
    backward = [(i + 1, i) for i in range(subtrees - 1)]
    from_low = lax.ppermute(packed, "leaf", forward)
    from_high = lax.ppermute(packed, "leaf", backward)

    moved = (
        jnp.transpose(local, (1, 0, 2))[:, :, None, None, :]
        - jnp.arange(-1, 2, dtype=jnp.float32)[None, None, :, None, None]
    )
    row = jnp.arange(16, dtype=jnp.int32)[None, None, None, :, None]
    axis = jnp.arange(3, dtype=jnp.int32)[None, :, None, None, None]
    term = jnp.where(
        row < 4,
        2 * SCALE * moved,
        -SCALE * moved * moved + jnp.where(axis == 0, SHIFT, 0.0),
    )
    term_a = rounded(term)
    term_b = rounded(term - term_a)
    term_c = term - term_a - term_b
    x_tiles = jnp.where(
        (row < 2) | (row == 4),
        term_a,
        jnp.where((row < 4) | (row == 5), term_b, jnp.where(row == 6, term_c, 0.0)),
    )
    x_tiles = x_tiles.astype(jnp.bfloat16).reshape(B, 9, 16, M)

    matrices = transfer.reshape(TB, K, K)
    siblings = matrices[1:].reshape(TB // 2, 2, K, K).transpose(0, 2, 1, 3).reshape(TB // 2, K, 2 * K)
    first = siblings[0]
    links = siblings[1:].reshape(B // 2 - 1, 2 * K, 2 * K)
    root = matrices[0]
    coupling_t = jnp.transpose(coupling.reshape(class_count, K, K), (0, 2, 1))

    columns = source_columns(far_src, top_src, position, subtrees, height)
    classes = by_parity(
        far_cls,
        lax.dynamic_slice_in_dim(top_cls, position, 1, 0),
        lax.dynamic_slice_in_dim(top_cls, subtrees + position // 2, 1, 0),
    )
    counts = class_counts(columns, classes, class_count, 2 * height)

    basis_pairs = whole_basis.reshape(B // 2, 2 * K, M)
    coefs = upward(values, basis_pairs, links, first, root)
    gathered = lax.all_gather(coefs, "leaf", axis=0)
    near = near_field(near_src, x_tiles, from_low, packed, from_high)
    place = jnp.full((1,), 0, jnp.int32) + position
    return downward(
        place, gathered, counts, coupling_t, links, first, root, basis_pairs, near
    )


def solution(mesh):
    in_specs = (
        P("vec", "leaf"),
        P(None, "leaf"),
        P(("leaf", "vec"), None, None),
        P("leaf", None),
        P(),
        P("leaf", None),
        P("leaf", None),
        P("leaf", None),
        P(),
        P(),
    )
    out_specs = P("vec", "leaf")
    return jax.shard_map(
        per_device, mesh=mesh, in_specs=in_specs, out_specs=out_specs, check_vma=False
    )
```

```python
import math

import jax
import jax.numpy as jnp
import numpy as np
from jax import lax
from jax.experimental import pallas as pl
from jax.experimental.pallas import tpu as pltpu
from jax.sharding import PartitionSpec as P

M = 128
K = 64
REACH = 13
TB = 127
ROW = 16
N = 16
B = 64
PAIRS = 64
RIM = 28

SCALE = math.log2(math.e) / 0.2
AMPLITUDE = 0.3
DEAD = -1000.0

NN = (((1,), (0,)), ((), ()))
NT = (((1,), (1,)), ((), ()))
TN = (((0,), (0,)), ((), ()))


def dot(a, b, dims=NN):
    return lax.dot_general(a, b, dims, preferred_element_type=jnp.float32)


def vmem():
    return pl.BlockSpec(memory_space=pltpu.VMEM)


def rounded(x):
    return lax.reduce_precision(x, 8, 7)


def near_kernel(near_ref, x_ref, low_ref, own_ref, high_ref, sel_ref, mask_ref, out_ref, yp_ref):
    layers = (low_ref, own_ref, high_ref)
    for l, src in enumerate(layers):

        def features(u, carry, l=l, src=src):
            first = pl.multiple_of(jnp.maximum(u - 1, 0) * M, M)
            second = pl.multiple_of(jnp.minimum(u, B - 1) * M, M)
            both = jnp.concatenate(
                [src[16:32, pl.ds(first, M)], src[16:32, pl.ds(second, M)]], axis=0
            )
            yp_ref[l, u] = dot(both, sel_ref[...], TN).astype(jnp.bfloat16)
            return carry

        lax.fori_loop(0, B + 1, features, 0, unroll=5)

    zero = jnp.zeros((64, M), jnp.bfloat16)

    def weights(t, a, b, c, slot):
        live = jnp.where(near_ref[t, slot] >= 0, 1, 0)
        return jnp.concatenate(
            [x_ref[t, a], x_ref[t, 3 + b], x_ref[t, 6 + c], mask_ref[live]], axis=0
        )

    for row in range(B // ROW):
        steps = [b for b in range(3) if 0 <= row + b - 1 < B // ROW]

        def pair(q, carry, row=row, steps=steps):
            t = row * ROW + 2 * q
            kernels, vectors = [], []
            for c in range(3):
                for b in steps:
                    for a in range(3):
                        slot = 9 * c + 3 * b + a
                        u = t + (b - 1) * ROW + a - 1
                        w = jnp.concatenate(
                            [
                                jnp.concatenate([weights(t, a, b, c, slot), zero], axis=1),
                                jnp.concatenate([zero, weights(t + 1, a, b, c, slot)], axis=1),
                            ],
                            axis=0,
                        )
                        e = dot(yp_ref[c, u + 1], w)
                        kernels.append(jnp.exp2(e.astype(jnp.bfloat16)))
                        first = pl.multiple_of(jnp.maximum(u, 0) * M, M)
                        second = pl.multiple_of(jnp.minimum(u + 1, B - 1) * M, M)
                        src = layers[c]
                        vectors.append(
                            jnp.concatenate(
                                [src[0:16, pl.ds(first, M)], src[0:16, pl.ds(second, M)]], axis=0
                            )
                        )
            total = dot(jnp.concatenate(vectors, axis=1), jnp.concatenate(kernels, axis=0))
            here = pl.multiple_of(t * M, M)
            out_ref[:, pl.ds(here, M)] = AMPLITUDE * total[0:16, 0:M]
            out_ref[:, pl.ds(here + M, M)] = AMPLITUDE * total[16:32, M : 2 * M]
            return carry

        lax.fori_loop(0, ROW // 2, pair, 0)


def near_field(near_src, x_tiles, low, own, high):
    sel = np.zeros((32, 128), np.float32)
    for half in range(2):
        for k in range(3):
            for r, source in enumerate((2 * k, 2 * k + 1, 2 * k, 2 * k + 1, 9, 9, 9)):
                sel[16 * half + source, 64 * half + 16 * k + r] = 1
        for r, source in enumerate((9, 6, 7, 8)):
            sel[16 * half + source, 64 * half + 48 + r] = 1
    mask = np.zeros((2, 16, 128), np.float32)
    mask[:, 1:4] = 1
    mask[0, 0] = DEAD
    return pl.pallas_call(
        near_kernel,
        name="near_field",
        out_shape=jax.ShapeDtypeStruct((N, B * M), jnp.float32),
        in_specs=[pl.BlockSpec(memory_space=pltpu.SMEM)] + [vmem()] * 6,
        out_specs=vmem(),
        scratch_shapes=[pltpu.VMEM((3, B + 1, M, M), jnp.bfloat16)],
        compiler_params=pltpu.CompilerParams(vmem_limit_bytes=40 << 20),
        cost_estimate=pl.CostEstimate(
            flops=20_000_000_000, bytes_accessed=5_000_000, transcendentals=28_000_000
        ),
    )(
        near_src,
        x_tiles,
        low,
        own,
        high,
        jnp.asarray(sel, jnp.bfloat16),
        jnp.asarray(mask, jnp.bfloat16),
    )


def counts_kernel(col_ref, cls_ref, a_ref):
    classes = a_ref.shape[0]
    width = a_ref.shape[2]
    slots = col_ref.shape[1]
    spread = slots * 8
    lane = lax.broadcasted_iota(jnp.int32, (slots, spread), 1)
    copies = (lane // 8 == lax.broadcasted_iota(jnp.int32, (slots, spread), 0)).astype(jnp.float32)
    columns = lax.broadcasted_iota(jnp.int32, (8, width), 1)
    match = (
        lax.broadcasted_iota(jnp.int32, (8, spread), 1) % 8
        == lax.broadcasted_iota(jnp.int32, (8, spread), 0)
    )

    def block(g, carry):
        halves = []
        for h in range(2):
            rows = pl.ds(pl.multiple_of(g * 16 + h * 8, 8), 8)
            col = col_ref[rows, :]
            wide = dot(cls_ref[rows, :].astype(jnp.float32), copies).astype(jnp.int32)
            wide = jnp.where(match, wide, -1)
            left = jnp.concatenate(
                [jnp.where(wide == c, 1.0, 0.0) for c in range(classes)], axis=0
            ).astype(jnp.bfloat16)
            right = jnp.concatenate(
                [jnp.where(col[:, e : e + 1] == columns, 1.0, 0.0) for e in range(slots)], axis=0
            ).astype(jnp.bfloat16)
            halves.append(dot(left, right))
        for c in range(classes):
            both = jnp.concatenate([half[8 * c : 8 * c + 8] for half in halves], axis=0)
            a_ref[c, pl.ds(pl.multiple_of(g * 16, 16), 16), :] = both.astype(jnp.bfloat16)
        return carry

    lax.fori_loop(0, 2 * PAIRS // 16, block, 0)


def class_counts(columns, classes, class_count, width):
    return pl.pallas_call(
        counts_kernel,
        name="class_counts",
        out_shape=jax.ShapeDtypeStruct((class_count, 2 * PAIRS, width), jnp.bfloat16),
        in_specs=[vmem()] * 2,
        out_specs=vmem(),
        compiler_params=pltpu.CompilerParams(vmem_limit_bytes=20 << 20),
        cost_estimate=pl.CostEstimate(
            flops=2_000_000_000, bytes_accessed=1_600_000, transcendentals=0
        ),
    )(columns, classes)


FIRST_ROWS = tuple(range(14)) + tuple(range(15, 22)) + tuple(range(31, 38))
LAST_ROWS = tuple(range(7)) + tuple(range(8, 15)) + tuple(range(24, 31)) + tuple(range(56, 63))
RIM_ROWS = 32


def children_of(matrix_ref, slot):
    return jnp.concatenate([matrix_ref[2 * slot + 1], matrix_ref[2 * slot + 2]], axis=1)


def links_of(matrix_ref, pair_index):
    return jnp.concatenate(
        [children_of(matrix_ref, 2 * pair_index + 1), children_of(matrix_ref, 2 * pair_index + 2)],
        axis=0,
    )


def up_kernel(
    values_ref, basis_ref, matrix_ref, out_ref, first_ref, last_ref, root_ref, cs_ref, fs_ref, ls_ref
):
    lower = lax.broadcasted_iota(jnp.int32, (N, 2 * K), 1) < K

    def keep(pair_index, tile):
        cs_ref[pl.ds(pair_index, N, stride=PAIRS), :] = tile
        for rows, ref in ((FIRST_ROWS, fs_ref), (LAST_ROWS, ls_ref)):
            if pair_index in rows:
                ref[pl.ds(rows.index(pair_index), N, stride=RIM_ROWS), :] = tile

    def lift(stacked, matrix):
        both = dot(stacked, matrix, NT)
        return jnp.where(lower, both[:N], both[N:]).astype(jnp.bfloat16)

    tiles = {}
    for i in range(B // 2):
        stacked = jnp.concatenate(
            [values_ref[:, 2 * i * M : (2 * i + 1) * M], values_ref[:, (2 * i + 1) * M : (2 * i + 2) * M]],
            axis=0,
        )
        tiles[B // 2 - 1 + i] = lift(stacked, basis_ref[i])
        keep(B // 2 - 1 + i, tiles[B // 2 - 1 + i].astype(jnp.float32))
    for j in reversed(range(B // 2 - 1)):
        stacked = jnp.concatenate([tiles[2 * j + 1], tiles[2 * j + 2]], axis=0)
        tiles[j] = lift(stacked, links_of(matrix_ref, j))
        keep(j, tiles[j].astype(jnp.float32))
    root = dot(tiles[0], children_of(matrix_ref, 0), NT).astype(jnp.bfloat16)
    up = dot(root, matrix_ref[0], NT)
    last = jnp.concatenate([root.astype(jnp.float32), up], axis=1)
    keep(PAIRS - 1, last)
    root_ref[...] = last.astype(jnp.bfloat16)
    for n in range(N):
        out_ref[n] = cs_ref[n * PAIRS : (n + 1) * PAIRS, :].astype(jnp.bfloat16)
        for source, target in ((fs_ref, first_ref), (ls_ref, last_ref)):
            base = n * RIM_ROWS
            source[base + RIM : base + RIM_ROWS, :] = jnp.zeros((RIM_ROWS - RIM, 2 * K), jnp.float32)
            target[n] = source[base : base + RIM_ROWS, :].astype(jnp.bfloat16)


def upward(values, basis, matrices):
    return pl.pallas_call(
        up_kernel,
        name="upward",
        out_shape=[
            jax.ShapeDtypeStruct((N, PAIRS, 2 * K), jnp.bfloat16),
            jax.ShapeDtypeStruct((N, RIM_ROWS, 2 * K), jnp.bfloat16),
            jax.ShapeDtypeStruct((N, RIM_ROWS, 2 * K), jnp.bfloat16),
            jax.ShapeDtypeStruct((N, 2 * K), jnp.bfloat16),
        ],
        in_specs=[vmem()] * 3,
        out_specs=[vmem()] * 4,
        scratch_shapes=[
            pltpu.VMEM((N * PAIRS, 2 * K), jnp.float32),
            pltpu.VMEM((N * RIM_ROWS, 2 * K), jnp.float32),
            pltpu.VMEM((N * RIM_ROWS, 2 * K), jnp.float32),
        ],
        compiler_params=pltpu.CompilerParams(vmem_limit_bytes=20 << 20),
        cost_estimate=pl.CostEstimate(
            flops=300_000_000, bytes_accessed=3_000_000, transcendentals=0
        ),
    )(values, basis, matrices)


def down_kernel(
    low_ref,
    own_ref,
    high_ref,
    tops_ref,
    a_ref,
    coupling_ref,
    matrix_ref,
    basis_ref,
    near_ref,
    out_ref,
    cf_ref,
    call_ref,
    bd_ref,
    lhs_ref,
    fs_ref,
):
    classes = a_ref.shape[0]
    height = a_ref.shape[2] // 2
    subtrees = tops_ref.shape[0]
    lower = lax.broadcasted_iota(jnp.int32, (N, 2 * K), 1) < K

    used = PAIRS + 2 * RIM + subtrees
    for n in range(N):
        base = n * height
        cf_ref[base : base + PAIRS, :] = own_ref[n].astype(jnp.float32)
        at = base + PAIRS
        cf_ref[at : at + RIM, :] = low_ref[n].astype(jnp.float32)[:RIM]
        at += RIM
        cf_ref[at : at + RIM, :] = high_ref[n].astype(jnp.float32)[:RIM]
        if used < height:
            cf_ref[base + used : base + height, :] = jnp.zeros((height - used, 2 * K), jnp.float32)
    for q in range(subtrees // 2):
        even = tops_ref[2 * q].astype(jnp.float32)
        odd = tops_ref[2 * q + 1].astype(jnp.float32)
        at = PAIRS + 2 * RIM + 2 * q
        cf_ref[pl.ds(at, N, stride=height), :] = jnp.where(lower, even, even + odd)
        cf_ref[pl.ds(at + 1, N, stride=height), :] = odd
    wide_lower = lax.broadcasted_iota(jnp.int32, (height, 2 * K), 1) < K
    for m in range(N // 2):
        one = cf_ref[2 * m * height : (2 * m + 1) * height, :]
        two = cf_ref[(2 * m + 1) * height : (2 * m + 2) * height, :]
        lanes = slice(m * 2 * K, (m + 1) * 2 * K)
        call_ref[0:height, lanes] = jnp.where(
            wide_lower, one, pltpu.roll(two, K, 1)
        ).astype(jnp.bfloat16)
        call_ref[height : 2 * height, lanes] = jnp.where(
            wide_lower, pltpu.roll(one, K, 1), two
        ).astype(jnp.bfloat16)

    def spread(c, carry):
        s = coupling_ref[c]
        z = jnp.zeros((K, K), jnp.bfloat16)
        at = pl.multiple_of(c * 4 * K, 4 * K)
        for block in range(4):
            place = (0, 2, 1, 3)[block]
            bd_ref[pl.ds(at + block * K, K), :] = jnp.concatenate(
                [s if place == i else z for i in range(4)], axis=1
            )
        return carry

    lax.fori_loop(0, classes, spread, 0)

    for c in range(classes):
        grouped = dot(a_ref[c], call_ref[...]).astype(jnp.bfloat16)
        for m in range(N // 2):
            for parity in range(2):
                lhs_ref[
                    m * PAIRS : (m + 1) * PAIRS,
                    (2 * c + parity) * 2 * K : (2 * c + parity + 1) * 2 * K,
                ] = grouped[parity * PAIRS : (parity + 1) * PAIRS, m * 2 * K : (m + 1) * 2 * K]
    for m in range(N // 2):
        field = dot(lhs_ref[m * PAIRS : (m + 1) * PAIRS, :], bd_ref[...])
        fs_ref[2 * m * PAIRS : (2 * m + 1) * PAIRS, :] = field[:, 0 : 2 * K]
        fs_ref[(2 * m + 1) * PAIRS : (2 * m + 2) * PAIRS, :] = field[:, 2 * K : 4 * K]

    def field_of(pair_index):
        return fs_ref[pl.ds(pair_index, N, stride=PAIRS), :]

    def push(tile, matrix):
        none = jnp.zeros_like(tile)
        stacked = jnp.concatenate(
            [jnp.where(lower, tile, none), jnp.where(lower, none, tile)], axis=0
        ).astype(jnp.bfloat16)
        return dot(stacked, matrix)

    last = field_of(PAIRS - 1)
    top = last[:, K : 2 * K].astype(jnp.bfloat16)
    root = (last[:, 0:K] + dot(top, matrix_ref[0])).astype(jnp.bfloat16)
    tiles = {0: field_of(0) + dot(root, children_of(matrix_ref, 0))}
    for j in range(B // 2 - 1):
        both = push(tiles[j], links_of(matrix_ref, j))
        tiles[2 * j + 1] = field_of(2 * j + 1) + both[:N]
        tiles[2 * j + 2] = field_of(2 * j + 2) + both[N:]
    for i in range(B // 2):
        both = push(tiles[B // 2 - 1 + i], basis_ref[i])
        for h in range(2):
            lanes = slice((2 * i + h) * M, (2 * i + h + 1) * M)
            out_ref[:, lanes] = (near_ref[:, lanes] + both[h * N : (h + 1) * N]).astype(jnp.bfloat16)


def downward(low, own, high, tops, counts, coupling, matrices, basis, near):
    classes = counts.shape[0]
    height = counts.shape[2] // 2
    return pl.pallas_call(
        down_kernel,
        name="downward",
        out_shape=jax.ShapeDtypeStruct((N, B * M), jnp.bfloat16),
        in_specs=[vmem()] * 9,
        out_specs=vmem(),
        scratch_shapes=[
            pltpu.VMEM((N * height, 2 * K), jnp.float32),
            pltpu.VMEM((2 * height, N * K), jnp.bfloat16),
            pltpu.VMEM((classes * 4 * K, 4 * K), jnp.bfloat16),
            pltpu.VMEM((N // 2 * PAIRS, classes * 4 * K), jnp.bfloat16),
            pltpu.VMEM((N * PAIRS, 2 * K), jnp.float32),
        ],
        compiler_params=pltpu.CompilerParams(vmem_limit_bytes=40 << 20),
        cost_estimate=pl.CostEstimate(
            flops=4_000_000_000, bytes_accessed=6_000_000, transcendentals=0
        ),
    )(low, own, high, tops, counts, coupling, matrices, basis, near)


def source_columns(far_src, top_src, position, subtrees, height):
    owner = far_src // TB
    slot = far_src % TB
    count = jnp.ones_like(slot)
    for bit in range(1, 7):
        count = jnp.where(slot + 1 >= 2**bit, 2**bit, count)
    first = (count - 2) // 2
    inside = (slot - (count - 1)) // 2
    pairs = count // 2
    width = jnp.minimum(pairs, 7)
    rim_first = jnp.where(count <= 16, first, jnp.where(count == 32, 14, 21))
    side = owner - position
    row = jnp.where(
        side == 0,
        first + inside,
        jnp.where(
            side < 0,
            PAIRS + rim_first + inside - (pairs - width),
            PAIRS + RIM + rim_first + inside,
        ),
    )
    column = jnp.where(far_src >= 0, row + ((slot - 1) % 2) * height, -1)
    base = PAIRS + 2 * RIM
    roots = lax.dynamic_slice_in_dim(top_src, position, 1, 0)
    tops = lax.dynamic_slice_in_dim(top_src, subtrees + position // 2, 1, 0)
    roots = jnp.where(roots >= 0, base + roots, -1)
    tops = jnp.where(tops >= 0, height + base + 2 * tops, -1)
    return by_parity(column, roots, tops)


def by_parity(rows, root, top):
    paired = rows[1:].reshape(PAIRS - 1, 2, rows.shape[1])
    return jnp.concatenate([paired[:, 0], root, paired[:, 1], top], axis=0)


def per_device(
    values, coords, basis, transfer, coupling, near_src, far_src, far_cls, top_src, top_cls
):
    position = lax.axis_index("leaf")
    subtrees = lax.axis_size("leaf")
    class_count = coupling.shape[0]
    height = -(-(PAIRS + 2 * RIM + subtrees) // 64) * 64

    whole_basis = lax.all_gather(basis, "vec", axis=0, tiled=True)

    box = jnp.arange(B, dtype=jnp.int32)
    centre = jnp.stack(
        [box % ROW, box // ROW, jnp.full((B,), 0, jnp.int32) + position]
    ).astype(jnp.float32) + 0.5
    local = coords.reshape(3, B, M) - centre[:, :, None]
    flat = coords - jnp.repeat(centre, M, axis=1)
    coarse = rounded(flat)
    rest = rounded(flat - coarse)
    held = coarse + rest
    size = -SCALE * (held[0] ** 2 + held[1] ** 2 + held[2] ** 2)
    size_a = rounded(size)
    size_b = rounded(size - size_a)
    size_c = size - size_a - size_b
    rows = []
    for k in range(3):
        rows += [coarse[k], rest[k]]
    rows += [size_a, size_b, size_c, jnp.ones_like(size)]
    rows += [jnp.zeros_like(size)] * 6
    packed = jnp.concatenate([values, jnp.stack(rows).astype(jnp.bfloat16)], axis=0)
    forward = [(i, i + 1) for i in range(subtrees - 1)]
    backward = [(i + 1, i) for i in range(subtrees - 1)]
    from_low = lax.ppermute(packed, "leaf", forward)
    from_high = lax.ppermute(packed, "leaf", backward)

    moved = (
        jnp.transpose(local, (1, 0, 2))[:, :, None, None, :]
        - jnp.arange(-1, 2, dtype=jnp.float32)[None, None, :, None, None]
    )
    row = jnp.arange(16, dtype=jnp.int32)[None, None, None, :, None]
    term = jnp.where(
        row < 4,
        2 * SCALE * moved,
        -SCALE * moved * moved,
    )
    term_a = rounded(term)
    term_b = rounded(term - term_a)
    term_c = term - term_a - term_b
    x_tiles = jnp.where(
        (row < 2) | (row == 4),
        term_a,
        jnp.where((row < 4) | (row == 5), term_b, jnp.where(row == 6, term_c, 0.0)),
    )
    x_tiles = x_tiles.astype(jnp.bfloat16).reshape(B, 9, 16, M)

    matrices = transfer.reshape(TB, K, K)
    coupling_t = jnp.transpose(coupling.reshape(class_count, K, K), (0, 2, 1))

    columns = source_columns(far_src, top_src, position, subtrees, height)
    classes = by_parity(
        far_cls,
        lax.dynamic_slice_in_dim(top_cls, position, 1, 0),
        lax.dynamic_slice_in_dim(top_cls, subtrees + position // 2, 1, 0),
    )
    counts = class_counts(columns, classes, class_count, 2 * height)

    whole_basis, counts, x_tiles = lax.optimization_barrier((whole_basis, counts, x_tiles))
    basis_pairs = whole_basis.reshape(B // 2, 2 * K, M)
    coefs, first, last, root = upward(values, basis_pairs, matrices)
    tops = lax.all_gather(root, "leaf", axis=0)
    low = lax.ppermute(last, "leaf", forward)
    high = lax.ppermute(first, "leaf", backward)
    near = near_field(near_src, x_tiles, from_low, packed, from_high)
    return downward(low, coefs, high, tops, counts, coupling_t, matrices, basis_pairs, near)


def solution(mesh):
    in_specs = (
        P("vec", "leaf"),
        P(None, "leaf"),
        P(("leaf", "vec"), None, None),
        P("leaf", None),
        P(),
        P("leaf", None),
        P("leaf", None),
        P("leaf", None),
        P(),
        P(),
    )
    out_specs = P("vec", "leaf")
    return jax.shard_map(
        per_device, mesh=mesh, in_specs=in_specs, out_specs=out_specs, check_vma=False
    )
```

```python
import math

import jax
import jax.numpy as jnp
import numpy as np
from jax import lax
from jax.experimental import pallas as pl
from jax.experimental.pallas import tpu as pltpu
from jax.sharding import PartitionSpec as P

M = 128
K = 64
REACH = 13
TB = 127
ROW = 16
N = 16
B = 64
PAIRS = 64
RIM = 28

SCALE = math.log2(math.e) / 0.2
AMPLITUDE = 0.3
DEAD = -1000.0

NN = (((1,), (0,)), ((), ()))
NT = (((1,), (1,)), ((), ()))
TN = (((0,), (0,)), ((), ()))


def dot(a, b, dims=NN):
    return lax.dot_general(a, b, dims, preferred_element_type=jnp.float32)


def vmem():
    return pl.BlockSpec(memory_space=pltpu.VMEM)


def rounded(x):
    return lax.reduce_precision(x, 8, 7)


def near_tables():
    def split(value, parts):
        out = []
        for _ in range(parts):
            part = float(np.float32(np.asarray(value).astype(jnp.bfloat16)))
            out.append(part)
            value -= part
        return out

    one = 9
    lanes = []
    for k in range(3):
        high, rest = 2 * k, 2 * k + 1
        x_high, x_rest = 10 + 2 * k, 11 + 2 * k
        for y in (high, rest):
            for x in (x_high, x_rest):
                lanes.append((y, None, x, 1.0))
            for part in split(-2 * SCALE, 2):
                lanes.append((y, k, one, part))
        for x in (x_high, x_rest):
            lanes.append((one, k, x, 1.0))
    for row in (6, 7, 8):
        lanes.append((one, None, row, 1.0))
        lanes.append((row, None, one, 1.0))
    for part in split(-SCALE, 3):
        lanes.append((one, 3, one, part))
    lanes.append((one, 4, one, DEAD))
    source = np.zeros((32, 128), np.float32)
    target = np.zeros((64, 16), np.float32)
    factor = np.zeros((27, 16, 128), np.float32)
    dead = np.zeros((4, 16, 128), np.float32)
    for lane, (y, kind, x, part) in enumerate(lanes):
        target[lane, x] = part
        for half in range(2):
            at = 64 * half + lane
            source[16 * half + y, at] = 1
            for slot in range(27):
                step = (slot % 3 - 1, slot // 3 % 3 - 1, slot // 9 - 1)
                if kind is None:
                    factor[slot, :, at] = 1
                elif kind < 3:
                    factor[slot, :, at] = step[kind]
                elif kind == 3:
                    factor[slot, :, at] = sum(d * d for d in step)
            if kind == 4:
                for flags in range(4):
                    dead[flags, :, at] = flags >> half & 1
    return [jnp.asarray(x, jnp.bfloat16) for x in (source, target, factor, dead)]


def near_kernel(
    near_ref, low_ref, own_ref, high_ref, source_ref, target_ref, factor_ref, dead_ref, out_ref, yp_ref
):
    layers = (low_ref, own_ref, high_ref)

    def at(u):
        return pl.ds(pl.multiple_of(jnp.clip(u, 0, B - 1) * M, M), M)

    for l, src in enumerate(layers):

        def features(u, carry, l=l, src=src):
            both = jnp.concatenate([src[16:32, at(u - 1)], src[16:32, at(u)]], axis=0)
            yp_ref[l, u] = dot(both, source_ref[...], TN).astype(jnp.bfloat16)
            return carry

        lax.fori_loop(0, B + 1, features, 0, unroll=5)

    zero = jnp.zeros((64, M), jnp.bfloat16)

    def target(t):
        return dot(target_ref[...], own_ref[16:32, at(t)]).astype(jnp.bfloat16)

    def pair(t, steps):
        w = jnp.concatenate(
            [
                jnp.concatenate([target(t), zero], axis=1),
                jnp.concatenate([zero, target(t + 1)], axis=1),
            ],
            axis=0,
        )
        kernels, vectors = [], []
        for c in range(3):
            src = layers[c]
            for b in steps:
                for a in range(3):
                    slot = 9 * c + 3 * b + a
                    u = t + (b - 1) * ROW + a - 1
                    flags = jnp.where(near_ref[t, slot] < 0, 1, 0) + jnp.where(
                        near_ref[t + 1, slot] < 0, 2, 0
                    )
                    factor = factor_ref[slot] + dead_ref[flags]
                    left = yp_ref[c, u + 1] * jnp.concatenate([factor] * 8, axis=0)
                    kernels.append(jnp.exp2(dot(left, w)).astype(jnp.bfloat16))
                    vectors.append(jnp.concatenate([src[0:16, at(u)], src[0:16, at(u + 1)]], axis=0))
        total = dot(jnp.concatenate(vectors, axis=1), jnp.concatenate(kernels, axis=0))
        out_ref[:, at(t)] = AMPLITUDE * total[0:16, 0:M]
        out_ref[:, at(t + 1)] = AMPLITUDE * total[16:32, M : 2 * M]

    rows = B // ROW
    for first, last, steps in ((0, 1, (1, 2)), (1, rows - 1, (0, 1, 2)), (rows - 1, rows, (0, 1))):

        def step(q, carry, first=first, steps=steps):
            t = first * ROW + 4 * q
            pair(t, steps)
            pair(t + 2, steps)
            return carry

        lax.fori_loop(0, (last - first) * ROW // 4, step, 0)


def near_field(near_src, low, own, high):
    return pl.pallas_call(
        near_kernel,
        name="near_field",
        out_shape=jax.ShapeDtypeStruct((N, B * M), jnp.float32),
        in_specs=[pl.BlockSpec(memory_space=pltpu.SMEM)] + [vmem()] * 7,
        out_specs=vmem(),
        scratch_shapes=[pltpu.VMEM((3, B + 1, M, M), jnp.bfloat16)],
        compiler_params=pltpu.CompilerParams(vmem_limit_bytes=40 << 20),
        cost_estimate=pl.CostEstimate(
            flops=20_000_000_000, bytes_accessed=5_000_000, transcendentals=28_000_000
        ),
    )(near_src, low, own, high, *near_tables())


def relay_kernel(transfer_ref, coupling_ref, links_ref, coupling_t_ref, flat_ref, pair_ref):
    lower = lax.broadcasted_iota(jnp.int32, (K // 2, 2 * K), 1) < K

    def unpack(ref):
        for i in range(K // 2):
            flat_ref[pl.ds(i, ref.shape[0], stride=K // 2), :] = ref[
                :, 2 * K * i : 2 * K * (i + 1)
            ].astype(jnp.float32)

    def join(left, right):
        one = flat_ref[left * (K // 2) : (left + 1) * (K // 2), :]
        two = flat_ref[right * (K // 2) : (right + 1) * (K // 2), :]
        pair_ref[pl.ds(0, K // 2, stride=2), :] = jnp.where(lower, one, pltpu.roll(two, K, 1))
        pair_ref[pl.ds(1, K // 2, stride=2), :] = jnp.where(lower, pltpu.roll(one, K, 1), two)
        return pair_ref[...]

    unpack(transfer_ref)
    for p in range(PAIRS - 1):
        links_ref[p] = join(2 * p + 1, 2 * p + 2).astype(jnp.bfloat16)
    links_ref[PAIRS - 1] = join(0, 0).astype(jnp.bfloat16)
    unpack(coupling_ref)
    for p in range(coupling_ref.shape[0] // 2):
        both = jnp.transpose(join(2 * p, 2 * p + 1)).astype(jnp.bfloat16)
        coupling_t_ref[2 * p] = both[0:K]
        coupling_t_ref[2 * p + 1] = both[K : 2 * K]


def relay(transfer, coupling):
    return pl.pallas_call(
        relay_kernel,
        name="relay",
        out_shape=[
            jax.ShapeDtypeStruct((PAIRS, K, 2 * K), jnp.bfloat16),
            jax.ShapeDtypeStruct((coupling.shape[0], K, K), jnp.bfloat16),
        ],
        in_specs=[vmem()] * 2,
        out_specs=[vmem()] * 2,
        scratch_shapes=[
            pltpu.VMEM(((TB + 1) * K // 2, 2 * K), jnp.float32),
            pltpu.VMEM((K, 2 * K), jnp.float32),
        ],
        compiler_params=pltpu.CompilerParams(vmem_limit_bytes=16 << 20),
        cost_estimate=pl.CostEstimate(flops=1000, bytes_accessed=100_000, transcendentals=0),
    )(transfer, coupling)


def counts_kernel(col_ref, cls_ref, a_ref):
    classes = a_ref.shape[0]
    width = a_ref.shape[2]
    slots = col_ref.shape[1]
    spread = slots * 8
    lane = lax.broadcasted_iota(jnp.int32, (slots, spread), 1)
    copies = (lane // 8 == lax.broadcasted_iota(jnp.int32, (slots, spread), 0)).astype(jnp.float32)
    columns = lax.broadcasted_iota(jnp.int32, (8, width), 1)
    match = (
        lax.broadcasted_iota(jnp.int32, (8, spread), 1) % 8
        == lax.broadcasted_iota(jnp.int32, (8, spread), 0)
    )

    def block(g, carry):
        halves = []
        for h in range(2):
            rows = pl.ds(pl.multiple_of(g * 16 + h * 8, 8), 8)
            col = col_ref[rows, :]
            wide = dot(cls_ref[rows, :].astype(jnp.float32), copies).astype(jnp.int32)
            wide = jnp.where(match, wide, -1)
            left = jnp.concatenate(
                [jnp.where(wide == c, 1.0, 0.0) for c in range(classes)], axis=0
            ).astype(jnp.bfloat16)
            right = jnp.concatenate(
                [jnp.where(col[:, e : e + 1] == columns, 1.0, 0.0) for e in range(slots)], axis=0
            ).astype(jnp.bfloat16)
            halves.append(dot(left, right))
        for c in range(classes):
            both = jnp.concatenate([half[8 * c : 8 * c + 8] for half in halves], axis=0)
            a_ref[c, pl.ds(pl.multiple_of(g * 16, 16), 16), :] = both.astype(jnp.bfloat16)
        return carry

    lax.fori_loop(0, 2 * PAIRS // 16, block, 0)


def class_counts(columns, classes, class_count, width):
    return pl.pallas_call(
        counts_kernel,
        name="class_counts",
        out_shape=jax.ShapeDtypeStruct((class_count, 2 * PAIRS, width), jnp.bfloat16),
        in_specs=[vmem()] * 2,
        out_specs=vmem(),
        compiler_params=pltpu.CompilerParams(vmem_limit_bytes=20 << 20),
        cost_estimate=pl.CostEstimate(
            flops=1000, bytes_accessed=100_000, transcendentals=0
        ),
    )(columns, classes)


FIRST_ROWS = tuple(range(14)) + tuple(range(15, 22)) + tuple(range(31, 38))
LAST_ROWS = tuple(range(7)) + tuple(range(8, 15)) + tuple(range(24, 31)) + tuple(range(56, 63))
RIM_ROWS = 32


def links_of(links_ref, pair_index):
    return jnp.concatenate([links_ref[2 * pair_index + 1], links_ref[2 * pair_index + 2]], axis=0)


def up_kernel(
    values_ref, basis_ref, links_ref, out_ref, first_ref, last_ref, root_ref, cs_ref, fs_ref, ls_ref
):
    lower = lax.broadcasted_iota(jnp.int32, (N, 2 * K), 1) < K

    def keep(pair_index, tile):
        cs_ref[pl.ds(pair_index, N, stride=PAIRS), :] = tile
        for rows, ref in ((FIRST_ROWS, fs_ref), (LAST_ROWS, ls_ref)):
            if pair_index in rows:
                ref[pl.ds(rows.index(pair_index), N, stride=RIM_ROWS), :] = tile

    def lift(stacked, matrix):
        both = dot(stacked, matrix, NT)
        return jnp.where(lower, both[:N], both[N:]).astype(jnp.bfloat16)

    tiles = {}
    for i in range(B // 2):
        stacked = jnp.concatenate(
            [values_ref[:, 2 * i * M : (2 * i + 1) * M], values_ref[:, (2 * i + 1) * M : (2 * i + 2) * M]],
            axis=0,
        )
        tiles[B // 2 - 1 + i] = lift(stacked, basis_ref[i])
        keep(B // 2 - 1 + i, tiles[B // 2 - 1 + i].astype(jnp.float32))
    for j in reversed(range(B // 2 - 1)):
        stacked = jnp.concatenate([tiles[2 * j + 1], tiles[2 * j + 2]], axis=0)
        tiles[j] = lift(stacked, links_of(links_ref, j))
        keep(j, tiles[j].astype(jnp.float32))
    root = dot(tiles[0], links_ref[0], NT).astype(jnp.bfloat16)
    up = dot(root, links_ref[PAIRS - 1][:, 0:K], NT)
    last = jnp.concatenate([root.astype(jnp.float32), up], axis=1)
    keep(PAIRS - 1, last)
    root_ref[0] = last.astype(jnp.bfloat16)
    root_ref[1:] = jnp.zeros((N - 1, N, 2 * K), jnp.bfloat16)
    for n in range(N):
        out_ref[n] = cs_ref[n * PAIRS : (n + 1) * PAIRS, :].astype(jnp.bfloat16)
        for source, target in ((fs_ref, first_ref), (ls_ref, last_ref)):
            base = n * RIM_ROWS
            source[base + RIM : base + RIM_ROWS, :] = jnp.zeros((RIM_ROWS - RIM, 2 * K), jnp.float32)
            target[n] = source[base : base + RIM_ROWS, :].astype(jnp.bfloat16)


def upward(values, basis, links):
    return pl.pallas_call(
        up_kernel,
        name="upward",
        out_shape=[
            jax.ShapeDtypeStruct((N, PAIRS, 2 * K), jnp.bfloat16),
            jax.ShapeDtypeStruct((N, RIM_ROWS, 2 * K), jnp.bfloat16),
            jax.ShapeDtypeStruct((N, RIM_ROWS, 2 * K), jnp.bfloat16),
            jax.ShapeDtypeStruct((N, N, 2 * K), jnp.bfloat16),
        ],
        in_specs=[vmem()] * 3,
        out_specs=[vmem()] * 4,
        scratch_shapes=[
            pltpu.VMEM((N * PAIRS, 2 * K), jnp.float32),
            pltpu.VMEM((N * RIM_ROWS, 2 * K), jnp.float32),
            pltpu.VMEM((N * RIM_ROWS, 2 * K), jnp.float32),
        ],
        compiler_params=pltpu.CompilerParams(vmem_limit_bytes=20 << 20),
        cost_estimate=pl.CostEstimate(
            flops=300_000_000, bytes_accessed=3_000_000, transcendentals=0
        ),
    )(values, basis, links)


def down_kernel(
    low_ref,
    own_ref,
    high_ref,
    tops_ref,
    a_ref,
    coupling_ref,
    links_ref,
    basis_ref,
    near_ref,
    out_ref,
    cf_ref,
    call_ref,
    bd_ref,
    lhs_ref,
    fs_ref,
):
    classes = a_ref.shape[0]
    height = a_ref.shape[2] // 2
    subtrees = tops_ref.shape[0]
    lower = lax.broadcasted_iota(jnp.int32, (N, 2 * K), 1) < K

    used = PAIRS + 2 * RIM + subtrees
    for n in range(N):
        base = n * height
        cf_ref[base : base + PAIRS, :] = own_ref[n].astype(jnp.float32)
        at = base + PAIRS
        cf_ref[at : at + RIM, :] = low_ref[n].astype(jnp.float32)[:RIM]
        at += RIM
        cf_ref[at : at + RIM, :] = high_ref[n].astype(jnp.float32)[:RIM]
        if used < height:
            cf_ref[base + used : base + height, :] = jnp.zeros((height - used, 2 * K), jnp.float32)
    for q in range(subtrees // 2):
        even = tops_ref[2 * q, 0].astype(jnp.float32)
        odd = tops_ref[2 * q + 1, 0].astype(jnp.float32)
        at = PAIRS + 2 * RIM + 2 * q
        cf_ref[pl.ds(at, N, stride=height), :] = jnp.where(lower, even, even + odd)
        cf_ref[pl.ds(at + 1, N, stride=height), :] = odd
    wide_lower = lax.broadcasted_iota(jnp.int32, (height, 2 * K), 1) < K
    for m in range(N // 2):
        one = cf_ref[2 * m * height : (2 * m + 1) * height, :]
        two = cf_ref[(2 * m + 1) * height : (2 * m + 2) * height, :]
        lanes = slice(m * 2 * K, (m + 1) * 2 * K)
        call_ref[0:height, lanes] = jnp.where(
            wide_lower, one, pltpu.roll(two, K, 1)
        ).astype(jnp.bfloat16)
        call_ref[height : 2 * height, lanes] = jnp.where(
            wide_lower, pltpu.roll(one, K, 1), two
        ).astype(jnp.bfloat16)

    def spread(c, carry):
        s = coupling_ref[c]
        z = jnp.zeros((K, K), jnp.bfloat16)
        at = pl.multiple_of(c * 4 * K, 4 * K)
        for block in range(4):
            place = (0, 2, 1, 3)[block]
            bd_ref[pl.ds(at + block * K, K), :] = jnp.concatenate(
                [s if place == i else z for i in range(4)], axis=1
            )
        return carry

    lax.fori_loop(0, classes, spread, 0)

    for c in range(classes):
        grouped = dot(a_ref[c], call_ref[...]).astype(jnp.bfloat16)
        for m in range(N // 2):
            for parity in range(2):
                lhs_ref[
                    m * PAIRS : (m + 1) * PAIRS,
                    (2 * c + parity) * 2 * K : (2 * c + parity + 1) * 2 * K,
                ] = grouped[parity * PAIRS : (parity + 1) * PAIRS, m * 2 * K : (m + 1) * 2 * K]
    for m in range(N // 2):
        field = dot(lhs_ref[m * PAIRS : (m + 1) * PAIRS, :], bd_ref[...])
        fs_ref[2 * m * PAIRS : (2 * m + 1) * PAIRS, :] = field[:, 0 : 2 * K]
        fs_ref[(2 * m + 1) * PAIRS : (2 * m + 2) * PAIRS, :] = field[:, 2 * K : 4 * K]

    def field_of(pair_index):
        return fs_ref[pl.ds(pair_index, N, stride=PAIRS), :]

    def push(tile, matrix):
        none = jnp.zeros_like(tile)
        stacked = jnp.concatenate(
            [jnp.where(lower, tile, none), jnp.where(lower, none, tile)], axis=0
        ).astype(jnp.bfloat16)
        return dot(stacked, matrix)

    last = field_of(PAIRS - 1)
    top = last[:, K : 2 * K].astype(jnp.bfloat16)
    root = (last[:, 0:K] + dot(top, links_ref[PAIRS - 1][:, 0:K])).astype(jnp.bfloat16)
    tiles = {0: field_of(0) + dot(root, links_ref[0])}
    for j in range(B // 2 - 1):
        both = push(tiles[j], links_of(links_ref, j))
        tiles[2 * j + 1] = field_of(2 * j + 1) + both[:N]
        tiles[2 * j + 2] = field_of(2 * j + 2) + both[N:]
    for i in range(B // 2):
        both = push(tiles[B // 2 - 1 + i], basis_ref[i])
        for h in range(2):
            lanes = slice((2 * i + h) * M, (2 * i + h + 1) * M)
            out_ref[:, lanes] = (near_ref[:, lanes] + both[h * N : (h + 1) * N]).astype(jnp.bfloat16)


def downward(low, own, high, tops, counts, coupling, links, basis, near):
    classes = counts.shape[0]
    height = counts.shape[2] // 2
    return pl.pallas_call(
        down_kernel,
        name="downward",
        out_shape=jax.ShapeDtypeStruct((N, B * M), jnp.bfloat16),
        in_specs=[vmem()] * 9,
        out_specs=vmem(),
        scratch_shapes=[
            pltpu.VMEM((N * height, 2 * K), jnp.float32),
            pltpu.VMEM((2 * height, N * K), jnp.bfloat16),
            pltpu.VMEM((classes * 4 * K, 4 * K), jnp.bfloat16),
            pltpu.VMEM((N // 2 * PAIRS, classes * 4 * K), jnp.bfloat16),
            pltpu.VMEM((N * PAIRS, 2 * K), jnp.float32),
        ],
        compiler_params=pltpu.CompilerParams(vmem_limit_bytes=40 << 20),
        cost_estimate=pl.CostEstimate(
            flops=4_000_000_000, bytes_accessed=6_000_000, transcendentals=0
        ),
    )(low, own, high, tops, counts, coupling, links, basis, near)


def source_columns(far_src, top_src, position, subtrees, height):
    owner = far_src // TB
    slot = far_src % TB
    count = jnp.ones_like(slot)
    for bit in range(1, 7):
        count = jnp.where(slot + 1 >= 2**bit, 2**bit, count)
    first = (count - 2) // 2
    inside = (slot - (count - 1)) // 2
    pairs = count // 2
    width = jnp.minimum(pairs, 7)
    rim_first = jnp.where(count <= 16, first, jnp.where(count == 32, 14, 21))
    side = owner - position
    row = jnp.where(
        side == 0,
        first + inside,
        jnp.where(
            side < 0,
            PAIRS + rim_first + inside - (pairs - width),
            PAIRS + RIM + rim_first + inside,
        ),
    )
    column = jnp.where(far_src >= 0, row + ((slot - 1) % 2) * height, -1)
    base = PAIRS + 2 * RIM
    roots = lax.dynamic_slice_in_dim(top_src, position, 1, 0)
    tops = lax.dynamic_slice_in_dim(top_src, subtrees + position // 2, 1, 0)
    roots = jnp.where(roots >= 0, base + roots, -1)
    tops = jnp.where(tops >= 0, height + base + 2 * tops, -1)
    return by_parity(column, roots, tops)


def by_parity(rows, root, top):
    paired = rows[1:].reshape(PAIRS - 1, 2, rows.shape[1])
    return jnp.concatenate([paired[:, 0], root, paired[:, 1], top], axis=0)


def per_device(
    values, coords, basis, transfer, coupling, near_src, far_src, far_cls, top_src, top_cls
):
    position = lax.axis_index("leaf")
    subtrees = lax.axis_size("leaf")
    class_count = coupling.shape[0]
    height = -(-(PAIRS + 2 * RIM + subtrees) // 64) * 64

    whole_basis = lax.all_gather(basis, "vec", axis=0, tiled=True)

    box = jnp.arange(B, dtype=jnp.int32)
    centre = jnp.stack(
        [box % ROW, box // ROW, jnp.full((B,), 0, jnp.int32) + position]
    ).astype(jnp.float32) + 0.5
    flat = coords - jnp.repeat(centre, M, axis=1)
    coarse = rounded(flat)
    rest = rounded(flat - coarse)
    held = coarse + rest
    size = -SCALE * (held[0] ** 2 + held[1] ** 2 + held[2] ** 2)
    size_a = rounded(size)
    size_b = rounded(size - size_a)
    size_c = size - size_a - size_b
    rows = []
    for k in range(3):
        rows += [coarse[k], rest[k]]
    rows += [size_a, size_b, size_c, jnp.ones_like(size)]
    doubled = 2 * SCALE * flat
    doubled_a = rounded(doubled)
    doubled_b = rounded(doubled - doubled_a)
    for k in range(3):
        rows += [doubled_a[k], doubled_b[k]]
    packed = jnp.concatenate([values, jnp.stack(rows).astype(jnp.bfloat16)], axis=0)
    links, coupling_t = relay(transfer, coupling)
    columns = source_columns(far_src, top_src, position, subtrees, height)
    classes = by_parity(
        far_cls,
        lax.dynamic_slice_in_dim(top_cls, position, 1, 0),
        lax.dynamic_slice_in_dim(top_cls, subtrees + position // 2, 1, 0),
    )
    counts = class_counts(columns, classes, class_count, 2 * height)

    packed, counts, links = lax.optimization_barrier((packed, counts, links))
    forward = [(i, i + 1) for i in range(subtrees - 1)]
    backward = [(i + 1, i) for i in range(subtrees - 1)]
    from_low = lax.ppermute(packed, "leaf", forward)
    from_high = lax.ppermute(packed, "leaf", backward)
    whole_basis, counts, links = lax.optimization_barrier((whole_basis, counts, links))
    basis_pairs = whole_basis.reshape(B // 2, 2 * K, M)
    coefs, first, last, root = upward(values, basis_pairs, links)
    tops = lax.all_gather(root, "leaf", axis=0)
    low = lax.ppermute(last, "leaf", forward)
    high = lax.ppermute(first, "leaf", backward)
    near = near_field(near_src, from_low, packed, from_high)
    return downward(low, coefs, high, tops, counts, coupling_t, links, basis_pairs, near)


def solution(mesh):
    in_specs = (
        P("vec", "leaf"),
        P(None, "leaf"),
        P(("leaf", "vec"), None, None),
        P("leaf", None),
        P(),
        P("leaf", None),
        P("leaf", None),
        P("leaf", None),
        P(),
        P(),
    )
    out_specs = P("vec", "leaf")
    return jax.shard_map(
        per_device, mesh=mesh, in_specs=in_specs, out_specs=out_specs, check_vma=False
    )
```

```python
import jax
import jax.numpy as jnp
import numpy as np
from jax import lax
from jax.experimental import pallas as pl
from jax.experimental.pallas import tpu as pltpu
from jax.sharding import PartitionSpec as P

M = 128
K = 64
REACH = 13
TB = 127
ROW = 16
N = 16
B = 64
PAIRS = 64
RIM = 28

AMPLITUDE = 0.3
DEAD = -1000.0

NN = (((1,), (0,)), ((), ()))
NT = (((1,), (1,)), ((), ()))
TN = (((0,), (0,)), ((), ()))


def dot(a, b, dims=NN):
    return lax.dot_general(a, b, dims, preferred_element_type=jnp.float32)


def vmem():
    return pl.BlockSpec(memory_space=pltpu.VMEM)


def rounded(x):
    return lax.reduce_precision(x, 8, 7)


def near_tables():
    one = 8
    source = np.zeros((32, 128), np.float32)
    target = np.zeros((11 * 16, 32), np.float32)

    def lane(at, y):
        for half in range(2):
            source[(8 * half + y) if y < one else 16, 64 * half + at] = 1

    def row(tile, at, x, factor):
        target[16 * tile + at, x if x < one else 16] = factor

    for k in range(3):
        parts = [(x, p) for x in (2 * k, 2 * k + 1) for p in (8, 2)]
        terms = [(y, x, p, None) for y in (2 * k, 2 * k + 1) for x, p in parts]
        terms += [(y, one, -10, 1) for y in (2 * k, 2 * k + 1)]
        terms += [(one, x, p, 1) for x, p in parts]
        terms += [(one, one, -5, 2)]
        for at, (y, x, factor, power) in enumerate(terms):
            lane(16 * k + at, y)
            for step in range(3):
                scale = 1 if power is None else (step - 1) ** power
                row(3 * k + step, at, x, factor * scale)
    for at, (y, x) in enumerate(((6, one), (7, one), (one, 6), (one, 7))):
        lane(48 + at, y)
        for tile in (9, 10):
            row(tile, at, x, 1)
    lane(52, one)
    row(10, 4, one, DEAD)
    return [jnp.asarray(x, jnp.bfloat16) for x in (source, target)]


def near_kernel(
    near_ref, low_ref, own_ref, high_ref, source_ref, target_ref, out_ref, yp_ref, x_ref
):
    layers = (low_ref, own_ref, high_ref)
    ones = jnp.ones((16, M), jnp.float32)

    def at(u):
        return pl.ds(pl.multiple_of(jnp.clip(u, 0, B - 1) * M, M), M)

    def points(ref, first, second):
        two = [ref[:, at(u)].astype(jnp.float32)[16:24] for u in (first, second)]
        return jnp.concatenate(two + [ones], axis=0).astype(jnp.bfloat16)

    for l, src in enumerate(layers):

        def features(u, carry, l=l, src=src):
            yp_ref[l, u] = dot(points(src, u - 1, u), source_ref[...], TN).astype(jnp.bfloat16)
            return carry

        lax.fori_loop(0, B + 1, features, 0, unroll=13)

    def targets(t, carry):
        x_ref[t] = dot(target_ref[...], points(own_ref, t, t)).astype(jnp.bfloat16)
        return carry

    lax.fori_loop(0, B, targets, 0, unroll=8)

    zero = jnp.zeros((64, M), jnp.bfloat16)

    def weights(t, a, b, c, slot):
        last = jnp.where(near_ref[t, slot] >= 0, 9, 10) * 16
        tiles = [x_ref[t, 16 * i : 16 * (i + 1), :] for i in (a, 3 + b, 6 + c)]
        return jnp.concatenate(tiles + [x_ref[t, pl.ds(pl.multiple_of(last, 16), 16), :]], axis=0)

    def kernel(t, a, b, c):
        slot = 9 * c + 3 * b + a
        u = t + (b - 1) * ROW + a - 1
        w = jnp.concatenate(
            [
                jnp.concatenate([weights(t, a, b, c, slot), zero], axis=1),
                jnp.concatenate([zero, weights(t + 1, a, b, c, slot)], axis=1),
            ],
            axis=0,
        )
        src = layers[c]
        vectors = jnp.concatenate([src[0:16, at(u)], src[0:16, at(u + 1)]], axis=0)
        return vectors, jnp.exp(dot(yp_ref[c, u + 1], w)).astype(jnp.bfloat16)

    rows = B // ROW
    for first, last, steps in ((0, 1, (1, 2)), (1, rows - 1, (0, 1, 2)), (rows - 1, rows, (0, 1))):
        slots = [(a, b, c) for c in range(3) for b in steps for a in range(3)]
        groups = [slots[i : i + 2] for i in range(0, len(slots), 2)]

        def step(q, carry, first=first, groups=groups):
            pairs = [first * ROW + 4 * q, first * ROW + 4 * q + 2]
            totals = [jnp.zeros((32, 2 * M), jnp.float32) for _ in pairs]
            for group in groups:
                for p, t in enumerate(pairs):
                    both = [kernel(t, *slot) for slot in group]
                    totals[p] += dot(
                        jnp.concatenate([v for v, _ in both], axis=1),
                        jnp.concatenate([k for _, k in both], axis=0),
                    )
            for p, t in enumerate(pairs):
                out_ref[:, at(t)] = AMPLITUDE * totals[p][0:16, 0:M]
                out_ref[:, at(t + 1)] = AMPLITUDE * totals[p][16:32, M : 2 * M]
            return carry

        lax.fori_loop(0, (last - first) * ROW // 4, step, 0)


def near_field(near_src, low, own, high):
    return pl.pallas_call(
        near_kernel,
        name="near_field",
        out_shape=jax.ShapeDtypeStruct((N, B * M), jnp.float32),
        in_specs=[pl.BlockSpec(memory_space=pltpu.SMEM)] + [vmem()] * 5,
        out_specs=vmem(),
        scratch_shapes=[
            pltpu.VMEM((3, B + 1, M, M), jnp.bfloat16),
            pltpu.VMEM((B, 11 * 16, M), jnp.bfloat16),
        ],
        compiler_params=pltpu.CompilerParams(vmem_limit_bytes=40 << 20),
        cost_estimate=pl.CostEstimate(
            flops=20_000_000_000, bytes_accessed=5_000_000, transcendentals=28_000_000
        ),
    )(near_src, low, own, high, *near_tables())


def relay_kernel(transfer_ref, coupling_ref, links_ref, coupling_t_ref, flat_ref, pair_ref):
    lower = lax.broadcasted_iota(jnp.int32, (K // 2, 2 * K), 1) < K

    def unpack(ref):
        for i in range(K // 2):
            flat_ref[pl.ds(i, ref.shape[0], stride=K // 2), :] = ref[
                :, 2 * K * i : 2 * K * (i + 1)
            ].astype(jnp.float32)

    def join(left, right):
        one = flat_ref[left * (K // 2) : (left + 1) * (K // 2), :]
        two = flat_ref[right * (K // 2) : (right + 1) * (K // 2), :]
        pair_ref[pl.ds(0, K // 2, stride=2), :] = jnp.where(lower, one, pltpu.roll(two, K, 1))
        pair_ref[pl.ds(1, K // 2, stride=2), :] = jnp.where(lower, pltpu.roll(one, K, 1), two)
        return pair_ref[...]

    unpack(transfer_ref)
    for p in range(PAIRS - 1):
        links_ref[p] = join(2 * p + 1, 2 * p + 2).astype(jnp.bfloat16)
    links_ref[PAIRS - 1] = join(0, 0).astype(jnp.bfloat16)
    unpack(coupling_ref)
    for p in range(coupling_ref.shape[0] // 2):
        both = jnp.transpose(join(2 * p, 2 * p + 1)).astype(jnp.bfloat16)
        coupling_t_ref[2 * p] = both[0:K]
        coupling_t_ref[2 * p + 1] = both[K : 2 * K]


def relay(transfer, coupling):
    return pl.pallas_call(
        relay_kernel,
        name="relay",
        out_shape=[
            jax.ShapeDtypeStruct((PAIRS, K, 2 * K), jnp.bfloat16),
            jax.ShapeDtypeStruct((coupling.shape[0], K, K), jnp.bfloat16),
        ],
        in_specs=[vmem()] * 2,
        out_specs=[vmem()] * 2,
        scratch_shapes=[
            pltpu.VMEM(((TB + 1) * K // 2, 2 * K), jnp.float32),
            pltpu.VMEM((K, 2 * K), jnp.float32),
        ],
        compiler_params=pltpu.CompilerParams(vmem_limit_bytes=16 << 20),
        cost_estimate=pl.CostEstimate(flops=1000, bytes_accessed=100_000, transcendentals=0),
    )(transfer, coupling)


def counts_kernel(col_ref, cls_ref, a_ref):
    classes = a_ref.shape[0]
    width = a_ref.shape[2]
    slots = col_ref.shape[1]
    spread = slots * 8
    lane = lax.broadcasted_iota(jnp.int32, (slots, spread), 1)
    copies = (lane // 8 == lax.broadcasted_iota(jnp.int32, (slots, spread), 0)).astype(jnp.float32)
    columns = lax.broadcasted_iota(jnp.int32, (8, width), 1)
    match = (
        lax.broadcasted_iota(jnp.int32, (8, spread), 1) % 8
        == lax.broadcasted_iota(jnp.int32, (8, spread), 0)
    )

    def block(g, carry):
        halves = []
        for h in range(2):
            rows = pl.ds(pl.multiple_of(g * 16 + h * 8, 8), 8)
            col = col_ref[rows, :]
            wide = dot(cls_ref[rows, :].astype(jnp.float32), copies).astype(jnp.int32)
            wide = jnp.where(match, wide, -1)
            left = jnp.concatenate(
                [jnp.where(wide == c, 1.0, 0.0) for c in range(classes)], axis=0
            ).astype(jnp.bfloat16)
            right = jnp.concatenate(
                [jnp.where(col[:, e : e + 1] == columns, 1.0, 0.0) for e in range(slots)], axis=0
            ).astype(jnp.bfloat16)
            halves.append(dot(left, right))
        for c in range(classes):
            both = jnp.concatenate([half[8 * c : 8 * c + 8] for half in halves], axis=0)
            a_ref[c, pl.ds(pl.multiple_of(g * 16, 16), 16), :] = both.astype(jnp.bfloat16)
        return carry

    lax.fori_loop(0, 2 * PAIRS // 16, block, 0)


def class_counts(columns, classes, class_count, width):
    return pl.pallas_call(
        counts_kernel,
        name="class_counts",
        out_shape=jax.ShapeDtypeStruct((class_count, 2 * PAIRS, width), jnp.bfloat16),
        in_specs=[vmem()] * 2,
        out_specs=vmem(),
        compiler_params=pltpu.CompilerParams(vmem_limit_bytes=20 << 20),
        cost_estimate=pl.CostEstimate(
            flops=1000, bytes_accessed=100_000, transcendentals=0
        ),
    )(columns, classes)


FIRST_ROWS = tuple(range(14)) + tuple(range(15, 22)) + tuple(range(31, 38))
LAST_ROWS = tuple(range(7)) + tuple(range(8, 15)) + tuple(range(24, 31)) + tuple(range(56, 63))
RIM_ROWS = 32


def links_of(links_ref, pair_index):
    return jnp.concatenate([links_ref[2 * pair_index + 1], links_ref[2 * pair_index + 2]], axis=0)


def up_kernel(
    values_ref, basis_ref, links_ref, out_ref, first_ref, last_ref, root_ref, cs_ref, fs_ref, ls_ref
):
    lower = lax.broadcasted_iota(jnp.int32, (N, 2 * K), 1) < K

    def keep(pair_index, tile):
        cs_ref[pl.ds(pair_index, N, stride=PAIRS), :] = tile
        for rows, ref in ((FIRST_ROWS, fs_ref), (LAST_ROWS, ls_ref)):
            if pair_index in rows:
                ref[pl.ds(rows.index(pair_index), N, stride=RIM_ROWS), :] = tile

    def lift(stacked, matrix):
        both = dot(stacked, matrix, NT)
        return jnp.where(lower, both[:N], both[N:]).astype(jnp.bfloat16)

    tiles = {}
    for i in range(B // 2):
        stacked = jnp.concatenate(
            [values_ref[:, 2 * i * M : (2 * i + 1) * M], values_ref[:, (2 * i + 1) * M : (2 * i + 2) * M]],
            axis=0,
        )
        tiles[B // 2 - 1 + i] = lift(stacked, basis_ref[i])
        keep(B // 2 - 1 + i, tiles[B // 2 - 1 + i].astype(jnp.float32))
    for j in reversed(range(B // 2 - 1)):
        stacked = jnp.concatenate([tiles[2 * j + 1], tiles[2 * j + 2]], axis=0)
        tiles[j] = lift(stacked, links_of(links_ref, j))
        keep(j, tiles[j].astype(jnp.float32))
    root = dot(tiles[0], links_ref[0], NT).astype(jnp.bfloat16)
    up = dot(root, links_ref[PAIRS - 1][:, 0:K], NT)
    last = jnp.concatenate([root.astype(jnp.float32), up], axis=1)
    keep(PAIRS - 1, last)
    root_ref[0] = last.astype(jnp.bfloat16)
    root_ref[1:] = jnp.zeros((2 * N - 1, N, 2 * K), jnp.bfloat16)
    for n in range(N):
        out_ref[n] = cs_ref[n * PAIRS : (n + 1) * PAIRS, :].astype(jnp.bfloat16)
        for source, target in ((fs_ref, first_ref), (ls_ref, last_ref)):
            base = n * RIM_ROWS
            source[base + RIM : base + RIM_ROWS, :] = jnp.zeros((RIM_ROWS - RIM, 2 * K), jnp.float32)
            target[n] = source[base : base + RIM_ROWS, :].astype(jnp.bfloat16)


def upward(values, basis, links):
    return pl.pallas_call(
        up_kernel,
        name="upward",
        out_shape=[
            jax.ShapeDtypeStruct((N, PAIRS, 2 * K), jnp.bfloat16),
            jax.ShapeDtypeStruct((N, RIM_ROWS, 2 * K), jnp.bfloat16),
            jax.ShapeDtypeStruct((N, RIM_ROWS, 2 * K), jnp.bfloat16),
            jax.ShapeDtypeStruct((2 * N, N, 2 * K), jnp.bfloat16),
        ],
        in_specs=[vmem()] * 3,
        out_specs=[vmem()] * 4,
        scratch_shapes=[
            pltpu.VMEM((N * PAIRS, 2 * K), jnp.float32),
            pltpu.VMEM((N * RIM_ROWS, 2 * K), jnp.float32),
            pltpu.VMEM((N * RIM_ROWS, 2 * K), jnp.float32),
        ],
        compiler_params=pltpu.CompilerParams(vmem_limit_bytes=20 << 20),
        cost_estimate=pl.CostEstimate(
            flops=300_000_000, bytes_accessed=3_000_000, transcendentals=0
        ),
    )(values, basis, links)


def down_kernel(
    low_ref,
    own_ref,
    high_ref,
    tops_ref,
    a_ref,
    coupling_ref,
    links_ref,
    basis_ref,
    near_ref,
    out_ref,
    cf_ref,
    call_ref,
    bd_ref,
    lhs_ref,
    fs_ref,
):
    classes = a_ref.shape[0]
    height = a_ref.shape[2] // 2
    subtrees = tops_ref.shape[0]
    lower = lax.broadcasted_iota(jnp.int32, (N, 2 * K), 1) < K

    used = PAIRS + 2 * RIM + subtrees
    for n in range(N):
        base = n * height
        cf_ref[base : base + PAIRS, :] = own_ref[n].astype(jnp.float32)
        at = base + PAIRS
        cf_ref[at : at + RIM, :] = low_ref[n].astype(jnp.float32)[:RIM]
        at += RIM
        cf_ref[at : at + RIM, :] = high_ref[n].astype(jnp.float32)[:RIM]
        if used < height:
            cf_ref[base + used : base + height, :] = jnp.zeros((height - used, 2 * K), jnp.float32)
    for q in range(subtrees // 2):
        even = tops_ref[2 * q, 0].astype(jnp.float32)
        odd = tops_ref[2 * q + 1, 0].astype(jnp.float32)
        at = PAIRS + 2 * RIM + 2 * q
        cf_ref[pl.ds(at, N, stride=height), :] = jnp.where(lower, even, even + odd)
        cf_ref[pl.ds(at + 1, N, stride=height), :] = odd
    wide_lower = lax.broadcasted_iota(jnp.int32, (height, 2 * K), 1) < K
    for m in range(N // 2):
        one = cf_ref[2 * m * height : (2 * m + 1) * height, :]
        two = cf_ref[(2 * m + 1) * height : (2 * m + 2) * height, :]
        lanes = slice(m * 2 * K, (m + 1) * 2 * K)
        call_ref[0:height, lanes] = jnp.where(
            wide_lower, one, pltpu.roll(two, K, 1)
        ).astype(jnp.bfloat16)
        call_ref[height : 2 * height, lanes] = jnp.where(
            wide_lower, pltpu.roll(one, K, 1), two
        ).astype(jnp.bfloat16)

    def spread(c, carry):
        s = coupling_ref[c]
        z = jnp.zeros((K, K), jnp.bfloat16)
        at = pl.multiple_of(c * 4 * K, 4 * K)
        for block in range(4):
            place = (0, 2, 1, 3)[block]
            bd_ref[pl.ds(at + block * K, K), :] = jnp.concatenate(
                [s if place == i else z for i in range(4)], axis=1
            )
        return carry

    lax.fori_loop(0, classes, spread, 0)

    for c in range(classes):
        grouped = dot(a_ref[c], call_ref[...]).astype(jnp.bfloat16)
        for m in range(N // 2):
            for parity in range(2):
                lhs_ref[
                    m * PAIRS : (m + 1) * PAIRS,
                    (2 * c + parity) * 2 * K : (2 * c + parity + 1) * 2 * K,
                ] = grouped[parity * PAIRS : (parity + 1) * PAIRS, m * 2 * K : (m + 1) * 2 * K]
    for m in range(N // 2):
        field = dot(lhs_ref[m * PAIRS : (m + 1) * PAIRS, :], bd_ref[...])
        fs_ref[2 * m * PAIRS : (2 * m + 1) * PAIRS, :] = field[:, 0 : 2 * K]
        fs_ref[(2 * m + 1) * PAIRS : (2 * m + 2) * PAIRS, :] = field[:, 2 * K : 4 * K]

    def field_of(pair_index):
        return fs_ref[pl.ds(pair_index, N, stride=PAIRS), :]

    def push(tile, matrix):
        none = jnp.zeros_like(tile)
        stacked = jnp.concatenate(
            [jnp.where(lower, tile, none), jnp.where(lower, none, tile)], axis=0
        ).astype(jnp.bfloat16)
        return dot(stacked, matrix)

    last = field_of(PAIRS - 1)
    top = last[:, K : 2 * K].astype(jnp.bfloat16)
    root = (last[:, 0:K] + dot(top, links_ref[PAIRS - 1][:, 0:K])).astype(jnp.bfloat16)
    tiles = {0: field_of(0) + dot(root, links_ref[0])}
    for j in range(B // 2 - 1):
        both = push(tiles[j], links_of(links_ref, j))
        tiles[2 * j + 1] = field_of(2 * j + 1) + both[:N]
        tiles[2 * j + 2] = field_of(2 * j + 2) + both[N:]
    for i in range(B // 2):
        both = push(tiles[B // 2 - 1 + i], basis_ref[i])
        for h in range(2):
            lanes = slice((2 * i + h) * M, (2 * i + h + 1) * M)
            out_ref[:, lanes] = (near_ref[:, lanes] + both[h * N : (h + 1) * N]).astype(jnp.bfloat16)


def downward(low, own, high, tops, counts, coupling, links, basis, near):
    classes = counts.shape[0]
    height = counts.shape[2] // 2
    return pl.pallas_call(
        down_kernel,
        name="downward",
        out_shape=jax.ShapeDtypeStruct((N, B * M), jnp.bfloat16),
        in_specs=[vmem()] * 9,
        out_specs=vmem(),
        scratch_shapes=[
            pltpu.VMEM((N * height, 2 * K), jnp.float32),
            pltpu.VMEM((2 * height, N * K), jnp.bfloat16),
            pltpu.VMEM((classes * 4 * K, 4 * K), jnp.bfloat16),
            pltpu.VMEM((N // 2 * PAIRS, classes * 4 * K), jnp.bfloat16),
            pltpu.VMEM((N * PAIRS, 2 * K), jnp.float32),
        ],
        compiler_params=pltpu.CompilerParams(vmem_limit_bytes=40 << 20),
        cost_estimate=pl.CostEstimate(
            flops=4_000_000_000, bytes_accessed=6_000_000, transcendentals=0
        ),
    )(low, own, high, tops, counts, coupling, links, basis, near)


def source_columns(far_src, top_src, position, subtrees, height):
    owner = far_src // TB
    slot = far_src % TB
    count = jnp.ones_like(slot)
    for bit in range(1, 7):
        count = jnp.where(slot + 1 >= 2**bit, 2**bit, count)
    first = (count - 2) // 2
    inside = (slot - (count - 1)) // 2
    pairs = count // 2
    width = jnp.minimum(pairs, 7)
    rim_first = jnp.where(count <= 16, first, jnp.where(count == 32, 14, 21))
    side = owner - position
    row = jnp.where(
        side == 0,
        first + inside,
        jnp.where(
            side < 0,
            PAIRS + rim_first + inside - (pairs - width),
            PAIRS + RIM + rim_first + inside,
        ),
    )
    column = jnp.where(far_src >= 0, row + ((slot - 1) % 2) * height, -1)
    base = PAIRS + 2 * RIM
    roots = lax.dynamic_slice_in_dim(top_src, position, 1, 0)
    tops = lax.dynamic_slice_in_dim(top_src, subtrees + position // 2, 1, 0)
    roots = jnp.where(roots >= 0, base + roots, -1)
    tops = jnp.where(tops >= 0, height + base + 2 * tops, -1)
    return by_parity(column, roots, tops)


def by_parity(rows, root, top):
    paired = rows[1:].reshape(PAIRS - 1, 2, rows.shape[1])
    return jnp.concatenate([paired[:, 0], root, paired[:, 1], top], axis=0)


def per_device(
    values, coords, basis, transfer, coupling, near_src, far_src, far_cls, top_src, top_cls
):
    position = lax.axis_index("leaf")
    subtrees = lax.axis_size("leaf")
    class_count = coupling.shape[0]
    height = -(-(PAIRS + 2 * RIM + subtrees) // 64) * 64

    whole_basis = lax.all_gather(basis, "vec", axis=0, tiled=True)

    box = jnp.arange(B, dtype=jnp.int32)
    centre = jnp.stack(
        [box % ROW, box // ROW, jnp.full((B,), 0, jnp.int32) + position]
    ).astype(jnp.float32) + 0.5
    flat = coords - jnp.repeat(centre, M, axis=1)
    coarse = rounded(flat)
    rest = rounded(flat - coarse)
    held = coarse + rest
    size = -5.0 * (held[0] ** 2 + held[1] ** 2 + held[2] ** 2)
    size_a = rounded(size)
    size_b = size - size_a
    rows = []
    for k in range(3):
        rows += [coarse[k], rest[k]]
    rows += [size_a, size_b]
    packed = jnp.concatenate([values, jnp.stack(rows).astype(jnp.bfloat16)], axis=0)
    links, coupling_t = relay(transfer, coupling)
    columns = source_columns(far_src, top_src, position, subtrees, height)
    classes = by_parity(
        far_cls,
        lax.dynamic_slice_in_dim(top_cls, position, 1, 0),
        lax.dynamic_slice_in_dim(top_cls, subtrees + position // 2, 1, 0),
    )
    counts = class_counts(columns, classes, class_count, 2 * height)

    forward = [(i, i + 1) for i in range(subtrees - 1)]
    backward = [(i + 1, i) for i in range(subtrees - 1)]
    from_low = lax.ppermute(packed, "leaf", forward)
    from_high = lax.ppermute(packed, "leaf", backward)
    basis_pairs = whole_basis.reshape(B // 2, 2 * K, M)
    coefs, first, last, root = upward(values, basis_pairs, links)
    tops = lax.all_gather(root, "leaf", axis=0)
    low = lax.ppermute(last, "leaf", forward)
    high = lax.ppermute(first, "leaf", backward)
    near_src, coefs = lax.optimization_barrier((near_src, coefs))
    near = near_field(near_src, from_low, packed, from_high)
    tops = lax.slice_in_dim(tops, 0, 1, axis=1)
    return downward(low, coefs, high, tops, counts, coupling_t, links, basis_pairs, near)


def solution(mesh):
    in_specs = (
        P("vec", "leaf"),
        P(None, "leaf"),
        P(("leaf", "vec"), None, None),
        P("leaf", None),
        P(),
        P("leaf", None),
        P("leaf", None),
        P("leaf", None),
        P(),
        P(),
    )
    out_specs = P("vec", "leaf")
    return jax.shard_map(
        per_device, mesh=mesh, in_specs=in_specs, out_specs=out_specs, check_vma=False
    )
```

```python
import math

import jax
import jax.numpy as jnp
import numpy as np
from jax import lax
from jax.experimental import pallas as pl
from jax.experimental.pallas import tpu as pltpu
from jax.sharding import PartitionSpec as P

M = 128
K = 64
REACH = 13
TB = 127
ROW = 16
N = 16
B = 64
PAIRS = 64
RIM = 28

SCALE = math.log2(math.e) / 0.2
AMPLITUDE = 0.3
VMEM_BYTES = 60 << 20

NN = (((1,), (0,)), ((), ()))
NT = (((1,), (1,)), ((), ()))
TN = (((0,), (0,)), ((), ()))


def dot(a, b, dims=NN):
    return lax.dot_general(a, b, dims, preferred_element_type=jnp.float32)


def vmem():
    return pl.BlockSpec(memory_space=pltpu.VMEM)


ONE = 12
POINT_ROWS = 16


def parts_of(x):
    out = []
    for _ in range(3):
        part = x.astype(jnp.bfloat16).astype(jnp.float32)
        out.append(part)
        x = x - part
    return out


def pack_kernel(centre_ref, values_ref, coords_ref, own_ref, up_ref, down_ref, target_ref):
    box = lax.broadcasted_iota(jnp.int32, (8, M), 0)
    for g in range(B // 8):
        planes = []
        for k in range(3):
            rows = [coords_ref[k : k + 1, (8 * g + i) * M : (8 * g + i + 1) * M] for i in range(8)]
            planes.append(jnp.concatenate(rows, axis=0) - centre_ref[k])
        ones = jnp.ones((8, M), jnp.float32)
        zeros = jnp.zeros((8, M), jnp.float32)

        def write(ref, base, shift, scale):
            moved = planes[:2] + [planes[2] + shift]
            size = -SCALE * (moved[0] * moved[0] + moved[1] * moved[1] + moved[2] * moved[2])
            rows = []
            for x in moved:
                rows += parts_of(scale * x)
            rows += parts_of(size) + [ones, zeros, zeros, zeros]
            for i in range(8):
                tile = jnp.concatenate([x[i : i + 1] for x in rows], axis=0)
                at = slice((8 * g + i) * M, (8 * g + i + 1) * M)
                ref[base : base + POINT_ROWS, at] = tile.astype(jnp.bfloat16)

        write(own_ref, N, 0.0, 1.0)
        write(up_ref, N, -1.0, 1.0)
        write(down_ref, N, 1.0, 1.0)
        write(target_ref, 0, 0.0, 2 * SCALE)
    for ref in (own_ref, up_ref, down_ref):
        ref[0:N, :] = values_ref[...]


def pack(centre, values, coords):
    wide = jax.ShapeDtypeStruct((N + POINT_ROWS, B * M), jnp.bfloat16)
    return pl.pallas_call(
        pack_kernel,
        name="pack",
        out_shape=[wide, wide, wide, jax.ShapeDtypeStruct((POINT_ROWS, B * M), jnp.bfloat16)],
        in_specs=[pl.BlockSpec(memory_space=pltpu.SMEM)] + [vmem()] * 2,
        out_specs=[vmem()] * 4,
        compiler_params=pltpu.CompilerParams(vmem_limit_bytes=VMEM_BYTES),
        cost_estimate=pl.CostEstimate(flops=1000, bytes_accessed=100_000, transcendentals=0),
    )(centre, values, coords)


def near_tables():
    lanes = []
    for k in range(3):
        for i, j in ((0, 0), (0, 1), (1, 0), (1, 1), (0, 2), (2, 0)):
            lanes.append((3 * k + i, 3 * k + j))
    for i in range(3):
        lanes += [(9 + i, ONE), (ONE, 9 + i)]
    source = np.zeros((3 * POINT_ROWS, 2 * M), np.float32)
    target = np.zeros((64, POINT_ROWS), np.float32)
    for lane, (y, x) in enumerate(lanes):
        target[lane, x] = 1
        for half, box in enumerate((0, 1, 1, 2)):
            source[POINT_ROWS * box + y, 64 * half + lane] = 1
    return [jnp.asarray(x, jnp.bfloat16) for x in (source, target)]


def near_kernel(
    near_ref, low_ref, own_ref, high_ref, xs_ref, source_ref, target_ref, out_ref, yp_ref, w_ref
):
    layers = (low_ref, own_ref, high_ref)

    def at(u):
        return pl.ds(pl.multiple_of(jnp.clip(u, 0, B - 1) * M, M), M)

    for l, src in enumerate(layers):

        def features(q, carry, l=l, src=src):
            u = 2 * q
            rows = jnp.concatenate([src[N:, at(u + i)] for i in (-1, 0, 1)], axis=0)
            both = dot(rows, source_ref[...], TN).astype(jnp.bfloat16)
            yp_ref[l, u] = both[:, 0:M]
            yp_ref[l, u + 1] = both[:, M : 2 * M]
            return carry

        lax.fori_loop(0, B // 2 + 1, features, 0, unroll=11)

    zero = jnp.zeros((64, M), jnp.bfloat16)

    def targets(q, carry):
        one, two = [
            dot(target_ref[...], xs_ref[:, at(2 * q + i)]).astype(jnp.bfloat16) for i in range(2)
        ]
        w_ref[q] = jnp.concatenate(
            [jnp.concatenate([one, zero], axis=1), jnp.concatenate([zero, two], axis=1)], axis=0
        )
        return carry

    lax.fori_loop(0, B // 2, targets, 0, unroll=8)

    none = jnp.zeros((N, M), jnp.bfloat16)
    rows = B // ROW
    for first, last, steps in ((0, 1, (1, 2)), (1, rows - 1, (0, 1, 2)), (rows - 1, rows, (0, 1))):

        def step(q, carry, first=first, steps=steps):
            t = first * ROW + 2 * q
            sources, vectors = [], []
            for c in range(3):
                for b in steps:
                    for a in range(3):
                        slot = 9 * c + 3 * b + a
                        u = t + (b - 1) * ROW + a - 1
                        sources.append(yp_ref[c, u + 1])
                        vectors.append(
                            jnp.concatenate(
                                [
                                    jnp.where(
                                        near_ref[t + i, slot] >= 0, layers[c][0:N, at(u + i)], none
                                    )
                                    for i in range(2)
                                ],
                                axis=0,
                            )
                        )
            e = dot(jnp.concatenate(sources, axis=0), w_ref[first * ROW // 2 + q])
            kernel = jnp.exp2(e).astype(jnp.bfloat16)
            total = dot(jnp.concatenate(vectors, axis=1), kernel)
            out_ref[:, at(t)] = AMPLITUDE * total[0:N, 0:M]
            out_ref[:, at(t + 1)] = AMPLITUDE * total[N : 2 * N, M : 2 * M]
            return carry

        lax.fori_loop(0, (last - first) * ROW // 2, step, 0)


def near_field(near_src, low, own, high, targets):
    return pl.pallas_call(
        near_kernel,
        name="near_field",
        out_shape=jax.ShapeDtypeStruct((N, B * M), jnp.float32),
        in_specs=[pl.BlockSpec(memory_space=pltpu.SMEM)] + [vmem()] * 6,
        out_specs=vmem(),
        scratch_shapes=[
            pltpu.VMEM((3, B + 2, M, M), jnp.bfloat16),
            pltpu.VMEM((B // 2, M, 2 * M), jnp.bfloat16),
        ],
        compiler_params=pltpu.CompilerParams(vmem_limit_bytes=VMEM_BYTES),
        cost_estimate=pl.CostEstimate(
            flops=20_000_000_000, bytes_accessed=5_000_000, transcendentals=28_000_000
        ),
    )(near_src, low, own, high, targets, *near_tables())


def relay_kernel(transfer_ref, coupling_ref, links_ref, coupling_t_ref, flat_ref, pair_ref):
    lower = lax.broadcasted_iota(jnp.int32, (K // 2, 2 * K), 1) < K

    def unpack(ref):
        for i in range(K // 2):
            flat_ref[pl.ds(i, ref.shape[0], stride=K // 2), :] = ref[
                :, 2 * K * i : 2 * K * (i + 1)
            ].astype(jnp.float32)

    def join(left, right):
        one = flat_ref[left * (K // 2) : (left + 1) * (K // 2), :]
        two = flat_ref[right * (K // 2) : (right + 1) * (K // 2), :]
        pair_ref[pl.ds(0, K // 2, stride=2), :] = jnp.where(lower, one, pltpu.roll(two, K, 1))
        pair_ref[pl.ds(1, K // 2, stride=2), :] = jnp.where(lower, pltpu.roll(one, K, 1), two)
        return pair_ref[...]

    unpack(transfer_ref)
    for p in range(PAIRS - 1):
        links_ref[p] = join(2 * p + 1, 2 * p + 2).astype(jnp.bfloat16)
    links_ref[PAIRS - 1] = join(0, 0).astype(jnp.bfloat16)
    unpack(coupling_ref)
    for p in range(coupling_ref.shape[0] // 2):
        both = jnp.transpose(join(2 * p, 2 * p + 1)).astype(jnp.bfloat16)
        coupling_t_ref[2 * p] = both[0:K]
        coupling_t_ref[2 * p + 1] = both[K : 2 * K]


def relay(transfer, coupling):
    return pl.pallas_call(
        relay_kernel,
        name="relay",
        out_shape=[
            jax.ShapeDtypeStruct((PAIRS, K, 2 * K), jnp.bfloat16),
            jax.ShapeDtypeStruct((coupling.shape[0], K, K), jnp.bfloat16),
        ],
        in_specs=[vmem()] * 2,
        out_specs=[vmem()] * 2,
        scratch_shapes=[
            pltpu.VMEM(((TB + 1) * K // 2, 2 * K), jnp.float32),
            pltpu.VMEM((K, 2 * K), jnp.float32),
        ],
        compiler_params=pltpu.CompilerParams(vmem_limit_bytes=VMEM_BYTES),
        cost_estimate=pl.CostEstimate(flops=1000, bytes_accessed=100_000, transcendentals=0),
    )(transfer, coupling)


def counts_kernel(col_ref, cls_ref, a_ref):
    classes = a_ref.shape[0]
    width = a_ref.shape[2]
    slots = col_ref.shape[1]
    spread = slots * 8
    lane = lax.broadcasted_iota(jnp.int32, (slots, spread), 1)
    copies = (lane // 8 == lax.broadcasted_iota(jnp.int32, (slots, spread), 0)).astype(jnp.float32)
    columns = lax.broadcasted_iota(jnp.int32, (8, width), 1)
    match = (
        lax.broadcasted_iota(jnp.int32, (8, spread), 1) % 8
        == lax.broadcasted_iota(jnp.int32, (8, spread), 0)
    )

    def block(g, carry):
        halves = []
        for h in range(2):
            rows = pl.ds(pl.multiple_of(g * 16 + h * 8, 8), 8)
            col = col_ref[rows, :]
            wide = dot(cls_ref[rows, :].astype(jnp.float32), copies).astype(jnp.int32)
            wide = jnp.where(match, wide, -1)
            left = jnp.concatenate(
                [jnp.where(wide == c, 1.0, 0.0) for c in range(classes)], axis=0
            ).astype(jnp.bfloat16)
            right = jnp.concatenate(
                [jnp.where(col[:, e : e + 1] == columns, 1.0, 0.0) for e in range(slots)], axis=0
            ).astype(jnp.bfloat16)
            halves.append(dot(left, right))
        for c in range(classes):
            both = jnp.concatenate([half[8 * c : 8 * c + 8] for half in halves], axis=0)
            a_ref[c, pl.ds(pl.multiple_of(g * 16, 16), 16), :] = both.astype(jnp.bfloat16)
        return carry

    lax.fori_loop(0, 2 * PAIRS // 16, block, 0)


def class_counts(columns, classes, class_count, width):
    return pl.pallas_call(
        counts_kernel,
        name="class_counts",
        out_shape=jax.ShapeDtypeStruct((class_count, 2 * PAIRS, width), jnp.bfloat16),
        in_specs=[vmem()] * 2,
        out_specs=vmem(),
        compiler_params=pltpu.CompilerParams(vmem_limit_bytes=VMEM_BYTES),
        cost_estimate=pl.CostEstimate(
            flops=1000, bytes_accessed=100_000, transcendentals=0
        ),
    )(columns, classes)


FIRST_ROWS = tuple(range(14)) + tuple(range(15, 22)) + tuple(range(31, 38))
LAST_ROWS = tuple(range(7)) + tuple(range(8, 15)) + tuple(range(24, 31)) + tuple(range(56, 63))
RIM_ROWS = 32


def links_of(links_ref, pair_index):
    return jnp.concatenate([links_ref[2 * pair_index + 1], links_ref[2 * pair_index + 2]], axis=0)


def up_kernel(
    values_ref, basis_ref, links_ref, out_ref, first_ref, last_ref, root_ref, cs_ref, fs_ref, ls_ref
):
    lower = lax.broadcasted_iota(jnp.int32, (N, 2 * K), 1) < K

    def keep(pair_index, tile):
        cs_ref[pl.ds(pair_index, N, stride=PAIRS), :] = tile
        for rows, ref in ((FIRST_ROWS, fs_ref), (LAST_ROWS, ls_ref)):
            if pair_index in rows:
                ref[pl.ds(rows.index(pair_index), N, stride=RIM_ROWS), :] = tile

    def lift(stacked, matrix):
        both = dot(stacked, matrix, NT)
        return jnp.where(lower, both[:N], both[N:]).astype(jnp.bfloat16)

    tiles = {}
    for i in range(B // 2):
        stacked = jnp.concatenate(
            [values_ref[:, 2 * i * M : (2 * i + 1) * M], values_ref[:, (2 * i + 1) * M : (2 * i + 2) * M]],
            axis=0,
        )
        tiles[B // 2 - 1 + i] = lift(stacked, basis_ref[i])
        keep(B // 2 - 1 + i, tiles[B // 2 - 1 + i].astype(jnp.float32))
    for j in reversed(range(B // 2 - 1)):
        stacked = jnp.concatenate([tiles[2 * j + 1], tiles[2 * j + 2]], axis=0)
        tiles[j] = lift(stacked, links_of(links_ref, j))
        keep(j, tiles[j].astype(jnp.float32))
    root = dot(tiles[0], links_ref[0], NT).astype(jnp.bfloat16)
    up = dot(root, links_ref[PAIRS - 1][:, 0:K], NT)
    last = jnp.concatenate([root.astype(jnp.float32), up], axis=1)
    keep(PAIRS - 1, last)
    root_ref[0] = last.astype(jnp.bfloat16)
    root_ref[1:] = jnp.zeros((2 * N - 1, N, 2 * K), jnp.bfloat16)
    for n in range(N):
        out_ref[n] = cs_ref[n * PAIRS : (n + 1) * PAIRS, :].astype(jnp.bfloat16)
        for source, target in ((fs_ref, first_ref), (ls_ref, last_ref)):
            base = n * RIM_ROWS
            source[base + RIM : base + RIM_ROWS, :] = jnp.zeros((RIM_ROWS - RIM, 2 * K), jnp.float32)
            target[n] = source[base : base + RIM_ROWS, :].astype(jnp.bfloat16)


def upward(values, basis, links):
    return pl.pallas_call(
        up_kernel,
        name="upward",
        out_shape=[
            jax.ShapeDtypeStruct((N, PAIRS, 2 * K), jnp.bfloat16),
            jax.ShapeDtypeStruct((N, RIM_ROWS, 2 * K), jnp.bfloat16),
            jax.ShapeDtypeStruct((N, RIM_ROWS, 2 * K), jnp.bfloat16),
            jax.ShapeDtypeStruct((2 * N, N, 2 * K), jnp.bfloat16),
        ],
        in_specs=[vmem()] * 3,
        out_specs=[vmem()] * 4,
        scratch_shapes=[
            pltpu.VMEM((N * PAIRS, 2 * K), jnp.float32),
            pltpu.VMEM((N * RIM_ROWS, 2 * K), jnp.float32),
            pltpu.VMEM((N * RIM_ROWS, 2 * K), jnp.float32),
        ],
        compiler_params=pltpu.CompilerParams(vmem_limit_bytes=VMEM_BYTES),
        cost_estimate=pl.CostEstimate(
            flops=300_000_000, bytes_accessed=3_000_000, transcendentals=0
        ),
    )(values, basis, links)


def down_kernel(
    low_ref,
    own_ref,
    high_ref,
    tops_ref,
    a_ref,
    coupling_ref,
    links_ref,
    basis_ref,
    near_ref,
    out_ref,
    cf_ref,
    call_ref,
    bd_ref,
    lhs_ref,
    fs_ref,
):
    classes = a_ref.shape[0]
    height = a_ref.shape[2] // 2
    subtrees = tops_ref.shape[0]
    lower = lax.broadcasted_iota(jnp.int32, (N, 2 * K), 1) < K

    used = PAIRS + 2 * RIM + subtrees
    for n in range(N):
        base = n * height
        cf_ref[base : base + PAIRS, :] = own_ref[n].astype(jnp.float32)
        at = base + PAIRS
        cf_ref[at : at + RIM, :] = low_ref[n].astype(jnp.float32)[:RIM]
        at += RIM
        cf_ref[at : at + RIM, :] = high_ref[n].astype(jnp.float32)[:RIM]
        if used < height:
            cf_ref[base + used : base + height, :] = jnp.zeros((height - used, 2 * K), jnp.float32)
    for q in range(subtrees // 2):
        even = tops_ref[2 * q, 0].astype(jnp.float32)
        odd = tops_ref[2 * q + 1, 0].astype(jnp.float32)
        at = PAIRS + 2 * RIM + 2 * q
        cf_ref[pl.ds(at, N, stride=height), :] = jnp.where(lower, even, even + odd)
        cf_ref[pl.ds(at + 1, N, stride=height), :] = odd
    wide_lower = lax.broadcasted_iota(jnp.int32, (height, 2 * K), 1) < K
    for m in range(N // 2):
        one = cf_ref[2 * m * height : (2 * m + 1) * height, :]
        two = cf_ref[(2 * m + 1) * height : (2 * m + 2) * height, :]
        lanes = slice(m * 2 * K, (m + 1) * 2 * K)
        call_ref[0:height, lanes] = jnp.where(
            wide_lower, one, pltpu.roll(two, K, 1)
        ).astype(jnp.bfloat16)
        call_ref[height : 2 * height, lanes] = jnp.where(
            wide_lower, pltpu.roll(one, K, 1), two
        ).astype(jnp.bfloat16)

    def spread(c, carry):
        s = coupling_ref[c]
        z = jnp.zeros((K, K), jnp.bfloat16)
        at = pl.multiple_of(c * 4 * K, 4 * K)
        for block in range(4):
            place = (0, 2, 1, 3)[block]
            bd_ref[pl.ds(at + block * K, K), :] = jnp.concatenate(
                [s if place == i else z for i in range(4)], axis=1
            )
        return carry

    lax.fori_loop(0, classes, spread, 0)

    for c in range(classes):
        grouped = dot(a_ref[c], call_ref[...]).astype(jnp.bfloat16)
        for m in range(N // 2):
            for parity in range(2):
                lhs_ref[
                    m * PAIRS : (m + 1) * PAIRS,
                    (2 * c + parity) * 2 * K : (2 * c + parity + 1) * 2 * K,
                ] = grouped[parity * PAIRS : (parity + 1) * PAIRS, m * 2 * K : (m + 1) * 2 * K]
    for m in range(N // 2):
        field = dot(lhs_ref[m * PAIRS : (m + 1) * PAIRS, :], bd_ref[...])
        fs_ref[2 * m * PAIRS : (2 * m + 1) * PAIRS, :] = field[:, 0 : 2 * K]
        fs_ref[(2 * m + 1) * PAIRS : (2 * m + 2) * PAIRS, :] = field[:, 2 * K : 4 * K]

    def field_of(pair_index):
        return fs_ref[pl.ds(pair_index, N, stride=PAIRS), :]

    def push(tile, matrix):
        none = jnp.zeros_like(tile)
        stacked = jnp.concatenate(
            [jnp.where(lower, tile, none), jnp.where(lower, none, tile)], axis=0
        ).astype(jnp.bfloat16)
        return dot(stacked, matrix)

    last = field_of(PAIRS - 1)
    top = last[:, K : 2 * K].astype(jnp.bfloat16)
    root = (last[:, 0:K] + dot(top, links_ref[PAIRS - 1][:, 0:K])).astype(jnp.bfloat16)
    tiles = {0: field_of(0) + dot(root, links_ref[0])}
    for j in range(B // 2 - 1):
        both = push(tiles[j], links_of(links_ref, j))
        tiles[2 * j + 1] = field_of(2 * j + 1) + both[:N]
        tiles[2 * j + 2] = field_of(2 * j + 2) + both[N:]
    for i in range(B // 2):
        both = push(tiles[B // 2 - 1 + i], basis_ref[i])
        for h in range(2):
            lanes = slice((2 * i + h) * M, (2 * i + h + 1) * M)
            out_ref[:, lanes] = (near_ref[:, lanes] + both[h * N : (h + 1) * N]).astype(jnp.bfloat16)


def downward(low, own, high, tops, counts, coupling, links, basis, near):
    classes = counts.shape[0]
    height = counts.shape[2] // 2
    return pl.pallas_call(
        down_kernel,
        name="downward",
        out_shape=jax.ShapeDtypeStruct((N, B * M), jnp.bfloat16),
        in_specs=[vmem()] * 9,
        out_specs=vmem(),
        scratch_shapes=[
            pltpu.VMEM((N * height, 2 * K), jnp.float32),
            pltpu.VMEM((2 * height, N * K), jnp.bfloat16),
            pltpu.VMEM((classes * 4 * K, 4 * K), jnp.bfloat16),
            pltpu.VMEM((N // 2 * PAIRS, classes * 4 * K), jnp.bfloat16),
            pltpu.VMEM((N * PAIRS, 2 * K), jnp.float32),
        ],
        compiler_params=pltpu.CompilerParams(vmem_limit_bytes=VMEM_BYTES),
        cost_estimate=pl.CostEstimate(
            flops=4_000_000_000, bytes_accessed=6_000_000, transcendentals=0
        ),
    )(low, own, high, tops, counts, coupling, links, basis, near)


def source_columns(far_src, top_src, position, subtrees, height):
    owner = far_src // TB
    slot = far_src % TB
    count = jnp.ones_like(slot)
    for bit in range(1, 7):
        count = jnp.where(slot + 1 >= 2**bit, 2**bit, count)
    first = (count - 2) // 2
    inside = (slot - (count - 1)) // 2
    pairs = count // 2
    width = jnp.minimum(pairs, 7)
    rim_first = jnp.where(count <= 16, first, jnp.where(count == 32, 14, 21))
    side = owner - position
    row = jnp.where(
        side == 0,
        first + inside,
        jnp.where(
            side < 0,
            PAIRS + rim_first + inside - (pairs - width),
            PAIRS + RIM + rim_first + inside,
        ),
    )
    column = jnp.where(far_src >= 0, row + ((slot - 1) % 2) * height, -1)
    base = PAIRS + 2 * RIM
    roots = lax.dynamic_slice_in_dim(top_src, position, 1, 0)
    tops = lax.dynamic_slice_in_dim(top_src, subtrees + position // 2, 1, 0)
    roots = jnp.where(roots >= 0, base + roots, -1)
    tops = jnp.where(tops >= 0, height + base + 2 * tops, -1)
    return by_parity(column, roots, tops)


def by_parity(rows, root, top):
    paired = rows[1:].reshape(PAIRS - 1, 2, rows.shape[1])
    return jnp.concatenate([paired[:, 0], root, paired[:, 1], top], axis=0)


def per_device(
    values, coords, basis, transfer, coupling, near_src, far_src, far_cls, top_src, top_cls
):
    position = lax.axis_index("leaf")
    subtrees = lax.axis_size("leaf")
    class_count = coupling.shape[0]
    height = -(-(PAIRS + 2 * RIM + subtrees) // 64) * 64

    whole_basis = lax.all_gather(basis, "vec", axis=0, tiled=True)

    middle = (ROW / 2, B // ROW / 2, position.astype(jnp.float32) + 0.5)
    centre = jnp.stack([jnp.asarray(x, jnp.float32) for x in middle])
    packed, for_high, for_low, targets = pack(centre, values, coords)

    links, coupling_t = relay(transfer, coupling)
    columns = source_columns(far_src, top_src, position, subtrees, height)
    classes = by_parity(
        far_cls,
        lax.dynamic_slice_in_dim(top_cls, position, 1, 0),
        lax.dynamic_slice_in_dim(top_cls, subtrees + position // 2, 1, 0),
    )
    counts = class_counts(columns, classes, class_count, 2 * height)

    forward = [(i, i + 1) for i in range(subtrees - 1)]
    backward = [(i + 1, i) for i in range(subtrees - 1)]
    for_high, for_low, counts, links = lax.optimization_barrier((for_high, for_low, counts, links))
    from_low = lax.ppermute(for_high, "leaf", forward)
    from_high = lax.ppermute(for_low, "leaf", backward)
    basis_pairs = whole_basis.reshape(B // 2, 2 * K, M)
    coefs, first, last, root = upward(values, basis_pairs, links)
    tops = lax.all_gather(root, "leaf", axis=0)
    low = lax.ppermute(last, "leaf", forward)
    high = lax.ppermute(first, "leaf", backward)
    near_src, coefs = lax.optimization_barrier((near_src, coefs))
    near = near_field(near_src, from_low, packed, from_high, targets)
    tops = lax.slice_in_dim(tops, 0, 1, axis=1)
    return downward(low, coefs, high, tops, counts, coupling_t, links, basis_pairs, near)


def solution(mesh):
    in_specs = (
        P("vec", "leaf"),
        P(None, "leaf"),
        P(("leaf", "vec"), None, None),
        P("leaf", None),
        P(),
        P("leaf", None),
        P("leaf", None),
        P("leaf", None),
        P(),
        P(),
    )
    out_specs = P("vec", "leaf")
    return jax.shard_map(
        per_device, mesh=mesh, in_specs=in_specs, out_specs=out_specs, check_vma=False
    )
```

```python
import functools
import math

import jax
import jax.numpy as jnp
import numpy as np
from jax import lax
from jax.experimental import pallas as pl
from jax.experimental.pallas import tpu as pltpu
from jax.sharding import PartitionSpec as P

M = 128
K = 64
REACH = 13
TB = 127
ROW = 16
N = 16
B = 64
PAIRS = 64
RIM = 28

SCALE = math.log2(math.e) / 0.2
AMPLITUDE = 0.3
VMEM_BYTES = 32 << 20
QUAD = 4
LANES = 32

NN = (((1,), (0,)), ((), ()))
NT = (((1,), (1,)), ((), ()))
TN = (((0,), (0,)), ((), ()))


def dot(a, b, dims=NN):
    return lax.dot_general(a, b, dims, preferred_element_type=jnp.float32)


def vmem():
    return pl.BlockSpec(memory_space=pltpu.VMEM)


ONE = 12
POINT_ROWS = 16


def parts_of(x):
    out = []
    for _ in range(3):
        part = x.astype(jnp.bfloat16).astype(jnp.float32)
        out.append(part)
        x = x - part
    return out


def pack_kernel(centre_ref, values_ref, coords_ref, own_ref, up_ref, down_ref, target_ref):
    box = lax.broadcasted_iota(jnp.int32, (8, M), 0)
    for g in range(B // 8):
        planes = []
        for k in range(3):
            rows = [coords_ref[k : k + 1, (8 * g + i) * M : (8 * g + i + 1) * M] for i in range(8)]
            planes.append(jnp.concatenate(rows, axis=0) - centre_ref[k])
        ones = jnp.ones((8, M), jnp.float32)
        zeros = jnp.zeros((8, M), jnp.float32)

        def write(ref, base, shift, scale):
            moved = planes[:2] + [planes[2] + shift]
            size = -SCALE * (moved[0] * moved[0] + moved[1] * moved[1] + moved[2] * moved[2])
            rows = []
            for x in moved:
                rows += parts_of(scale * x)
            rows += parts_of(size) + [ones, zeros, zeros, zeros]
            for i in range(8):
                tile = jnp.concatenate([x[i : i + 1] for x in rows], axis=0)
                at = slice((8 * g + i) * M, (8 * g + i + 1) * M)
                ref[base : base + POINT_ROWS, at] = tile.astype(jnp.bfloat16)

        write(own_ref, N, 0.0, 1.0)
        write(up_ref, N, -1.0, 1.0)
        write(down_ref, N, 1.0, 1.0)
        write(target_ref, 0, 0.0, 2 * SCALE)
    for ref in (own_ref, up_ref, down_ref):
        ref[0:N, :] = values_ref[...]


def pack(centre, values, coords):
    wide = jax.ShapeDtypeStruct((N + POINT_ROWS, B * M), jnp.bfloat16)
    return pl.pallas_call(
        pack_kernel,
        name="pack",
        out_shape=[wide, wide, wide, jax.ShapeDtypeStruct((POINT_ROWS, B * M), jnp.bfloat16)],
        in_specs=[pl.BlockSpec(memory_space=pltpu.SMEM)] + [vmem()] * 2,
        out_specs=[vmem()] * 4,
        compiler_params=pltpu.CompilerParams(vmem_limit_bytes=16 << 20),
        cost_estimate=pl.CostEstimate(flops=1000, bytes_accessed=100_000, transcendentals=0),
    )(centre, values, coords)


def near_tables():
    lanes = []
    for k in range(3):
        for i, j in ((0, 0), (0, 1), (1, 0), (1, 1), (0, 2), (2, 0)):
            lanes.append((3 * k + i, 3 * k + j))
    for i in range(3):
        lanes += [(9 + i, ONE), (ONE, 9 + i)]
    source = np.zeros(((QUAD + 2) * POINT_ROWS, 3 * M), np.float32)
    target = np.zeros((LANES, POINT_ROWS), np.float32)
    for lane, (y, x) in enumerate(lanes):
        target[lane, x] = 1
        for step in range(3):
            for i in range(QUAD):
                source[POINT_ROWS * (step + i) + y, M * step + LANES * i + lane] = 1
    return [jnp.asarray(x, jnp.bfloat16) for x in (source, target)]


def near_kernel(layer, near_ref, src_ref, xs_ref, source_ref, target_ref, *rest):
    before_ref = rest[0] if len(rest) == 4 else None
    out_ref, yq_ref, w_ref = rest[-3:]

    def at(u):
        return pl.ds(pl.multiple_of(jnp.clip(u, 0, B - 1) * M, M), M)

    def features(q, carry):
        t = QUAD * q
        rows = jnp.concatenate([src_ref[N:, at(t + i)] for i in range(-1, QUAD + 1)], axis=0)
        wide = dot(rows, source_ref[...], TN).astype(jnp.bfloat16)
        for step in range(3):
            yq_ref[q, step * M : (step + 1) * M, :] = wide[:, step * M : (step + 1) * M]
        tiles = [dot(target_ref[...], xs_ref[:, at(t + i)]).astype(jnp.bfloat16) for i in range(QUAD)]
        zero = jnp.zeros((LANES, M), jnp.bfloat16)
        for i in range(QUAD):
            w_ref[q, LANES * i : LANES * (i + 1), :] = jnp.concatenate(
                [tiles[i] if i == j else zero for j in range(QUAD)], axis=1
            )
        return carry

    lax.fori_loop(0, B // QUAD, features, 0, unroll=8)

    none = jnp.zeros((N, M), jnp.bfloat16)
    rows = B // ROW
    row_quads = ROW // QUAD

    def quad(q, steps):
        t = QUAD * q
        sources, vectors = [], []
        for b in steps:
            sources.append(yq_ref[q + (b - 1) * row_quads])
            for a in range(3):
                slot = 9 * layer + 3 * b + a
                u = t + (b - 1) * ROW + a - 1
                vectors.append(
                    jnp.concatenate(
                        [
                            jnp.where(near_ref[t + i, slot] >= 0, src_ref[0:N, at(u + i)], none)
                            for i in range(QUAD)
                        ],
                        axis=0,
                    )
                )
        e = dot(jnp.concatenate(sources, axis=0), w_ref[q])
        total = dot(jnp.concatenate(vectors, axis=1), jnp.exp2(e).astype(jnp.bfloat16))
        for i in range(QUAD):
            tile = AMPLITUDE * total[N * i : N * (i + 1), M * i : M * (i + 1)]
            if before_ref is not None:
                tile = before_ref[:, at(t + i)] + tile
            out_ref[:, at(t + i)] = tile

    for first, last, steps in ((0, 1, (1, 2)), (1, rows - 1, (0, 1, 2)), (rows - 1, rows, (0, 1))):

        def step(q, carry, first=first, steps=steps):
            for i in range(2):
                quad(first * row_quads + 2 * q + i, steps)
            return carry

        lax.fori_loop(0, (last - first) * row_quads // 2, step, 0)


def near_field(layer, near_src, src, targets, before=None):
    operands = [near_src, src, targets, *near_tables()] + ([] if before is None else [before])
    return pl.pallas_call(
        functools.partial(near_kernel, layer),
        name=("near_low", "near_own", "near_high")[layer],
        out_shape=jax.ShapeDtypeStruct((N, B * M), jnp.float32),
        in_specs=[pl.BlockSpec(memory_space=pltpu.SMEM)] + [vmem()] * (len(operands) - 1),
        out_specs=vmem(),
        scratch_shapes=[
            pltpu.VMEM((B // QUAD, 3 * M, M), jnp.bfloat16),
            pltpu.VMEM((B // QUAD, M, QUAD * M), jnp.bfloat16),
        ],
        compiler_params=pltpu.CompilerParams(vmem_limit_bytes=VMEM_BYTES),
        cost_estimate=pl.CostEstimate(
            flops=7_000_000_000, bytes_accessed=2_000_000, transcendentals=9_000_000
        ),
    )(*operands)


def relay_kernel(transfer_ref, coupling_ref, links_ref, coupling_t_ref, flat_ref, pair_ref):
    lower = lax.broadcasted_iota(jnp.int32, (K // 2, 2 * K), 1) < K

    def unpack(ref):
        for i in range(K // 2):
            flat_ref[pl.ds(i, ref.shape[0], stride=K // 2), :] = ref[
                :, 2 * K * i : 2 * K * (i + 1)
            ].astype(jnp.float32)

    def join(left, right):
        one = flat_ref[left * (K // 2) : (left + 1) * (K // 2), :]
        two = flat_ref[right * (K // 2) : (right + 1) * (K // 2), :]
        pair_ref[pl.ds(0, K // 2, stride=2), :] = jnp.where(lower, one, pltpu.roll(two, K, 1))
        pair_ref[pl.ds(1, K // 2, stride=2), :] = jnp.where(lower, pltpu.roll(one, K, 1), two)
        return pair_ref[...]

    unpack(transfer_ref)
    for p in range(PAIRS - 1):
        links_ref[p] = join(2 * p + 1, 2 * p + 2).astype(jnp.bfloat16)
    links_ref[PAIRS - 1] = join(0, 0).astype(jnp.bfloat16)
    unpack(coupling_ref)
    for p in range(coupling_ref.shape[0] // 2):
        both = jnp.transpose(join(2 * p, 2 * p + 1)).astype(jnp.bfloat16)
        coupling_t_ref[2 * p] = both[0:K]
        coupling_t_ref[2 * p + 1] = both[K : 2 * K]


def relay(transfer, coupling):
    return pl.pallas_call(
        relay_kernel,
        name="relay",
        out_shape=[
            jax.ShapeDtypeStruct((PAIRS, K, 2 * K), jnp.bfloat16),
            jax.ShapeDtypeStruct((coupling.shape[0], K, K), jnp.bfloat16),
        ],
        in_specs=[vmem()] * 2,
        out_specs=[vmem()] * 2,
        scratch_shapes=[
            pltpu.VMEM(((TB + 1) * K // 2, 2 * K), jnp.float32),
            pltpu.VMEM((K, 2 * K), jnp.float32),
        ],
        compiler_params=pltpu.CompilerParams(vmem_limit_bytes=16 << 20),
        cost_estimate=pl.CostEstimate(flops=1000, bytes_accessed=100_000, transcendentals=0),
    )(transfer, coupling)


def counts_kernel(col_ref, cls_ref, a_ref):
    classes = a_ref.shape[0]
    width = a_ref.shape[2]
    slots = col_ref.shape[1]
    spread = slots * 8
    lane = lax.broadcasted_iota(jnp.int32, (slots, spread), 1)
    copies = (lane // 8 == lax.broadcasted_iota(jnp.int32, (slots, spread), 0)).astype(jnp.float32)
    columns = lax.broadcasted_iota(jnp.int32, (8, width), 1)
    match = (
        lax.broadcasted_iota(jnp.int32, (8, spread), 1) % 8
        == lax.broadcasted_iota(jnp.int32, (8, spread), 0)
    )

    def block(g, carry):
        halves = []
        for h in range(2):
            rows = pl.ds(pl.multiple_of(g * 16 + h * 8, 8), 8)
            col = col_ref[rows, :]
            wide = dot(cls_ref[rows, :].astype(jnp.float32), copies).astype(jnp.int32)
            wide = jnp.where(match, wide, -1)
            left = jnp.concatenate(
                [jnp.where(wide == c, 1.0, 0.0) for c in range(classes)], axis=0
            ).astype(jnp.bfloat16)
            right = jnp.concatenate(
                [jnp.where(col[:, e : e + 1] == columns, 1.0, 0.0) for e in range(slots)], axis=0
            ).astype(jnp.bfloat16)
            halves.append(dot(left, right))
        for c in range(classes):
            both = jnp.concatenate([half[8 * c : 8 * c + 8] for half in halves], axis=0)
            a_ref[c, pl.ds(pl.multiple_of(g * 16, 16), 16), :] = both.astype(jnp.bfloat16)
        return carry

    lax.fori_loop(0, 2 * PAIRS // 16, block, 0)


def class_counts(columns, classes, class_count, width):
    return pl.pallas_call(
        counts_kernel,
        name="class_counts",
        out_shape=jax.ShapeDtypeStruct((class_count, 2 * PAIRS, width), jnp.bfloat16),
        in_specs=[vmem()] * 2,
        out_specs=vmem(),
        compiler_params=pltpu.CompilerParams(vmem_limit_bytes=20 << 20),
        cost_estimate=pl.CostEstimate(
            flops=1000, bytes_accessed=100_000, transcendentals=0
        ),
    )(columns, classes)


FIRST_ROWS = tuple(range(14)) + tuple(range(15, 22)) + tuple(range(31, 38))
LAST_ROWS = tuple(range(7)) + tuple(range(8, 15)) + tuple(range(24, 31)) + tuple(range(56, 63))
RIM_ROWS = 32


def links_of(links_ref, pair_index):
    return jnp.concatenate([links_ref[2 * pair_index + 1], links_ref[2 * pair_index + 2]], axis=0)


def up_kernel(
    values_ref, basis_ref, links_ref, out_ref, first_ref, last_ref, root_ref, cs_ref, fs_ref, ls_ref
):
    lower = lax.broadcasted_iota(jnp.int32, (N, 2 * K), 1) < K

    def keep(pair_index, tile):
        cs_ref[pl.ds(pair_index, N, stride=PAIRS), :] = tile
        for rows, ref in ((FIRST_ROWS, fs_ref), (LAST_ROWS, ls_ref)):
            if pair_index in rows:
                ref[pl.ds(rows.index(pair_index), N, stride=RIM_ROWS), :] = tile

    def lift(stacked, matrix):
        both = dot(stacked, matrix, NT)
        return jnp.where(lower, both[:N], both[N:]).astype(jnp.bfloat16)

    tiles = {}
    for i in range(B // 2):
        stacked = jnp.concatenate(
            [values_ref[:, 2 * i * M : (2 * i + 1) * M], values_ref[:, (2 * i + 1) * M : (2 * i + 2) * M]],
            axis=0,
        )
        tiles[B // 2 - 1 + i] = lift(stacked, basis_ref[i])
        keep(B // 2 - 1 + i, tiles[B // 2 - 1 + i].astype(jnp.float32))
    for j in reversed(range(B // 2 - 1)):
        stacked = jnp.concatenate([tiles[2 * j + 1], tiles[2 * j + 2]], axis=0)
        tiles[j] = lift(stacked, links_of(links_ref, j))
        keep(j, tiles[j].astype(jnp.float32))
    root = dot(tiles[0], links_ref[0], NT).astype(jnp.bfloat16)
    up = dot(root, links_ref[PAIRS - 1][:, 0:K], NT)
    last = jnp.concatenate([root.astype(jnp.float32), up], axis=1)
    keep(PAIRS - 1, last)
    root_ref[...] = last.astype(jnp.bfloat16)
    for ref in (first_ref, last_ref):
        ref[N, 0:N, :] = last.astype(jnp.bfloat16)
        ref[N, N:RIM_ROWS, :] = jnp.zeros((RIM_ROWS - N, 2 * K), jnp.bfloat16)
    for n in range(N):
        out_ref[n] = cs_ref[n * PAIRS : (n + 1) * PAIRS, :].astype(jnp.bfloat16)
        for source, target in ((fs_ref, first_ref), (ls_ref, last_ref)):
            base = n * RIM_ROWS
            source[base + RIM : base + RIM_ROWS, :] = jnp.zeros((RIM_ROWS - RIM, 2 * K), jnp.float32)
            target[n] = source[base : base + RIM_ROWS, :].astype(jnp.bfloat16)


def upward(values, basis, links):
    return pl.pallas_call(
        up_kernel,
        name="upward",
        out_shape=[
            jax.ShapeDtypeStruct((N, PAIRS, 2 * K), jnp.bfloat16),
            jax.ShapeDtypeStruct((N + 1, RIM_ROWS, 2 * K), jnp.bfloat16),
            jax.ShapeDtypeStruct((N + 1, RIM_ROWS, 2 * K), jnp.bfloat16),
            jax.ShapeDtypeStruct((N, 2 * K), jnp.bfloat16),
        ],
        in_specs=[vmem()] * 3,
        out_specs=[vmem()] * 4,
        scratch_shapes=[
            pltpu.VMEM((N * PAIRS, 2 * K), jnp.float32),
            pltpu.VMEM((N * RIM_ROWS, 2 * K), jnp.float32),
            pltpu.VMEM((N * RIM_ROWS, 2 * K), jnp.float32),
        ],
        compiler_params=pltpu.CompilerParams(vmem_limit_bytes=20 << 20),
        cost_estimate=pl.CostEstimate(
            flops=300_000_000, bytes_accessed=3_000_000, transcendentals=0
        ),
    )(values, basis, links)


def down_kernel(
    place_ref,
    low_ref,
    own_ref,
    high_ref,
    a_ref,
    coupling_ref,
    links_ref,
    basis_ref,
    near_ref,
    *rest,
):
    tops_refs, (out_ref, cf_ref, call_ref, bd_ref, lhs_ref, fs_ref) = rest[:-6], rest[-6:]
    classes = a_ref.shape[0]
    height = a_ref.shape[2] // 2
    subtrees = sum(ref.shape[0] for ref in tops_refs)
    lower = lax.broadcasted_iota(jnp.int32, (N, 2 * K), 1) < K

    used = PAIRS + 2 * RIM + subtrees
    for n in range(N):
        base = n * height
        cf_ref[base : base + PAIRS, :] = own_ref[n].astype(jnp.float32)
        at = base + PAIRS
        cf_ref[at : at + RIM, :] = low_ref[n].astype(jnp.float32)[:RIM]
        at += RIM
        cf_ref[at : at + RIM, :] = high_ref[n].astype(jnp.float32)[:RIM]
        if used < height:
            cf_ref[base + used : base + height, :] = jnp.zeros((height - used, 2 * K), jnp.float32)
    duos = [(ref, i) for ref in tops_refs for i in range(0, ref.shape[0], 2)]
    for m, (ref, i) in enumerate(duos):
        even = ref[i].astype(jnp.float32)
        odd = ref[i + 1].astype(jnp.float32)
        at = PAIRS + 2 * RIM + 2 * ((place_ref[0] // 2) ^ m)
        cf_ref[pl.ds(at, N, stride=height), :] = jnp.where(lower, even, even + odd)
        cf_ref[pl.ds(at + 1, N, stride=height), :] = odd
    wide_lower = lax.broadcasted_iota(jnp.int32, (height, 2 * K), 1) < K
    for m in range(N // 2):
        one = cf_ref[2 * m * height : (2 * m + 1) * height, :]
        two = cf_ref[(2 * m + 1) * height : (2 * m + 2) * height, :]
        lanes = slice(m * 2 * K, (m + 1) * 2 * K)
        call_ref[0:height, lanes] = jnp.where(
            wide_lower, one, pltpu.roll(two, K, 1)
        ).astype(jnp.bfloat16)
        call_ref[height : 2 * height, lanes] = jnp.where(
            wide_lower, pltpu.roll(one, K, 1), two
        ).astype(jnp.bfloat16)

    def spread(c, carry):
        s = coupling_ref[c]
        z = jnp.zeros((K, K), jnp.bfloat16)
        at = pl.multiple_of(c * 4 * K, 4 * K)
        for block in range(4):
            place = (0, 2, 1, 3)[block]
            bd_ref[pl.ds(at + block * K, K), :] = jnp.concatenate(
                [s if place == i else z for i in range(4)], axis=1
            )
        return carry

    lax.fori_loop(0, classes, spread, 0)

    for c in range(classes):
        grouped = dot(a_ref[c], call_ref[...]).astype(jnp.bfloat16)
        for m in range(N // 2):
            for parity in range(2):
                lhs_ref[
                    m * PAIRS : (m + 1) * PAIRS,
                    (2 * c + parity) * 2 * K : (2 * c + parity + 1) * 2 * K,
                ] = grouped[parity * PAIRS : (parity + 1) * PAIRS, m * 2 * K : (m + 1) * 2 * K]
    for m in range(N // 2):
        field = dot(lhs_ref[m * PAIRS : (m + 1) * PAIRS, :], bd_ref[...])
        fs_ref[2 * m * PAIRS : (2 * m + 1) * PAIRS, :] = field[:, 0 : 2 * K]
        fs_ref[(2 * m + 1) * PAIRS : (2 * m + 2) * PAIRS, :] = field[:, 2 * K : 4 * K]

    def field_of(pair_index):
        return fs_ref[pl.ds(pair_index, N, stride=PAIRS), :]

    def push(tile, matrix):
        none = jnp.zeros_like(tile)
        stacked = jnp.concatenate(
            [jnp.where(lower, tile, none), jnp.where(lower, none, tile)], axis=0
        ).astype(jnp.bfloat16)
        return dot(stacked, matrix)

    last = field_of(PAIRS - 1)
    top = last[:, K : 2 * K].astype(jnp.bfloat16)
    root = (last[:, 0:K] + dot(top, links_ref[PAIRS - 1][:, 0:K])).astype(jnp.bfloat16)
    tiles = {0: field_of(0) + dot(root, links_ref[0])}
    for j in range(B // 2 - 1):
        both = push(tiles[j], links_of(links_ref, j))
        tiles[2 * j + 1] = field_of(2 * j + 1) + both[:N]
        tiles[2 * j + 2] = field_of(2 * j + 2) + both[N:]
    for i in range(B // 2):
        both = push(tiles[B // 2 - 1 + i], basis_ref[i])
        for h in range(2):
            lanes = slice((2 * i + h) * M, (2 * i + h + 1) * M)
            out_ref[:, lanes] = (near_ref[:, lanes] + both[h * N : (h + 1) * N]).astype(jnp.bfloat16)


def downward(place, low, own, high, counts, coupling, links, basis, near, tops):
    classes = counts.shape[0]
    height = counts.shape[2] // 2
    return pl.pallas_call(
        down_kernel,
        name="downward",
        out_shape=jax.ShapeDtypeStruct((N, B * M), jnp.bfloat16),
        in_specs=[pl.BlockSpec(memory_space=pltpu.SMEM)] + [vmem()] * (8 + len(tops)),
        out_specs=vmem(),
        scratch_shapes=[
            pltpu.VMEM((N * height, 2 * K), jnp.float32),
            pltpu.VMEM((2 * height, N * K), jnp.bfloat16),
            pltpu.VMEM((classes * 4 * K, 4 * K), jnp.bfloat16),
            pltpu.VMEM((N // 2 * PAIRS, classes * 4 * K), jnp.bfloat16),
            pltpu.VMEM((N * PAIRS, 2 * K), jnp.float32),
        ],
        compiler_params=pltpu.CompilerParams(vmem_limit_bytes=40 << 20),
        cost_estimate=pl.CostEstimate(
            flops=4_000_000_000, bytes_accessed=6_000_000, transcendentals=0
        ),
    )(place, low, own, high, counts, coupling, links, basis, near, *tops)


def source_columns(far_src, top_src, position, subtrees, height):
    owner = far_src // TB
    slot = far_src % TB
    count = jnp.ones_like(slot)
    for bit in range(1, 7):
        count = jnp.where(slot + 1 >= 2**bit, 2**bit, count)
    first = (count - 2) // 2
    inside = (slot - (count - 1)) // 2
    pairs = count // 2
    width = jnp.minimum(pairs, 7)
    rim_first = jnp.where(count <= 16, first, jnp.where(count == 32, 14, 21))
    side = owner - position
    row = jnp.where(
        side == 0,
        first + inside,
        jnp.where(
            side < 0,
            PAIRS + rim_first + inside - (pairs - width),
            PAIRS + RIM + rim_first + inside,
        ),
    )
    column = jnp.where(far_src >= 0, row + ((slot - 1) % 2) * height, -1)
    base = PAIRS + 2 * RIM
    roots = lax.dynamic_slice_in_dim(top_src, position, 1, 0)
    tops = lax.dynamic_slice_in_dim(top_src, subtrees + position // 2, 1, 0)
    roots = jnp.where(roots >= 0, base + roots, -1)
    tops = jnp.where(tops >= 0, height + base + 2 * tops, -1)
    return by_parity(column, roots, tops)


def by_parity(rows, root, top):
    paired = rows[1:].reshape(PAIRS - 1, 2, rows.shape[1])
    return jnp.concatenate([paired[:, 0], root, paired[:, 1], top], axis=0)


def per_device(
    values, coords, basis, transfer, coupling, near_src, far_src, far_cls, top_src, top_cls
):
    position = lax.axis_index("leaf")
    subtrees = lax.axis_size("leaf")
    class_count = coupling.shape[0]
    height = -(-(PAIRS + 2 * RIM + subtrees) // 64) * 64

    whole_basis = lax.all_gather(basis, "vec", axis=0, tiled=True)

    middle = (ROW / 2, B // ROW / 2, position.astype(jnp.float32) + 0.5)
    centre = jnp.stack([jnp.asarray(x, jnp.float32) for x in middle])
    packed, for_high, for_low, targets = pack(centre, values, coords)

    links, coupling_t = relay(transfer, coupling)
    columns = source_columns(far_src, top_src, position, subtrees, height)
    classes = by_parity(
        far_cls,
        lax.dynamic_slice_in_dim(top_cls, position, 1, 0),
        lax.dynamic_slice_in_dim(top_cls, subtrees + position // 2, 1, 0),
    )
    forward = [(i, i + 1) for i in range(subtrees - 1)]
    backward = [(i + 1, i) for i in range(subtrees - 1)]
    for_high, for_low, columns = lax.optimization_barrier((for_high, for_low, columns))
    from_low = lax.ppermute(for_high, "leaf", forward)
    from_high = lax.ppermute(for_low, "leaf", backward)
    counts = class_counts(columns, classes, class_count, 2 * height)

    basis_pairs = whole_basis.reshape(B // 2, 2 * K, M)
    coefs, first, last, root = upward(values, basis_pairs, links)
    low = lax.ppermute(last, "leaf", forward)
    high = lax.ppermute(first, "leaf", backward)
    near_src, coefs = lax.optimization_barrier((near_src, coefs))
    near = near_field(1, near_src, packed, targets)

    is_even = position % 2 == 0
    other = jnp.where(is_even, high[N, :N], low[N, :N])
    duo = jnp.where(is_even, jnp.stack([root, other]), jnp.stack([other, root]))
    tops = [duo]
    layers = [(0, from_low), (2, from_high)]
    step = 2
    while step < subtrees:
        known = jnp.concatenate(tops, axis=0) if len(tops) > 1 else duo
        known, near = lax.optimization_barrier((known, near))
        tops.append(lax.ppermute(known, "leaf", [(i, i ^ step) for i in range(subtrees)]))
        if layers:
            layer, source = layers.pop(0)
            near = near_field(layer, near_src, source, targets, near)
        step *= 2
    for layer, source in layers:
        near = near_field(layer, near_src, source, targets, near)
    place = jnp.full((1,), 0, jnp.int32) + position
    return downward(
        place, low, coefs, high, counts, coupling_t, links, basis_pairs, near, tops
    )


def solution(mesh):
    in_specs = (
        P("vec", "leaf"),
        P(None, "leaf"),
        P(("leaf", "vec"), None, None),
        P("leaf", None),
        P(),
        P("leaf", None),
        P("leaf", None),
        P("leaf", None),
        P(),
        P(),
    )
    out_specs = P("vec", "leaf")
    return jax.shard_map(
        per_device, mesh=mesh, in_specs=in_specs, out_specs=out_specs, check_vma=False
    )
```

```python
import functools
import math

import jax
import jax.numpy as jnp
import numpy as np
from jax import lax
from jax.experimental import pallas as pl
from jax.experimental.pallas import tpu as pltpu
from jax.sharding import PartitionSpec as P

M = 128
K = 64
REACH = 13
TB = 127
ROW = 16
N = 16
B = 64
PAIRS = 64
RIM = 28

SCALE = math.log2(math.e) / 0.2
AMPLITUDE = 0.3
VMEM_BYTES = 32 << 20
QUAD = 4
LANES = 32

NN = (((1,), (0,)), ((), ()))
NT = (((1,), (1,)), ((), ()))
TN = (((0,), (0,)), ((), ()))


def dot(a, b, dims=NN):
    return lax.dot_general(a, b, dims, preferred_element_type=jnp.float32)


def vmem():
    return pl.BlockSpec(memory_space=pltpu.VMEM)


ONE = 12
POINT_ROWS = 16


def parts_of(x):
    out = []
    for _ in range(3):
        part = x.astype(jnp.bfloat16).astype(jnp.float32)
        out.append(part)
        x = x - part
    return out


def pack_kernel(centre_ref, values_ref, coords_ref, own_ref, up_ref, down_ref, target_ref):
    box = lax.broadcasted_iota(jnp.int32, (8, M), 0)
    for g in range(B // 8):
        planes = []
        for k in range(3):
            rows = [coords_ref[k : k + 1, (8 * g + i) * M : (8 * g + i + 1) * M] for i in range(8)]
            planes.append(jnp.concatenate(rows, axis=0) - centre_ref[k])
        ones = jnp.ones((8, M), jnp.float32)
        zeros = jnp.zeros((8, M), jnp.float32)

        def write(ref, base, shift, scale):
            moved = planes[:2] + [planes[2] + shift]
            size = -SCALE * (moved[0] * moved[0] + moved[1] * moved[1] + moved[2] * moved[2])
            rows = []
            for x in moved:
                rows += parts_of(scale * x)
            rows += parts_of(size) + [ones, zeros, zeros, zeros]
            for i in range(8):
                tile = jnp.concatenate([x[i : i + 1] for x in rows], axis=0)
                at = slice((8 * g + i) * M, (8 * g + i + 1) * M)
                ref[base : base + POINT_ROWS, at] = tile.astype(jnp.bfloat16)

        write(own_ref, N, 0.0, 1.0)
        write(up_ref, N, -1.0, 1.0)
        write(down_ref, N, 1.0, 1.0)
        write(target_ref, 0, 0.0, 2 * SCALE)
    for ref in (own_ref, up_ref, down_ref):
        ref[0:N, :] = values_ref[...]


def pack(centre, values, coords):
    wide = jax.ShapeDtypeStruct((N + POINT_ROWS, B * M), jnp.bfloat16)
    return pl.pallas_call(
        pack_kernel,
        name="pack",
        out_shape=[wide, wide, wide, jax.ShapeDtypeStruct((POINT_ROWS, B * M), jnp.bfloat16)],
        in_specs=[pl.BlockSpec(memory_space=pltpu.SMEM)] + [vmem()] * 2,
        out_specs=[vmem()] * 4,
        compiler_params=pltpu.CompilerParams(vmem_limit_bytes=16 << 20),
        cost_estimate=pl.CostEstimate(flops=1000, bytes_accessed=100_000, transcendentals=0),
    )(centre, values, coords)


def terms(lane):
    k = (lane >= 6).astype(jnp.int32) + (lane >= 12).astype(jnp.int32)
    r = lane - 6 * k
    i = jnp.where((r == 2) | (r == 3), 1, jnp.where(r == 5, 2, 0))
    j = jnp.where((r == 1) | (r == 3), 1, jnp.where(r == 4, 2, 0))
    size = 9 + ((lane - 18) >> 1)
    even = (lane & 1) == 0
    y = jnp.where(lane < 18, 3 * k + i, jnp.where(even, size, ONE))
    x = jnp.where(lane < 18, 3 * k + j, jnp.where(even, ONE, size))
    return jnp.where(lane < 24, y, -1000), jnp.where(lane < 24, x, -1000)


def near_tables():
    shape = ((QUAD + 2) * POINT_ROWS, 3 * M)
    row = lax.broadcasted_iota(jnp.int32, shape, 0)
    column = lax.broadcasted_iota(jnp.int32, shape, 1)
    box = (column >> 7) + ((column & (M - 1)) >> 5)
    y, _ = terms(column & (LANES - 1))
    source = jnp.where(row == POINT_ROWS * box + y, 1.0, 0.0).astype(jnp.bfloat16)
    shape = (LANES, POINT_ROWS)
    _, x = terms(lax.broadcasted_iota(jnp.int32, shape, 0))
    target = jnp.where(lax.broadcasted_iota(jnp.int32, shape, 1) == x, 1.0, 0.0)
    return source, target.astype(jnp.bfloat16)


def near_kernel(layer, near_ref, src_ref, xs_ref, *rest):
    before_ref = rest[0] if len(rest) == 4 else None
    out_ref, yq_ref, w_ref = rest[-3:]
    source, target = near_tables()

    def at(u):
        return pl.ds(pl.multiple_of(jnp.clip(u, 0, B - 1) * M, M), M)

    def features(q, carry):
        t = QUAD * q
        rows = jnp.concatenate([src_ref[N:, at(t + i)] for i in range(-1, QUAD + 1)], axis=0)
        wide = dot(rows, source, TN).astype(jnp.bfloat16)
        for step in range(3):
            yq_ref[q, step * M : (step + 1) * M, :] = wide[:, step * M : (step + 1) * M]
        tiles = [dot(target, xs_ref[:, at(t + i)]).astype(jnp.bfloat16) for i in range(QUAD)]
        zero = jnp.zeros((LANES, M), jnp.bfloat16)
        for i in range(QUAD):
            w_ref[q, LANES * i : LANES * (i + 1), :] = jnp.concatenate(
                [tiles[i] if i == j else zero for j in range(QUAD)], axis=1
            )
        return carry

    lax.fori_loop(0, B // QUAD, features, 0, unroll=8)

    none = jnp.zeros((N, M), jnp.bfloat16)
    rows = B // ROW
    row_quads = ROW // QUAD

    def quad(q, steps):
        t = QUAD * q
        sources, vectors = [], []
        for b in steps:
            sources.append(yq_ref[q + (b - 1) * row_quads])
            for a in range(3):
                slot = 9 * layer + 3 * b + a
                u = t + (b - 1) * ROW + a - 1
                vectors.append(
                    jnp.concatenate(
                        [
                            jnp.where(near_ref[t + i, slot] >= 0, src_ref[0:N, at(u + i)], none)
                            for i in range(QUAD)
                        ],
                        axis=0,
                    )
                )
        e = dot(jnp.concatenate(sources, axis=0), w_ref[q])
        total = dot(jnp.concatenate(vectors, axis=1), jnp.exp2(e).astype(jnp.bfloat16))
        for i in range(QUAD):
            tile = AMPLITUDE * total[N * i : N * (i + 1), M * i : M * (i + 1)]
            if before_ref is not None:
                tile = before_ref[:, at(t + i)] + tile
            out_ref[:, at(t + i)] = tile

    for first, last, steps in ((0, 1, (1, 2)), (1, rows - 1, (0, 1, 2)), (rows - 1, rows, (0, 1))):

        def step(q, carry, first=first, steps=steps):
            for i in range(2):
                quad(first * row_quads + 2 * q + i, steps)
            return carry

        lax.fori_loop(0, (last - first) * row_quads // 2, step, 0)


def near_field(layer, near_src, src, targets, before=None):
    operands = [near_src, src, targets] + ([] if before is None else [before])
    return pl.pallas_call(
        functools.partial(near_kernel, layer),
        name=("near_low", "near_own", "near_high")[layer],
        out_shape=jax.ShapeDtypeStruct((N, B * M), jnp.float32),
        in_specs=[pl.BlockSpec(memory_space=pltpu.SMEM)] + [vmem()] * (len(operands) - 1),
        out_specs=vmem(),
        scratch_shapes=[
            pltpu.VMEM((B // QUAD, 3 * M, M), jnp.bfloat16),
            pltpu.VMEM((B // QUAD, M, QUAD * M), jnp.bfloat16),
        ],
        compiler_params=pltpu.CompilerParams(vmem_limit_bytes=VMEM_BYTES),
        cost_estimate=pl.CostEstimate(
            flops=7_000_000_000, bytes_accessed=2_000_000, transcendentals=9_000_000
        ),
    )(*operands)


def relay_kernel(transfer_ref, coupling_ref, links_ref, coupling_t_ref, flat_ref, pair_ref):
    lower = lax.broadcasted_iota(jnp.int32, (K // 2, 2 * K), 1) < K

    def unpack(ref):
        for i in range(K // 2):
            flat_ref[pl.ds(i, ref.shape[0], stride=K // 2), :] = ref[
                :, 2 * K * i : 2 * K * (i + 1)
            ].astype(jnp.float32)

    def join(left, right):
        one = flat_ref[left * (K // 2) : (left + 1) * (K // 2), :]
        two = flat_ref[right * (K // 2) : (right + 1) * (K // 2), :]
        pair_ref[pl.ds(0, K // 2, stride=2), :] = jnp.where(lower, one, pltpu.roll(two, K, 1))
        pair_ref[pl.ds(1, K // 2, stride=2), :] = jnp.where(lower, pltpu.roll(one, K, 1), two)
        return pair_ref[...]

    unpack(transfer_ref)
    for p in range(PAIRS - 1):
        links_ref[p] = join(2 * p + 1, 2 * p + 2).astype(jnp.bfloat16)
    links_ref[PAIRS - 1] = join(0, 0).astype(jnp.bfloat16)
    unpack(coupling_ref)
    for p in range(coupling_ref.shape[0] // 2):
        both = jnp.transpose(join(2 * p, 2 * p + 1)).astype(jnp.bfloat16)
        coupling_t_ref[2 * p] = both[0:K]
        coupling_t_ref[2 * p + 1] = both[K : 2 * K]


def relay(transfer, coupling):
    return pl.pallas_call(
        relay_kernel,
        name="relay",
        out_shape=[
            jax.ShapeDtypeStruct((PAIRS, K, 2 * K), jnp.bfloat16),
            jax.ShapeDtypeStruct((coupling.shape[0], K, K), jnp.bfloat16),
        ],
        in_specs=[vmem()] * 2,
        out_specs=[vmem()] * 2,
        scratch_shapes=[
            pltpu.VMEM(((TB + 1) * K // 2, 2 * K), jnp.float32),
            pltpu.VMEM((K, 2 * K), jnp.float32),
        ],
        compiler_params=pltpu.CompilerParams(vmem_limit_bytes=16 << 20),
        cost_estimate=pl.CostEstimate(flops=1000, bytes_accessed=100_000, transcendentals=0),
    )(transfer, coupling)


def counts_kernel(
    place_ref, far_src_ref, far_cls_ref, top_src_ref, top_cls_ref, a_ref, col_ref, cls_ref
):
    classes = a_ref.shape[0]
    width = a_ref.shape[2]
    height = width // 2
    place = place_ref[0]
    subtrees = top_src_ref.shape[0] * 2 // 3

    def column(source):
        owner = jnp.floor((source.astype(jnp.float32) + 0.5) * (1.0 / TB)).astype(jnp.int32)
        slot = source - TB * owner
        count = jnp.ones_like(slot)
        for bit in range(1, 7):
            count = jnp.where(slot + 1 >= 2**bit, 2**bit, count)
        pairs = count >> 1
        first = pairs - 1
        inside = (slot - (count - 1)) >> 1
        rim_first = jnp.where(count <= 16, first, jnp.where(count == 32, 14, 21))
        side = owner - place
        low = PAIRS + rim_first + inside - (pairs - jnp.minimum(pairs, 7))
        row = jnp.where(
            side == 0, first + inside, jnp.where(side < 0, low, PAIRS + RIM + rim_first + inside)
        )
        return jnp.where(source >= 0, row + ((slot + 1) & 1) * height, -1)

    base = PAIRS + 2 * RIM
    last = PAIRS - 1
    for parity in range(2):
        rows = pl.ds(1 + parity, last, stride=2)
        col_ref[parity * PAIRS : parity * PAIRS + last, :] = column(far_src_ref[rows, :])
        cls_ref[parity * PAIRS : parity * PAIRS + last, :] = far_cls_ref[rows, :]
    root, top = pl.ds(place, 1), pl.ds(subtrees + (place >> 1), 1)
    roots, tops = top_src_ref[root, :], top_src_ref[top, :]
    col_ref[last : last + 1, :] = jnp.where(roots >= 0, base + roots, -1)
    col_ref[PAIRS + last : PAIRS + last + 1, :] = jnp.where(
        tops >= 0, height + base + 2 * tops, -1
    )
    cls_ref[last : last + 1, :] = top_cls_ref[root, :]
    cls_ref[PAIRS + last : PAIRS + last + 1, :] = top_cls_ref[top, :]

    slots = col_ref.shape[1]
    spread = slots * 8
    lane = lax.broadcasted_iota(jnp.int32, (slots, spread), 1)
    copies = (lane // 8 == lax.broadcasted_iota(jnp.int32, (slots, spread), 0)).astype(jnp.float32)
    columns = lax.broadcasted_iota(jnp.int32, (8, width), 1)
    match = (
        lax.broadcasted_iota(jnp.int32, (8, spread), 1) % 8
        == lax.broadcasted_iota(jnp.int32, (8, spread), 0)
    )

    def block(g, carry):
        halves = []
        for h in range(2):
            rows = pl.ds(pl.multiple_of(g * 16 + h * 8, 8), 8)
            col = col_ref[rows, :]
            wide = dot(cls_ref[rows, :].astype(jnp.float32), copies).astype(jnp.int32)
            wide = jnp.where(match, wide, -1)
            left = jnp.concatenate(
                [jnp.where(wide == c, 1.0, 0.0) for c in range(classes)], axis=0
            ).astype(jnp.bfloat16)
            right = jnp.concatenate(
                [jnp.where(col[:, e : e + 1] == columns, 1.0, 0.0) for e in range(slots)], axis=0
            ).astype(jnp.bfloat16)
            halves.append(dot(left, right))
        for c in range(classes):
            both = jnp.concatenate([half[8 * c : 8 * c + 8] for half in halves], axis=0)
            a_ref[c, pl.ds(pl.multiple_of(g * 16, 16), 16), :] = both.astype(jnp.bfloat16)
        return carry

    lax.fori_loop(0, 2 * PAIRS // 16, block, 0)


def class_counts(place, far_src, far_cls, top_src, top_cls, class_count, width):
    return pl.pallas_call(
        counts_kernel,
        name="class_counts",
        out_shape=jax.ShapeDtypeStruct((class_count, 2 * PAIRS, width), jnp.bfloat16),
        in_specs=[pl.BlockSpec(memory_space=pltpu.SMEM)] + [vmem()] * 4,
        out_specs=vmem(),
        scratch_shapes=[pltpu.VMEM((2 * PAIRS, far_src.shape[1]), jnp.int32)] * 2,
        compiler_params=pltpu.CompilerParams(vmem_limit_bytes=20 << 20),
        cost_estimate=pl.CostEstimate(flops=1000, bytes_accessed=100_000, transcendentals=0),
    )(place, far_src, far_cls, top_src, top_cls)


FIRST_ROWS = tuple(range(14)) + tuple(range(15, 22)) + tuple(range(31, 38))
LAST_ROWS = tuple(range(7)) + tuple(range(8, 15)) + tuple(range(24, 31)) + tuple(range(56, 63))
RIM_ROWS = 32


def links_of(links_ref, pair_index):
    return jnp.concatenate([links_ref[2 * pair_index + 1], links_ref[2 * pair_index + 2]], axis=0)


def up_kernel(
    values_ref, basis_ref, links_ref, out_ref, first_ref, last_ref, root_ref, cs_ref, fs_ref, ls_ref
):
    lower = lax.broadcasted_iota(jnp.int32, (N, 2 * K), 1) < K

    def keep(pair_index, tile):
        cs_ref[pl.ds(pair_index, N, stride=PAIRS), :] = tile
        for rows, ref in ((FIRST_ROWS, fs_ref), (LAST_ROWS, ls_ref)):
            if pair_index in rows:
                ref[pl.ds(rows.index(pair_index), N, stride=RIM_ROWS), :] = tile

    def lift(stacked, matrix):
        both = dot(stacked, matrix, NT)
        return jnp.where(lower, both[:N], both[N:]).astype(jnp.bfloat16)

    tiles = {}
    for i in range(B // 2):
        stacked = jnp.concatenate(
            [values_ref[:, 2 * i * M : (2 * i + 1) * M], values_ref[:, (2 * i + 1) * M : (2 * i + 2) * M]],
            axis=0,
        )
        tiles[B // 2 - 1 + i] = lift(stacked, basis_ref[i])
        keep(B // 2 - 1 + i, tiles[B // 2 - 1 + i].astype(jnp.float32))
    for j in reversed(range(B // 2 - 1)):
        stacked = jnp.concatenate([tiles[2 * j + 1], tiles[2 * j + 2]], axis=0)
        tiles[j] = lift(stacked, links_of(links_ref, j))
        keep(j, tiles[j].astype(jnp.float32))
    root = dot(tiles[0], links_ref[0], NT).astype(jnp.bfloat16)
    up = dot(root, links_ref[PAIRS - 1][:, 0:K], NT)
    last = jnp.concatenate([root.astype(jnp.float32), up], axis=1)
    keep(PAIRS - 1, last)
    root_ref[...] = last.astype(jnp.bfloat16)
    for ref in (first_ref, last_ref):
        ref[N, 0:N, :] = last.astype(jnp.bfloat16)
        ref[N, N:RIM_ROWS, :] = jnp.zeros((RIM_ROWS - N, 2 * K), jnp.bfloat16)
    for n in range(N):
        out_ref[n] = cs_ref[n * PAIRS : (n + 1) * PAIRS, :].astype(jnp.bfloat16)
        for source, target in ((fs_ref, first_ref), (ls_ref, last_ref)):
            base = n * RIM_ROWS
            source[base + RIM : base + RIM_ROWS, :] = jnp.zeros((RIM_ROWS - RIM, 2 * K), jnp.float32)
            target[n] = source[base : base + RIM_ROWS, :].astype(jnp.bfloat16)


def upward(values, basis, links):
    return pl.pallas_call(
        up_kernel,
        name="upward",
        out_shape=[
            jax.ShapeDtypeStruct((N, PAIRS, 2 * K), jnp.bfloat16),
            jax.ShapeDtypeStruct((N + 1, RIM_ROWS, 2 * K), jnp.bfloat16),
            jax.ShapeDtypeStruct((N + 1, RIM_ROWS, 2 * K), jnp.bfloat16),
            jax.ShapeDtypeStruct((N, 2 * K), jnp.bfloat16),
        ],
        in_specs=[vmem()] * 3,
        out_specs=[vmem()] * 4,
        scratch_shapes=[
            pltpu.VMEM((N * PAIRS, 2 * K), jnp.float32),
            pltpu.VMEM((N * RIM_ROWS, 2 * K), jnp.float32),
            pltpu.VMEM((N * RIM_ROWS, 2 * K), jnp.float32),
        ],
        compiler_params=pltpu.CompilerParams(vmem_limit_bytes=20 << 20),
        cost_estimate=pl.CostEstimate(
            flops=300_000_000, bytes_accessed=3_000_000, transcendentals=0
        ),
    )(values, basis, links)


def down_kernel(
    place_ref,
    low_ref,
    own_ref,
    high_ref,
    a_ref,
    coupling_ref,
    links_ref,
    basis_ref,
    near_ref,
    *rest,
):
    tops_refs, (out_ref, cf_ref, call_ref, bd_ref, lhs_ref, fs_ref) = rest[:-6], rest[-6:]
    classes = a_ref.shape[0]
    height = a_ref.shape[2] // 2
    subtrees = sum(ref.shape[0] for ref in tops_refs)
    lower = lax.broadcasted_iota(jnp.int32, (N, 2 * K), 1) < K

    used = PAIRS + 2 * RIM + subtrees
    for n in range(N):
        base = n * height
        cf_ref[base : base + PAIRS, :] = own_ref[n].astype(jnp.float32)
        at = base + PAIRS
        cf_ref[at : at + RIM, :] = low_ref[n].astype(jnp.float32)[:RIM]
        at += RIM
        cf_ref[at : at + RIM, :] = high_ref[n].astype(jnp.float32)[:RIM]
        if used < height:
            cf_ref[base + used : base + height, :] = jnp.zeros((height - used, 2 * K), jnp.float32)
    duos = [(ref, i) for ref in tops_refs for i in range(0, ref.shape[0], 2)]
    for m, (ref, i) in enumerate(duos):
        even = ref[i].astype(jnp.float32)
        odd = ref[i + 1].astype(jnp.float32)
        at = PAIRS + 2 * RIM + 2 * ((place_ref[0] // 2) ^ m)
        cf_ref[pl.ds(at, N, stride=height), :] = jnp.where(lower, even, even + odd)
        cf_ref[pl.ds(at + 1, N, stride=height), :] = odd
    wide_lower = lax.broadcasted_iota(jnp.int32, (height, 2 * K), 1) < K
    for m in range(N // 2):
        one = cf_ref[2 * m * height : (2 * m + 1) * height, :]
        two = cf_ref[(2 * m + 1) * height : (2 * m + 2) * height, :]
        lanes = slice(m * 2 * K, (m + 1) * 2 * K)
        call_ref[0:height, lanes] = jnp.where(
            wide_lower, one, pltpu.roll(two, K, 1)
        ).astype(jnp.bfloat16)
        call_ref[height : 2 * height, lanes] = jnp.where(
            wide_lower, pltpu.roll(one, K, 1), two
        ).astype(jnp.bfloat16)

    def spread(c, carry):
        s = coupling_ref[c]
        z = jnp.zeros((K, K), jnp.bfloat16)
        at = pl.multiple_of(c * 4 * K, 4 * K)
        for block in range(4):
            place = (0, 2, 1, 3)[block]
            bd_ref[pl.ds(at + block * K, K), :] = jnp.concatenate(
                [s if place == i else z for i in range(4)], axis=1
            )
        return carry

    lax.fori_loop(0, classes, spread, 0)

    counts = a_ref[...].reshape(classes * 2 * PAIRS, 2 * height)
    wide = N * K // 2
    for half in range(2):
        grouped = dot(counts, call_ref[:, half * wide : (half + 1) * wide]).astype(jnp.bfloat16)
        for c in range(classes):
            for parity in range(2):
                row = (2 * c + parity) * PAIRS
                for i in range(N // 4):
                    m = half * (N // 4) + i
                    lhs_ref[
                        m * PAIRS : (m + 1) * PAIRS, (2 * c + parity) * 2 * K : (2 * c + parity + 1) * 2 * K
                    ] = grouped[row : row + PAIRS, i * 2 * K : (i + 1) * 2 * K]
    field = dot(lhs_ref[...], bd_ref[...])
    for m in range(N // 2):
        rows = slice(m * PAIRS, (m + 1) * PAIRS)
        fs_ref[2 * m * PAIRS : (2 * m + 1) * PAIRS, :] = field[rows, 0 : 2 * K]
        fs_ref[(2 * m + 1) * PAIRS : (2 * m + 2) * PAIRS, :] = field[rows, 2 * K : 4 * K]

    def field_of(pair_index):
        return fs_ref[pl.ds(pair_index, N, stride=PAIRS), :]

    def push(tile, matrix):
        none = jnp.zeros_like(tile)
        stacked = jnp.concatenate(
            [jnp.where(lower, tile, none), jnp.where(lower, none, tile)], axis=0
        ).astype(jnp.bfloat16)
        return dot(stacked, matrix)

    last = field_of(PAIRS - 1)
    top = last[:, K : 2 * K].astype(jnp.bfloat16)
    root = (last[:, 0:K] + dot(top, links_ref[PAIRS - 1][:, 0:K])).astype(jnp.bfloat16)
    tiles = {0: field_of(0) + dot(root, links_ref[0])}
    for j in range(B // 2 - 1):
        both = push(tiles[j], links_of(links_ref, j))
        tiles[2 * j + 1] = field_of(2 * j + 1) + both[:N]
        tiles[2 * j + 2] = field_of(2 * j + 2) + both[N:]
    for i in range(B // 2):
        both = push(tiles[B // 2 - 1 + i], basis_ref[i])
        for h in range(2):
            lanes = slice((2 * i + h) * M, (2 * i + h + 1) * M)
            out_ref[:, lanes] = (near_ref[:, lanes] + both[h * N : (h + 1) * N]).astype(jnp.bfloat16)


def downward(place, low, own, high, counts, coupling, links, basis, near, tops):
    classes = counts.shape[0]
    height = counts.shape[2] // 2
    return pl.pallas_call(
        down_kernel,
        name="downward",
        out_shape=jax.ShapeDtypeStruct((N, B * M), jnp.bfloat16),
        in_specs=[pl.BlockSpec(memory_space=pltpu.SMEM)] + [vmem()] * (8 + len(tops)),
        out_specs=vmem(),
        scratch_shapes=[
            pltpu.VMEM((N * height, 2 * K), jnp.float32),
            pltpu.VMEM((2 * height, N * K), jnp.bfloat16),
            pltpu.VMEM((classes * 4 * K, 4 * K), jnp.bfloat16),
            pltpu.VMEM((N // 2 * PAIRS, classes * 4 * K), jnp.bfloat16),
            pltpu.VMEM((N * PAIRS, 2 * K), jnp.float32),
        ],
        compiler_params=pltpu.CompilerParams(vmem_limit_bytes=40 << 20),
        cost_estimate=pl.CostEstimate(
            flops=4_000_000_000, bytes_accessed=6_000_000, transcendentals=0
        ),
    )(place, low, own, high, counts, coupling, links, basis, near, *tops)


def per_device(
    values, coords, basis, transfer, coupling, near_src, far_src, far_cls, top_src, top_cls
):
    position = lax.axis_index("leaf")
    subtrees = lax.axis_size("leaf")
    class_count = coupling.shape[0]
    height = -(-(PAIRS + 2 * RIM + subtrees) // 64) * 64

    whole_basis = lax.all_gather(basis, "vec", axis=0, tiled=True)

    place = jnp.full((1,), 0, jnp.int32) + position
    middle = (ROW / 2, B // ROW / 2, position.astype(jnp.float32) + 0.5)
    centre = jnp.stack([jnp.asarray(x, jnp.float32) for x in middle])
    packed, for_high, for_low, targets = pack(centre, values, coords)

    links, coupling_t = relay(transfer, coupling)
    forward = [(i, i + 1) for i in range(subtrees - 1)]
    backward = [(i + 1, i) for i in range(subtrees - 1)]
    from_low = lax.ppermute(for_high, "leaf", forward)
    from_high = lax.ppermute(for_low, "leaf", backward)
    counts = class_counts(place, far_src, far_cls, top_src, top_cls, class_count, 2 * height)

    basis_pairs = whole_basis.reshape(B // 2, 2 * K, M)
    coefs, first, last, root = upward(values, basis_pairs, links)
    low = lax.ppermute(last, "leaf", forward)
    high = lax.ppermute(first, "leaf", backward)
    packed, coefs = lax.optimization_barrier((packed, coefs))
    near = near_field(1, near_src, packed, targets)

    is_even = position % 2 == 0
    other = jnp.where(is_even, high[N, :N], low[N, :N])
    duo = jnp.where(is_even, jnp.stack([root, other]), jnp.stack([other, root]))
    tops = [duo]
    layers = [(0, from_low), (2, from_high)]
    step = 2
    while step < subtrees:
        known = jnp.concatenate(tops, axis=0) if len(tops) > 1 else duo
        known, near = lax.optimization_barrier((known, near))
        tops.append(lax.ppermute(known, "leaf", [(i, i ^ step) for i in range(subtrees)]))
        if layers:
            layer, source = layers.pop(0)
            near = near_field(layer, near_src, source, targets, near)
        step *= 2
    for layer, source in layers:
        near = near_field(layer, near_src, source, targets, near)
    return downward(
        place, low, coefs, high, counts, coupling_t, links, basis_pairs, near, tops
    )


def solution(mesh):
    in_specs = (
        P("vec", "leaf"),
        P(None, "leaf"),
        P(("leaf", "vec"), None, None),
        P("leaf", None),
        P(),
        P("leaf", None),
        P("leaf", None),
        P("leaf", None),
        P(),
        P(),
    )
    out_specs = P("vec", "leaf")
    return jax.shard_map(
        per_device, mesh=mesh, in_specs=in_specs, out_specs=out_specs, check_vma=False
    )
```

```python
import functools
import math

import jax
import jax.numpy as jnp
import numpy as np
from jax import lax
from jax.experimental import pallas as pl
from jax.experimental.pallas import tpu as pltpu
from jax.sharding import PartitionSpec as P

M = 128
K = 64
REACH = 13
TB = 127
ROW = 16
N = 16
B = 64
PAIRS = 64
RIM = 28

SCALE = math.log2(math.e) / 0.2
AMPLITUDE = 0.3
VMEM_BYTES = 32 << 20
QUAD = 4
LANES = 32

NN = (((1,), (0,)), ((), ()))
NT = (((1,), (1,)), ((), ()))
TN = (((0,), (0,)), ((), ()))


def dot(a, b, dims=NN):
    return lax.dot_general(a, b, dims, preferred_element_type=jnp.float32)


def vmem():
    return pl.BlockSpec(memory_space=pltpu.VMEM)


ONE = 12
POINT_ROWS = 16


def parts_of(x):
    out = []
    for _ in range(3):
        part = x.astype(jnp.bfloat16).astype(jnp.float32)
        out.append(part)
        x = x - part
    return out


def pack_kernel(centre_ref, values_ref, coords_ref, own_ref, up_ref, down_ref, target_ref):
    box = lax.broadcasted_iota(jnp.int32, (8, M), 0)
    for g in range(B // 8):
        planes = []
        for k in range(3):
            rows = [coords_ref[k : k + 1, (8 * g + i) * M : (8 * g + i + 1) * M] for i in range(8)]
            planes.append(jnp.concatenate(rows, axis=0) - centre_ref[k])
        ones = jnp.ones((8, M), jnp.float32)
        zeros = jnp.zeros((8, M), jnp.float32)

        def write(ref, base, shift, scale):
            moved = planes[:2] + [planes[2] + shift]
            size = -SCALE * (moved[0] * moved[0] + moved[1] * moved[1] + moved[2] * moved[2])
            rows = []
            for x in moved:
                rows += parts_of(scale * x)
            rows += parts_of(size) + [ones, zeros, zeros, zeros]
            for i in range(8):
                tile = jnp.concatenate([x[i : i + 1] for x in rows], axis=0)
                at = slice((8 * g + i) * M, (8 * g + i + 1) * M)
                ref[base : base + POINT_ROWS, at] = tile.astype(jnp.bfloat16)

        write(own_ref, N, 0.0, 1.0)
        write(up_ref, N, -1.0, 1.0)
        write(down_ref, N, 1.0, 1.0)
        write(target_ref, 0, 0.0, 2 * SCALE)
    for ref in (own_ref, up_ref, down_ref):
        ref[0:N, :] = values_ref[...]


def pack(centre, values, coords):
    wide = jax.ShapeDtypeStruct((N + POINT_ROWS, B * M), jnp.bfloat16)
    return pl.pallas_call(
        pack_kernel,
        name="pack",
        out_shape=[wide, wide, wide, jax.ShapeDtypeStruct((POINT_ROWS, B * M), jnp.bfloat16)],
        in_specs=[pl.BlockSpec(memory_space=pltpu.SMEM)] + [vmem()] * 2,
        out_specs=[vmem()] * 4,
        compiler_params=pltpu.CompilerParams(vmem_limit_bytes=16 << 20),
        cost_estimate=pl.CostEstimate(flops=1000, bytes_accessed=100_000, transcendentals=0),
    )(centre, values, coords)


def terms(lane):
    k = (lane >= 6).astype(jnp.int32) + (lane >= 12).astype(jnp.int32)
    r = lane - 6 * k
    i = jnp.where((r == 2) | (r == 3), 1, jnp.where(r == 5, 2, 0))
    j = jnp.where((r == 1) | (r == 3), 1, jnp.where(r == 4, 2, 0))
    size = 9 + ((lane - 18) >> 1)
    even = (lane & 1) == 0
    y = jnp.where(lane < 18, 3 * k + i, jnp.where(even, size, ONE))
    x = jnp.where(lane < 18, 3 * k + j, jnp.where(even, ONE, size))
    return jnp.where(lane < 24, y, -1000), jnp.where(lane < 24, x, -1000)


def near_tables():
    shape = ((QUAD + 2) * POINT_ROWS, 3 * M)
    row = lax.broadcasted_iota(jnp.int32, shape, 0)
    column = lax.broadcasted_iota(jnp.int32, shape, 1)
    box = (column >> 7) + ((column & (M - 1)) >> 5)
    y, _ = terms(column & (LANES - 1))
    source = jnp.where(row == POINT_ROWS * box + y, 1.0, 0.0).astype(jnp.bfloat16)
    shape = (LANES, POINT_ROWS)
    _, x = terms(lax.broadcasted_iota(jnp.int32, shape, 0))
    target = jnp.where(lax.broadcasted_iota(jnp.int32, shape, 1) == x, 1.0, 0.0)
    return source, target.astype(jnp.bfloat16)


def near_kernel(layer, near_ref, src_ref, xs_ref, *rest):
    before_ref = rest[0] if len(rest) == 4 else None
    out_ref, yq_ref, w_ref = rest[-3:]
    source, target = near_tables()

    def at(u):
        return pl.ds(pl.multiple_of(jnp.clip(u, 0, B - 1) * M, M), M)

    def features(q, carry):
        t = QUAD * q
        rows = jnp.concatenate([src_ref[N:, at(t + i)] for i in range(-1, QUAD + 1)], axis=0)
        wide = dot(rows, source, TN).astype(jnp.bfloat16)
        for step in range(3):
            yq_ref[q, step * M : (step + 1) * M, :] = wide[:, step * M : (step + 1) * M]
        tiles = [dot(target, xs_ref[:, at(t + i)]).astype(jnp.bfloat16) for i in range(QUAD)]
        zero = jnp.zeros((LANES, M), jnp.bfloat16)
        for i in range(QUAD):
            w_ref[q, LANES * i : LANES * (i + 1), :] = jnp.concatenate(
                [tiles[i] if i == j else zero for j in range(QUAD)], axis=1
            )
        return carry

    lax.fori_loop(0, B // QUAD, features, 0, unroll=8)

    none = jnp.zeros((N, M), jnp.bfloat16)
    rows = B // ROW
    row_quads = ROW // QUAD

    def quad(q, steps):
        t = QUAD * q
        sources, vectors = [], []
        for b in steps:
            sources.append(yq_ref[q + (b - 1) * row_quads])
            for a in range(3):
                slot = 9 * layer + 3 * b + a
                u = t + (b - 1) * ROW + a - 1
                vectors.append(
                    jnp.concatenate(
                        [
                            jnp.where(near_ref[t + i, slot] >= 0, src_ref[0:N, at(u + i)], none)
                            for i in range(QUAD)
                        ],
                        axis=0,
                    )
                )
        e = dot(jnp.concatenate(sources, axis=0), w_ref[q])
        total = dot(jnp.concatenate(vectors, axis=1), jnp.exp2(e.astype(jnp.bfloat16)))
        for i in range(QUAD):
            tile = AMPLITUDE * total[N * i : N * (i + 1), M * i : M * (i + 1)]
            if before_ref is not None:
                tile = before_ref[:, at(t + i)] + tile
            out_ref[:, at(t + i)] = tile

    for first, last, steps in ((0, 1, (1, 2)), (1, rows - 1, (0, 1, 2)), (rows - 1, rows, (0, 1))):

        def step(q, carry, first=first, steps=steps):
            for i in range(2):
                quad(first * row_quads + 2 * q + i, steps)
            return carry

        lax.fori_loop(0, (last - first) * row_quads // 2, step, 0)


def near_field(layer, near_src, src, targets, before=None):
    operands = [near_src, src, targets] + ([] if before is None else [before])
    return pl.pallas_call(
        functools.partial(near_kernel, layer),
        name=("near_low", "near_own", "near_high")[layer],
        out_shape=jax.ShapeDtypeStruct((N, B * M), jnp.float32),
        in_specs=[pl.BlockSpec(memory_space=pltpu.SMEM)] + [vmem()] * (len(operands) - 1),
        out_specs=vmem(),
        scratch_shapes=[
            pltpu.VMEM((B // QUAD, 3 * M, M), jnp.bfloat16),
            pltpu.VMEM((B // QUAD, M, QUAD * M), jnp.bfloat16),
        ],
        compiler_params=pltpu.CompilerParams(vmem_limit_bytes=VMEM_BYTES),
        cost_estimate=pl.CostEstimate(
            flops=7_000_000_000, bytes_accessed=2_000_000, transcendentals=9_000_000
        ),
    )(*operands)


def relay_kernel(transfer_ref, coupling_ref, links_ref, coupling_t_ref, flat_ref, pair_ref):
    lower = lax.broadcasted_iota(jnp.int32, (K // 2, 2 * K), 1) < K

    def unpack(ref):
        for i in range(K // 2):
            flat_ref[pl.ds(i, ref.shape[0], stride=K // 2), :] = ref[
                :, 2 * K * i : 2 * K * (i + 1)
            ].astype(jnp.float32)

    def join(left, right):
        one = flat_ref[left * (K // 2) : (left + 1) * (K // 2), :]
        two = flat_ref[right * (K // 2) : (right + 1) * (K // 2), :]
        pair_ref[pl.ds(0, K // 2, stride=2), :] = jnp.where(lower, one, pltpu.roll(two, K, 1))
        pair_ref[pl.ds(1, K // 2, stride=2), :] = jnp.where(lower, pltpu.roll(one, K, 1), two)
        return pair_ref[...]

    unpack(transfer_ref)
    for p in range(PAIRS - 1):
        links_ref[p] = join(2 * p + 1, 2 * p + 2).astype(jnp.bfloat16)
    links_ref[PAIRS - 1] = join(0, 0).astype(jnp.bfloat16)
    unpack(coupling_ref)
    for p in range(coupling_ref.shape[0] // 2):
        both = jnp.transpose(join(2 * p, 2 * p + 1)).astype(jnp.bfloat16)
        coupling_t_ref[2 * p] = both[0:K]
        coupling_t_ref[2 * p + 1] = both[K : 2 * K]


def relay(transfer, coupling):
    return pl.pallas_call(
        relay_kernel,
        name="relay",
        out_shape=[
            jax.ShapeDtypeStruct((PAIRS, K, 2 * K), jnp.bfloat16),
            jax.ShapeDtypeStruct((coupling.shape[0], K, K), jnp.bfloat16),
        ],
        in_specs=[vmem()] * 2,
        out_specs=[vmem()] * 2,
        scratch_shapes=[
            pltpu.VMEM(((TB + 1) * K // 2, 2 * K), jnp.float32),
            pltpu.VMEM((K, 2 * K), jnp.float32),
        ],
        compiler_params=pltpu.CompilerParams(vmem_limit_bytes=16 << 20),
        cost_estimate=pl.CostEstimate(flops=1000, bytes_accessed=100_000, transcendentals=0),
    )(transfer, coupling)


def counts_kernel(
    place_ref, far_src_ref, far_cls_ref, top_src_ref, top_cls_ref, a_ref, col_ref, cls_ref
):
    classes = a_ref.shape[0]
    width = a_ref.shape[2]
    height = width // 2
    place = place_ref[0]
    subtrees = top_src_ref.shape[0] * 2 // 3

    def column(source):
        owner = jnp.floor((source.astype(jnp.float32) + 0.5) * (1.0 / TB)).astype(jnp.int32)
        slot = source - TB * owner
        count = jnp.ones_like(slot)
        for bit in range(1, 7):
            count = jnp.where(slot + 1 >= 2**bit, 2**bit, count)
        pairs = count >> 1
        first = pairs - 1
        inside = (slot - (count - 1)) >> 1
        rim_first = jnp.where(count <= 16, first, jnp.where(count == 32, 14, 21))
        side = owner - place
        low = PAIRS + rim_first + inside - (pairs - jnp.minimum(pairs, 7))
        row = jnp.where(
            side == 0, first + inside, jnp.where(side < 0, low, PAIRS + RIM + rim_first + inside)
        )
        return jnp.where(source >= 0, row + ((slot + 1) & 1) * height, -1)

    base = PAIRS + 2 * RIM
    last = PAIRS - 1
    for parity in range(2):
        rows = pl.ds(1 + parity, last, stride=2)
        col_ref[parity * PAIRS : parity * PAIRS + last, :] = column(far_src_ref[rows, :])
        cls_ref[parity * PAIRS : parity * PAIRS + last, :] = far_cls_ref[rows, :]
    root, top = pl.ds(place, 1), pl.ds(subtrees + (place >> 1), 1)
    roots, tops = top_src_ref[root, :], top_src_ref[top, :]
    col_ref[last : last + 1, :] = jnp.where(roots >= 0, base + roots, -1)
    col_ref[PAIRS + last : PAIRS + last + 1, :] = jnp.where(
        tops >= 0, height + base + 2 * tops, -1
    )
    cls_ref[last : last + 1, :] = top_cls_ref[root, :]
    cls_ref[PAIRS + last : PAIRS + last + 1, :] = top_cls_ref[top, :]

    slots = col_ref.shape[1]
    spread = slots * 8
    lane = lax.broadcasted_iota(jnp.int32, (slots, spread), 1)
    copies = (lane // 8 == lax.broadcasted_iota(jnp.int32, (slots, spread), 0)).astype(jnp.float32)
    columns = lax.broadcasted_iota(jnp.int32, (8, width), 1)
    match = (
        lax.broadcasted_iota(jnp.int32, (8, spread), 1) % 8
        == lax.broadcasted_iota(jnp.int32, (8, spread), 0)
    )

    def block(g, carry):
        halves = []
        for h in range(2):
            rows = pl.ds(pl.multiple_of(g * 16 + h * 8, 8), 8)
            col = col_ref[rows, :]
            wide = dot(cls_ref[rows, :].astype(jnp.float32), copies).astype(jnp.int32)
            wide = jnp.where(match, wide, -1)
            left = jnp.concatenate(
                [jnp.where(wide == c, 1.0, 0.0) for c in range(classes)], axis=0
            ).astype(jnp.bfloat16)
            right = jnp.concatenate(
                [jnp.where(col[:, e : e + 1] == columns, 1.0, 0.0) for e in range(slots)], axis=0
            ).astype(jnp.bfloat16)
            halves.append(dot(left, right))
        for c in range(classes):
            both = jnp.concatenate([half[8 * c : 8 * c + 8] for half in halves], axis=0)
            a_ref[c, pl.ds(pl.multiple_of(g * 16, 16), 16), :] = both.astype(jnp.bfloat16)
        return carry

    lax.fori_loop(0, 2 * PAIRS // 16, block, 0)


def class_counts(place, far_src, far_cls, top_src, top_cls, class_count, width):
    return pl.pallas_call(
        counts_kernel,
        name="class_counts",
        out_shape=jax.ShapeDtypeStruct((class_count, 2 * PAIRS, width), jnp.bfloat16),
        in_specs=[pl.BlockSpec(memory_space=pltpu.SMEM)] + [vmem()] * 4,
        out_specs=vmem(),
        scratch_shapes=[pltpu.VMEM((2 * PAIRS, far_src.shape[1]), jnp.int32)] * 2,
        compiler_params=pltpu.CompilerParams(vmem_limit_bytes=20 << 20),
        cost_estimate=pl.CostEstimate(flops=1000, bytes_accessed=100_000, transcendentals=0),
    )(place, far_src, far_cls, top_src, top_cls)


FIRST_ROWS = tuple(range(14)) + tuple(range(15, 22)) + tuple(range(31, 38))
LAST_ROWS = tuple(range(7)) + tuple(range(8, 15)) + tuple(range(24, 31)) + tuple(range(56, 63))
RIM_ROWS = 32


def links_of(links_ref, pair_index):
    return jnp.concatenate([links_ref[2 * pair_index + 1], links_ref[2 * pair_index + 2]], axis=0)


def up_kernel(
    values_ref, basis_ref, links_ref, out_ref, first_ref, last_ref, root_ref, cs_ref, fs_ref, ls_ref
):
    lower = lax.broadcasted_iota(jnp.int32, (N, 2 * K), 1) < K

    def keep(pair_index, tile):
        cs_ref[pl.ds(pair_index, N, stride=PAIRS), :] = tile
        for rows, ref in ((FIRST_ROWS, fs_ref), (LAST_ROWS, ls_ref)):
            if pair_index in rows:
                ref[pl.ds(rows.index(pair_index), N, stride=RIM_ROWS), :] = tile

    def lift(stacked, matrix):
        both = dot(stacked, matrix, NT)
        return jnp.where(lower, both[:N], both[N:]).astype(jnp.bfloat16)

    tiles = {}
    for i in range(B // 2):
        stacked = jnp.concatenate(
            [values_ref[:, 2 * i * M : (2 * i + 1) * M], values_ref[:, (2 * i + 1) * M : (2 * i + 2) * M]],
            axis=0,
        )
        tiles[B // 2 - 1 + i] = lift(stacked, basis_ref[i])
        keep(B // 2 - 1 + i, tiles[B // 2 - 1 + i].astype(jnp.float32))
    for j in reversed(range(B // 2 - 1)):
        stacked = jnp.concatenate([tiles[2 * j + 1], tiles[2 * j + 2]], axis=0)
        tiles[j] = lift(stacked, links_of(links_ref, j))
        keep(j, tiles[j].astype(jnp.float32))
    root = dot(tiles[0], links_ref[0], NT).astype(jnp.bfloat16)
    up = dot(root, links_ref[PAIRS - 1][:, 0:K], NT)
    last = jnp.concatenate([root.astype(jnp.float32), up], axis=1)
    keep(PAIRS - 1, last)
    root_ref[...] = last.astype(jnp.bfloat16)
    for ref in (first_ref, last_ref):
        ref[N, 0:N, :] = last.astype(jnp.bfloat16)
        ref[N, N:RIM_ROWS, :] = jnp.zeros((RIM_ROWS - N, 2 * K), jnp.bfloat16)
    for n in range(N):
        out_ref[n] = cs_ref[n * PAIRS : (n + 1) * PAIRS, :].astype(jnp.bfloat16)
        for source, target in ((fs_ref, first_ref), (ls_ref, last_ref)):
            base = n * RIM_ROWS
            source[base + RIM : base + RIM_ROWS, :] = jnp.zeros((RIM_ROWS - RIM, 2 * K), jnp.float32)
            target[n] = source[base : base + RIM_ROWS, :].astype(jnp.bfloat16)


def upward(values, basis, links):
    return pl.pallas_call(
        up_kernel,
        name="upward",
        out_shape=[
            jax.ShapeDtypeStruct((N, PAIRS, 2 * K), jnp.bfloat16),
            jax.ShapeDtypeStruct((N + 1, RIM_ROWS, 2 * K), jnp.bfloat16),
            jax.ShapeDtypeStruct((N + 1, RIM_ROWS, 2 * K), jnp.bfloat16),
            jax.ShapeDtypeStruct((N, 2 * K), jnp.bfloat16),
        ],
        in_specs=[vmem()] * 3,
        out_specs=[vmem()] * 4,
        scratch_shapes=[
            pltpu.VMEM((N * PAIRS, 2 * K), jnp.float32),
            pltpu.VMEM((N * RIM_ROWS, 2 * K), jnp.float32),
            pltpu.VMEM((N * RIM_ROWS, 2 * K), jnp.float32),
        ],
        compiler_params=pltpu.CompilerParams(vmem_limit_bytes=20 << 20),
        cost_estimate=pl.CostEstimate(
            flops=300_000_000, bytes_accessed=3_000_000, transcendentals=0
        ),
    )(values, basis, links)


def down_kernel(
    place_ref,
    low_ref,
    own_ref,
    high_ref,
    a_ref,
    coupling_ref,
    links_ref,
    basis_ref,
    near_ref,
    *rest,
):
    tops_refs, (out_ref, cf_ref, call_ref, bd_ref, lhs_ref, fs_ref) = rest[:-6], rest[-6:]
    classes = a_ref.shape[0]
    height = a_ref.shape[2] // 2
    subtrees = sum(ref.shape[0] for ref in tops_refs)
    lower = lax.broadcasted_iota(jnp.int32, (N, 2 * K), 1) < K

    used = PAIRS + 2 * RIM + subtrees
    for n in range(N):
        base = n * height
        cf_ref[base : base + PAIRS, :] = own_ref[n].astype(jnp.float32)
        at = base + PAIRS
        cf_ref[at : at + RIM, :] = low_ref[n].astype(jnp.float32)[:RIM]
        at += RIM
        cf_ref[at : at + RIM, :] = high_ref[n].astype(jnp.float32)[:RIM]
        if used < height:
            cf_ref[base + used : base + height, :] = jnp.zeros((height - used, 2 * K), jnp.float32)
    duos = [(ref, i) for ref in tops_refs for i in range(0, ref.shape[0], 2)]
    for m, (ref, i) in enumerate(duos):
        even = ref[i].astype(jnp.float32)
        odd = ref[i + 1].astype(jnp.float32)
        at = PAIRS + 2 * RIM + 2 * ((place_ref[0] // 2) ^ m)
        cf_ref[pl.ds(at, N, stride=height), :] = jnp.where(lower, even, even + odd)
        cf_ref[pl.ds(at + 1, N, stride=height), :] = odd
    wide_lower = lax.broadcasted_iota(jnp.int32, (height, 2 * K), 1) < K
    for m in range(N // 2):
        one = cf_ref[2 * m * height : (2 * m + 1) * height, :]
        two = cf_ref[(2 * m + 1) * height : (2 * m + 2) * height, :]
        lanes = slice(m * 2 * K, (m + 1) * 2 * K)
        call_ref[0:height, lanes] = jnp.where(
            wide_lower, one, pltpu.roll(two, K, 1)
        ).astype(jnp.bfloat16)
        call_ref[height : 2 * height, lanes] = jnp.where(
            wide_lower, pltpu.roll(one, K, 1), two
        ).astype(jnp.bfloat16)

    def spread(c, carry):
        s = coupling_ref[c]
        z = jnp.zeros((K, K), jnp.bfloat16)
        at = pl.multiple_of(c * 4 * K, 4 * K)
        for block in range(4):
            place = (0, 2, 1, 3)[block]
            bd_ref[pl.ds(at + block * K, K), :] = jnp.concatenate(
                [s if place == i else z for i in range(4)], axis=1
            )
        return carry

    lax.fori_loop(0, classes, spread, 0)

    counts = a_ref[...].reshape(classes * 2 * PAIRS, 2 * height)
    wide = N * K // 2
    for half in range(2):
        grouped = dot(counts, call_ref[:, half * wide : (half + 1) * wide]).astype(jnp.bfloat16)
        for c in range(classes):
            for parity in range(2):
                row = (2 * c + parity) * PAIRS
                for i in range(N // 4):
                    m = half * (N // 4) + i
                    lhs_ref[
                        m * PAIRS : (m + 1) * PAIRS, (2 * c + parity) * 2 * K : (2 * c + parity + 1) * 2 * K
                    ] = grouped[row : row + PAIRS, i * 2 * K : (i + 1) * 2 * K]
    field = dot(lhs_ref[...], bd_ref[...])
    for m in range(N // 2):
        rows = slice(m * PAIRS, (m + 1) * PAIRS)
        fs_ref[2 * m * PAIRS : (2 * m + 1) * PAIRS, :] = field[rows, 0 : 2 * K]
        fs_ref[(2 * m + 1) * PAIRS : (2 * m + 2) * PAIRS, :] = field[rows, 2 * K : 4 * K]

    def field_of(pair_index):
        return fs_ref[pl.ds(pair_index, N, stride=PAIRS), :]

    def push(tile, matrix):
        none = jnp.zeros_like(tile)
        stacked = jnp.concatenate(
            [jnp.where(lower, tile, none), jnp.where(lower, none, tile)], axis=0
        ).astype(jnp.bfloat16)
        return dot(stacked, matrix)

    last = field_of(PAIRS - 1)
    top = last[:, K : 2 * K].astype(jnp.bfloat16)
    root = (last[:, 0:K] + dot(top, links_ref[PAIRS - 1][:, 0:K])).astype(jnp.bfloat16)
    tiles = {0: field_of(0) + dot(root, links_ref[0])}
    for j in range(B // 2 - 1):
        both = push(tiles[j], links_of(links_ref, j))
        tiles[2 * j + 1] = field_of(2 * j + 1) + both[:N]
        tiles[2 * j + 2] = field_of(2 * j + 2) + both[N:]
    for i in range(B // 2):
        both = push(tiles[B // 2 - 1 + i], basis_ref[i])
        for h in range(2):
            lanes = slice((2 * i + h) * M, (2 * i + h + 1) * M)
            out_ref[:, lanes] = (near_ref[:, lanes] + both[h * N : (h + 1) * N]).astype(jnp.bfloat16)


def downward(place, low, own, high, counts, coupling, links, basis, near, tops):
    classes = counts.shape[0]
    height = counts.shape[2] // 2
    return pl.pallas_call(
        down_kernel,
        name="downward",
        out_shape=jax.ShapeDtypeStruct((N, B * M), jnp.bfloat16),
        in_specs=[pl.BlockSpec(memory_space=pltpu.SMEM)] + [vmem()] * (8 + len(tops)),
        out_specs=vmem(),
        scratch_shapes=[
            pltpu.VMEM((N * height, 2 * K), jnp.float32),
            pltpu.VMEM((2 * height, N * K), jnp.bfloat16),
            pltpu.VMEM((classes * 4 * K, 4 * K), jnp.bfloat16),
            pltpu.VMEM((N // 2 * PAIRS, classes * 4 * K), jnp.bfloat16),
            pltpu.VMEM((N * PAIRS, 2 * K), jnp.float32),
        ],
        compiler_params=pltpu.CompilerParams(vmem_limit_bytes=40 << 20),
        cost_estimate=pl.CostEstimate(
            flops=4_000_000_000, bytes_accessed=6_000_000, transcendentals=0
        ),
    )(place, low, own, high, counts, coupling, links, basis, near, *tops)


def per_device(
    values, coords, basis, transfer, coupling, near_src, far_src, far_cls, top_src, top_cls
):
    position = lax.axis_index("leaf")
    subtrees = lax.axis_size("leaf")
    class_count = coupling.shape[0]
    height = -(-(PAIRS + 2 * RIM + subtrees) // 64) * 64

    whole_basis = lax.all_gather(basis, "vec", axis=0, tiled=True)

    place = jnp.full((1,), 0, jnp.int32) + position
    middle = (ROW / 2, B // ROW / 2, position.astype(jnp.float32) + 0.5)
    centre = jnp.stack([jnp.asarray(x, jnp.float32) for x in middle])
    packed, for_high, for_low, targets = pack(centre, values, coords)

    links, coupling_t = relay(transfer, coupling)
    forward = [(i, i + 1) for i in range(subtrees - 1)]
    backward = [(i + 1, i) for i in range(subtrees - 1)]
    from_low = lax.ppermute(for_high, "leaf", forward)
    from_high = lax.ppermute(for_low, "leaf", backward)
    counts = class_counts(place, far_src, far_cls, top_src, top_cls, class_count, 2 * height)

    basis_pairs = whole_basis.reshape(B // 2, 2 * K, M)
    coefs, first, last, root = upward(values, basis_pairs, links)
    low = lax.ppermute(last, "leaf", forward)
    high = lax.ppermute(first, "leaf", backward)
    packed, coefs = lax.optimization_barrier((packed, coefs))
    near = near_field(1, near_src, packed, targets)

    is_even = position % 2 == 0
    other = jnp.where(is_even, high[N, :N], low[N, :N])
    duo = jnp.where(is_even, jnp.stack([root, other]), jnp.stack([other, root]))
    tops = [duo]
    layers = [(0, from_low), (2, from_high)]
    step = 2
    while step < subtrees:
        known = jnp.concatenate(tops, axis=0) if len(tops) > 1 else duo
        known, near = lax.optimization_barrier((known, near))
        tops.append(lax.ppermute(known, "leaf", [(i, i ^ step) for i in range(subtrees)]))
        if layers:
            layer, source = layers.pop(0)
            near = near_field(layer, near_src, source, targets, near)
        step *= 2
    for layer, source in layers:
        near = near_field(layer, near_src, source, targets, near)
    return downward(
        place, low, coefs, high, counts, coupling_t, links, basis_pairs, near, tops
    )


def solution(mesh):
    in_specs = (
        P("vec", "leaf"),
        P(None, "leaf"),
        P(("leaf", "vec"), None, None),
        P("leaf", None),
        P(),
        P("leaf", None),
        P("leaf", None),
        P("leaf", None),
        P(),
        P(),
    )
    out_specs = P("vec", "leaf")
    return jax.shard_map(
        per_device, mesh=mesh, in_specs=in_specs, out_specs=out_specs, check_vma=False
    )
```

```python
import functools
import math

import jax
import jax.numpy as jnp
import numpy as np
from jax import lax
from jax.experimental import pallas as pl
from jax.experimental.pallas import tpu as pltpu
from jax.sharding import PartitionSpec as P

M = 128
K = 64
REACH = 13
TB = 127
ROW = 16
N = 16
B = 64
PAIRS = 64
RIM = 28

SCALE = math.log2(math.e) / 0.2
AMPLITUDE = 0.3
VMEM_BYTES = 32 << 20
QUAD = 4
LANES = 32

NN = (((1,), (0,)), ((), ()))
NT = (((1,), (1,)), ((), ()))
TN = (((0,), (0,)), ((), ()))


def dot(a, b, dims=NN):
    return lax.dot_general(a, b, dims, preferred_element_type=jnp.float32)


def vmem():
    return pl.BlockSpec(memory_space=pltpu.VMEM)


ONE = 12
POINT_ROWS = 16


def parts_of(x):
    out = []
    for _ in range(3):
        part = x.astype(jnp.bfloat16).astype(jnp.float32)
        out.append(part)
        x = x - part
    return out


def pack_kernel(centre_ref, values_ref, coords_ref, own_ref, up_ref, down_ref, target_ref):
    box = lax.broadcasted_iota(jnp.int32, (8, M), 0)
    for g in range(B // 8):
        planes = []
        for k in range(3):
            rows = [coords_ref[k : k + 1, (8 * g + i) * M : (8 * g + i + 1) * M] for i in range(8)]
            planes.append(jnp.concatenate(rows, axis=0) - centre_ref[k])
        ones = jnp.ones((8, M), jnp.float32)
        zeros = jnp.zeros((8, M), jnp.float32)

        def write(ref, base, shift, scale):
            moved = planes[:2] + [planes[2] + shift]
            size = -SCALE * (moved[0] * moved[0] + moved[1] * moved[1] + moved[2] * moved[2])
            rows = []
            for x in moved:
                rows += parts_of(scale * x)
            rows += parts_of(size) + [ones, zeros, zeros, zeros]
            for i in range(8):
                tile = jnp.concatenate([x[i : i + 1] for x in rows], axis=0)
                at = slice((8 * g + i) * M, (8 * g + i + 1) * M)
                ref[base : base + POINT_ROWS, at] = tile.astype(jnp.bfloat16)

        write(own_ref, N, 0.0, 1.0)
        write(up_ref, N, -1.0, 1.0)
        write(down_ref, N, 1.0, 1.0)
        write(target_ref, 0, 0.0, 2 * SCALE)
    for ref in (own_ref, up_ref, down_ref):
        ref[0:N, :] = values_ref[...]


def pack(centre, values, coords):
    wide = jax.ShapeDtypeStruct((N + POINT_ROWS, B * M), jnp.bfloat16)
    return pl.pallas_call(
        pack_kernel,
        name="pack",
        out_shape=[wide, wide, wide, jax.ShapeDtypeStruct((POINT_ROWS, B * M), jnp.bfloat16)],
        in_specs=[pl.BlockSpec(memory_space=pltpu.SMEM)] + [vmem()] * 2,
        out_specs=[vmem()] * 4,
        compiler_params=pltpu.CompilerParams(vmem_limit_bytes=16 << 20),
        cost_estimate=pl.CostEstimate(flops=1000, bytes_accessed=100_000, transcendentals=0),
    )(centre, values, coords)


def terms(lane):
    k = (lane >= 6).astype(jnp.int32) + (lane >= 12).astype(jnp.int32)
    r = lane - 6 * k
    i = jnp.where((r == 2) | (r == 3), 1, jnp.where(r == 5, 2, 0))
    j = jnp.where((r == 1) | (r == 3), 1, jnp.where(r == 4, 2, 0))
    size = 9 + ((lane - 18) >> 1)
    even = (lane & 1) == 0
    y = jnp.where(lane < 18, 3 * k + i, jnp.where(even, size, ONE))
    x = jnp.where(lane < 18, 3 * k + j, jnp.where(even, ONE, size))
    return jnp.where(lane < 24, y, -1000), jnp.where(lane < 24, x, -1000)


def near_tables():
    shape = ((QUAD + 2) * POINT_ROWS, 3 * M)
    row = lax.broadcasted_iota(jnp.int32, shape, 0)
    column = lax.broadcasted_iota(jnp.int32, shape, 1)
    box = (column >> 7) + ((column & (M - 1)) >> 5)
    y, _ = terms(column & (LANES - 1))
    source = jnp.where(row == POINT_ROWS * box + y, 1.0, 0.0).astype(jnp.bfloat16)
    shape = (LANES, POINT_ROWS)
    _, x = terms(lax.broadcasted_iota(jnp.int32, shape, 0))
    target = jnp.where(lax.broadcasted_iota(jnp.int32, shape, 1) == x, 1.0, 0.0)
    return source, target.astype(jnp.bfloat16)


def near_kernel(layer, near_ref, src_ref, xs_ref, *rest):
    before_ref = rest[0] if len(rest) == 4 else None
    out_ref, yq_ref, w_ref = rest[-3:]
    source, target = near_tables()

    def at(u):
        return pl.ds(pl.multiple_of(jnp.clip(u, 0, B - 1) * M, M), M)

    def features(q, carry):
        t = QUAD * q
        rows = jnp.concatenate([src_ref[N:, at(t + i)] for i in range(-1, QUAD + 1)], axis=0)
        wide = dot(rows, source, TN).astype(jnp.bfloat16)
        for step in range(3):
            yq_ref[q, step * M : (step + 1) * M, :] = wide[:, step * M : (step + 1) * M]
        tiles = [dot(target, xs_ref[:, at(t + i)]).astype(jnp.bfloat16) for i in range(QUAD)]
        zero = jnp.zeros((LANES, M), jnp.bfloat16)
        for i in range(QUAD):
            w_ref[q, LANES * i : LANES * (i + 1), :] = jnp.concatenate(
                [tiles[i] if i == j else zero for j in range(QUAD)], axis=1
            )
        return carry

    lax.fori_loop(0, B // QUAD, features, 0, unroll=8)

    none = jnp.zeros((N, M), jnp.bfloat16)
    rows = B // ROW
    row_quads = ROW // QUAD

    def quad(q, steps):
        t = QUAD * q
        sources, vectors = [], []
        for b in steps:
            sources.append(yq_ref[q + (b - 1) * row_quads])
            for a in range(3):
                slot = 9 * layer + 3 * b + a
                u = t + (b - 1) * ROW + a - 1
                vectors.append(
                    jnp.concatenate(
                        [
                            jnp.where(near_ref[t + i, slot] >= 0, src_ref[0:N, at(u + i)], none)
                            for i in range(QUAD)
                        ],
                        axis=0,
                    )
                )
        e = dot(jnp.concatenate(sources, axis=0), w_ref[q])
        total = dot(jnp.concatenate(vectors, axis=1), jnp.exp2(e).astype(jnp.bfloat16))
        for i in range(QUAD):
            tile = AMPLITUDE * total[N * i : N * (i + 1), M * i : M * (i + 1)]
            if before_ref is not None:
                tile = before_ref[:, at(t + i)] + tile
            out_ref[:, at(t + i)] = tile

    for first, last, steps in ((0, 1, (1, 2)), (1, rows - 1, (0, 1, 2)), (rows - 1, rows, (0, 1))):

        def step(q, carry, first=first, steps=steps):
            for i in range(2):
                quad(first * row_quads + 2 * q + i, steps)
            return carry

        lax.fori_loop(0, (last - first) * row_quads // 2, step, 0)


def near_field(layer, near_src, src, targets, before=None):
    operands = [near_src, src, targets] + ([] if before is None else [before])
    return pl.pallas_call(
        functools.partial(near_kernel, layer),
        name=("near_low", "near_own", "near_high")[layer],
        out_shape=jax.ShapeDtypeStruct((N, B * M), jnp.float32),
        in_specs=[pl.BlockSpec(memory_space=pltpu.SMEM)] + [vmem()] * (len(operands) - 1),
        out_specs=vmem(),
        scratch_shapes=[
            pltpu.VMEM((B // QUAD, 3 * M, M), jnp.bfloat16),
            pltpu.VMEM((B // QUAD, M, QUAD * M), jnp.bfloat16),
        ],
        compiler_params=pltpu.CompilerParams(vmem_limit_bytes=VMEM_BYTES),
        cost_estimate=pl.CostEstimate(
            flops=7_000_000_000, bytes_accessed=2_000_000, transcendentals=9_000_000
        ),
    )(*operands)


def relay_kernel(transfer_ref, coupling_ref, links_ref, coupling_t_ref, flat_ref, pair_ref):
    lower = lax.broadcasted_iota(jnp.int32, (K // 2, 2 * K), 1) < K

    def unpack(ref):
        for i in range(K // 2):
            flat_ref[pl.ds(i, ref.shape[0], stride=K // 2), :] = ref[
                :, 2 * K * i : 2 * K * (i + 1)
            ].astype(jnp.float32)

    def join(left, right):
        one = flat_ref[left * (K // 2) : (left + 1) * (K // 2), :]
        two = flat_ref[right * (K // 2) : (right + 1) * (K // 2), :]
        pair_ref[pl.ds(0, K // 2, stride=2), :] = jnp.where(lower, one, pltpu.roll(two, K, 1))
        pair_ref[pl.ds(1, K // 2, stride=2), :] = jnp.where(lower, pltpu.roll(one, K, 1), two)
        return pair_ref[...]

    unpack(transfer_ref)
    for p in range(PAIRS - 1):
        links_ref[p] = join(2 * p + 1, 2 * p + 2).astype(jnp.bfloat16)
    links_ref[PAIRS - 1] = join(0, 0).astype(jnp.bfloat16)
    unpack(coupling_ref)
    for p in range(coupling_ref.shape[0] // 2):
        both = jnp.transpose(join(2 * p, 2 * p + 1)).astype(jnp.bfloat16)
        coupling_t_ref[2 * p] = both[0:K]
        coupling_t_ref[2 * p + 1] = both[K : 2 * K]


def relay(transfer, coupling):
    return pl.pallas_call(
        relay_kernel,
        name="relay",
        out_shape=[
            jax.ShapeDtypeStruct((PAIRS, K, 2 * K), jnp.bfloat16),
            jax.ShapeDtypeStruct((coupling.shape[0], K, K), jnp.bfloat16),
        ],
        in_specs=[vmem()] * 2,
        out_specs=[vmem()] * 2,
        scratch_shapes=[
            pltpu.VMEM(((TB + 1) * K // 2, 2 * K), jnp.float32),
            pltpu.VMEM((K, 2 * K), jnp.float32),
        ],
        compiler_params=pltpu.CompilerParams(vmem_limit_bytes=16 << 20),
        cost_estimate=pl.CostEstimate(flops=1000, bytes_accessed=100_000, transcendentals=0),
    )(transfer, coupling)


def counts_kernel(
    place_ref, far_src_ref, far_cls_ref, top_src_ref, top_cls_ref, a_ref, col_ref, cls_ref
):
    classes = a_ref.shape[0]
    width = a_ref.shape[2]
    height = width // 2
    place = place_ref[0]
    subtrees = top_src_ref.shape[0] * 2 // 3

    def column(source):
        owner = jnp.floor((source.astype(jnp.float32) + 0.5) * (1.0 / TB)).astype(jnp.int32)
        slot = source - TB * owner
        count = jnp.ones_like(slot)
        for bit in range(1, 7):
            count = jnp.where(slot + 1 >= 2**bit, 2**bit, count)
        pairs = count >> 1
        first = pairs - 1
        inside = (slot - (count - 1)) >> 1
        rim_first = jnp.where(count <= 16, first, jnp.where(count == 32, 14, 21))
        side = owner - place
        low = PAIRS + rim_first + inside - (pairs - jnp.minimum(pairs, 7))
        row = jnp.where(
            side == 0, first + inside, jnp.where(side < 0, low, PAIRS + RIM + rim_first + inside)
        )
        return jnp.where(source >= 0, row + ((slot + 1) & 1) * height, -1)

    base = PAIRS + 2 * RIM
    last = PAIRS - 1
    for parity in range(2):
        rows = pl.ds(1 + parity, last, stride=2)
        col_ref[parity * PAIRS : parity * PAIRS + last, :] = column(far_src_ref[rows, :])
        cls_ref[parity * PAIRS : parity * PAIRS + last, :] = far_cls_ref[rows, :]
    root, top = pl.ds(place, 1), pl.ds(subtrees + (place >> 1), 1)
    roots, tops = top_src_ref[root, :], top_src_ref[top, :]
    col_ref[last : last + 1, :] = jnp.where(roots >= 0, base + roots, -1)
    col_ref[PAIRS + last : PAIRS + last + 1, :] = jnp.where(
        tops >= 0, height + base + 2 * tops, -1
    )
    cls_ref[last : last + 1, :] = top_cls_ref[root, :]
    cls_ref[PAIRS + last : PAIRS + last + 1, :] = top_cls_ref[top, :]

    slots = col_ref.shape[1]
    spread = slots * 8
    lane = lax.broadcasted_iota(jnp.int32, (slots, spread), 1)
    copies = (lane // 8 == lax.broadcasted_iota(jnp.int32, (slots, spread), 0)).astype(jnp.float32)
    columns = lax.broadcasted_iota(jnp.int32, (8, width), 1)
    match = (
        lax.broadcasted_iota(jnp.int32, (8, spread), 1) % 8
        == lax.broadcasted_iota(jnp.int32, (8, spread), 0)
    )

    def block(g, carry):
        halves = []
        for h in range(2):
            rows = pl.ds(pl.multiple_of(g * 16 + h * 8, 8), 8)
            col = col_ref[rows, :]
            wide = dot(cls_ref[rows, :].astype(jnp.float32), copies).astype(jnp.int32)
            wide = jnp.where(match, wide, -1)
            left = jnp.concatenate(
                [jnp.where(wide == c, 1.0, 0.0) for c in range(classes)], axis=0
            ).astype(jnp.bfloat16)
            right = jnp.concatenate(
                [jnp.where(col[:, e : e + 1] == columns, 1.0, 0.0) for e in range(slots)], axis=0
            ).astype(jnp.bfloat16)
            halves.append(dot(left, right))
        for c in range(classes):
            both = jnp.concatenate([half[8 * c : 8 * c + 8] for half in halves], axis=0)
            a_ref[c, pl.ds(pl.multiple_of(g * 16, 16), 16), :] = both.astype(jnp.bfloat16)
        return carry

    lax.fori_loop(0, 2 * PAIRS // 16, block, 0)


def class_counts(place, far_src, far_cls, top_src, top_cls, class_count, width):
    return pl.pallas_call(
        counts_kernel,
        name="class_counts",
        out_shape=jax.ShapeDtypeStruct((class_count, 2 * PAIRS, width), jnp.bfloat16),
        in_specs=[pl.BlockSpec(memory_space=pltpu.SMEM)] + [vmem()] * 4,
        out_specs=vmem(),
        scratch_shapes=[pltpu.VMEM((2 * PAIRS, far_src.shape[1]), jnp.int32)] * 2,
        compiler_params=pltpu.CompilerParams(vmem_limit_bytes=20 << 20),
        cost_estimate=pl.CostEstimate(flops=1000, bytes_accessed=100_000, transcendentals=0),
    )(place, far_src, far_cls, top_src, top_cls)


FIRST_ROWS = tuple(range(14)) + tuple(range(15, 22)) + tuple(range(31, 38))
LAST_ROWS = tuple(range(7)) + tuple(range(8, 15)) + tuple(range(24, 31)) + tuple(range(56, 63))
RIM_ROWS = 32


def links_of(links_ref, pair_index):
    return jnp.concatenate([links_ref[2 * pair_index + 1], links_ref[2 * pair_index + 2]], axis=0)


def up_kernel(
    values_ref, basis_ref, links_ref, out_ref, first_ref, last_ref, root_ref, cs_ref, fs_ref, ls_ref
):
    lower = lax.broadcasted_iota(jnp.int32, (N, 2 * K), 1) < K

    def keep(pair_index, tile):
        cs_ref[pl.ds(pair_index, N, stride=PAIRS), :] = tile
        for rows, ref in ((FIRST_ROWS, fs_ref), (LAST_ROWS, ls_ref)):
            if pair_index in rows:
                ref[pl.ds(rows.index(pair_index), N, stride=RIM_ROWS), :] = tile

    def lift(stacked, matrix):
        both = dot(stacked, matrix, NT)
        return jnp.where(lower, both[:N], both[N:]).astype(jnp.bfloat16)

    tiles = {}
    for i in range(B // 2):
        stacked = jnp.concatenate(
            [values_ref[:, 2 * i * M : (2 * i + 1) * M], values_ref[:, (2 * i + 1) * M : (2 * i + 2) * M]],
            axis=0,
        )
        tiles[B // 2 - 1 + i] = lift(stacked, basis_ref[i])
        keep(B // 2 - 1 + i, tiles[B // 2 - 1 + i].astype(jnp.float32))
    for j in reversed(range(B // 2 - 1)):
        stacked = jnp.concatenate([tiles[2 * j + 1], tiles[2 * j + 2]], axis=0)
        tiles[j] = lift(stacked, links_of(links_ref, j))
        keep(j, tiles[j].astype(jnp.float32))
    root = dot(tiles[0], links_ref[0], NT).astype(jnp.bfloat16)
    up = dot(root, links_ref[PAIRS - 1][:, 0:K], NT)
    last = jnp.concatenate([root.astype(jnp.float32), up], axis=1)
    keep(PAIRS - 1, last)
    root_ref[...] = last.astype(jnp.bfloat16)
    for ref in (first_ref, last_ref):
        ref[N, 0:N, :] = last.astype(jnp.bfloat16)
        ref[N, N:RIM_ROWS, :] = jnp.zeros((RIM_ROWS - N, 2 * K), jnp.bfloat16)
    for n in range(N):
        out_ref[n] = cs_ref[n * PAIRS : (n + 1) * PAIRS, :].astype(jnp.bfloat16)
        for source, target in ((fs_ref, first_ref), (ls_ref, last_ref)):
            base = n * RIM_ROWS
            source[base + RIM : base + RIM_ROWS, :] = jnp.zeros((RIM_ROWS - RIM, 2 * K), jnp.float32)
            target[n] = source[base : base + RIM_ROWS, :].astype(jnp.bfloat16)


def upward(values, basis, links):
    return pl.pallas_call(
        up_kernel,
        name="upward",
        out_shape=[
            jax.ShapeDtypeStruct((N, PAIRS, 2 * K), jnp.bfloat16),
            jax.ShapeDtypeStruct((N + 1, RIM_ROWS, 2 * K), jnp.bfloat16),
            jax.ShapeDtypeStruct((N + 1, RIM_ROWS, 2 * K), jnp.bfloat16),
            jax.ShapeDtypeStruct((N, 2 * K), jnp.bfloat16),
        ],
        in_specs=[vmem()] * 3,
        out_specs=[vmem()] * 4,
        scratch_shapes=[
            pltpu.VMEM((N * PAIRS, 2 * K), jnp.float32),
            pltpu.VMEM((N * RIM_ROWS, 2 * K), jnp.float32),
            pltpu.VMEM((N * RIM_ROWS, 2 * K), jnp.float32),
        ],
        compiler_params=pltpu.CompilerParams(vmem_limit_bytes=20 << 20),
        cost_estimate=pl.CostEstimate(
            flops=300_000_000, bytes_accessed=3_000_000, transcendentals=0
        ),
    )(values, basis, links)


def down_kernel(
    place_ref,
    low_ref,
    own_ref,
    high_ref,
    a_ref,
    coupling_ref,
    links_ref,
    basis_ref,
    near_ref,
    *rest,
):
    tops_refs, (out_ref, cf_ref, call_ref, bd_ref, lhs_ref, fs_ref) = rest[:-6], rest[-6:]
    classes = a_ref.shape[0]
    height = a_ref.shape[2] // 2
    subtrees = sum(ref.shape[0] for ref in tops_refs)
    lower = lax.broadcasted_iota(jnp.int32, (N, 2 * K), 1) < K

    used = PAIRS + 2 * RIM + subtrees
    for n in range(N):
        base = n * height
        cf_ref[base : base + PAIRS, :] = own_ref[n].astype(jnp.float32)
        at = base + PAIRS
        cf_ref[at : at + RIM, :] = low_ref[n].astype(jnp.float32)[:RIM]
        at += RIM
        cf_ref[at : at + RIM, :] = high_ref[n].astype(jnp.float32)[:RIM]
        if used < height:
            cf_ref[base + used : base + height, :] = jnp.zeros((height - used, 2 * K), jnp.float32)
    duos = [(ref, i) for ref in tops_refs for i in range(0, ref.shape[0], 2)]
    for m, (ref, i) in enumerate(duos):
        even = ref[i].astype(jnp.float32)
        odd = ref[i + 1].astype(jnp.float32)
        at = PAIRS + 2 * RIM + 2 * ((place_ref[0] // 2) ^ m)
        cf_ref[pl.ds(at, N, stride=height), :] = jnp.where(lower, even, even + odd)
        cf_ref[pl.ds(at + 1, N, stride=height), :] = odd
    wide_lower = lax.broadcasted_iota(jnp.int32, (height, 2 * K), 1) < K
    for m in range(N // 2):
        one = cf_ref[2 * m * height : (2 * m + 1) * height, :]
        two = cf_ref[(2 * m + 1) * height : (2 * m + 2) * height, :]
        lanes = slice(m * 2 * K, (m + 1) * 2 * K)
        call_ref[0:height, lanes] = jnp.where(
            wide_lower, one, pltpu.roll(two, K, 1)
        ).astype(jnp.bfloat16)
        call_ref[height : 2 * height, lanes] = jnp.where(
            wide_lower, pltpu.roll(one, K, 1), two
        ).astype(jnp.bfloat16)

    def spread(c, carry):
        s = coupling_ref[c]
        z = jnp.zeros((K, K), jnp.bfloat16)
        at = pl.multiple_of(c * 4 * K, 4 * K)
        for block in range(4):
            place = (0, 2, 1, 3)[block]
            bd_ref[pl.ds(at + block * K, K), :] = jnp.concatenate(
                [s if place == i else z for i in range(4)], axis=1
            )
        return carry

    lax.fori_loop(0, classes, spread, 0)

    def group(c, carry):
        grouped = dot(a_ref[c], call_ref[...]).astype(jnp.bfloat16)
        for parity in range(2):
            lanes = pl.ds(pl.multiple_of((2 * c + parity) * 2 * K, 2 * K), 2 * K)
            for m in range(N // 2):
                lhs_ref[m * PAIRS : (m + 1) * PAIRS, lanes] = grouped[
                    parity * PAIRS : (parity + 1) * PAIRS, m * 2 * K : (m + 1) * 2 * K
                ]
        return carry

    lax.fori_loop(0, classes, group, 0, unroll=2)

    some = N // 4 * PAIRS

    def couple(half, carry):
        field = dot(lhs_ref[pl.ds(pl.multiple_of(half * some, some), some), :], bd_ref[...])
        for i in range(N // 4):
            at = pl.multiple_of(2 * half * some + 2 * i * PAIRS, PAIRS)
            rows = slice(i * PAIRS, (i + 1) * PAIRS)
            fs_ref[pl.ds(at, PAIRS), :] = field[rows, 0 : 2 * K]
            fs_ref[pl.ds(at + PAIRS, PAIRS), :] = field[rows, 2 * K : 4 * K]
        return carry

    lax.fori_loop(0, 2, couple, 0)

    def field_of(pair_index):
        return fs_ref[pl.ds(pair_index, N, stride=PAIRS), :]

    def push(tile, matrix):
        none = jnp.zeros_like(tile)
        stacked = jnp.concatenate(
            [jnp.where(lower, tile, none), jnp.where(lower, none, tile)], axis=0
        ).astype(jnp.bfloat16)
        return dot(stacked, matrix)

    last = field_of(PAIRS - 1)
    top = last[:, K : 2 * K].astype(jnp.bfloat16)
    root = (last[:, 0:K] + dot(top, links_ref[PAIRS - 1][:, 0:K])).astype(jnp.bfloat16)
    tiles = {0: field_of(0) + dot(root, links_ref[0])}
    for j in range(B // 2 - 1):
        both = push(tiles[j], links_of(links_ref, j))
        tiles[2 * j + 1] = field_of(2 * j + 1) + both[:N]
        tiles[2 * j + 2] = field_of(2 * j + 2) + both[N:]
    for i in range(B // 2):
        both = push(tiles[B // 2 - 1 + i], basis_ref[i])
        for h in range(2):
            lanes = slice((2 * i + h) * M, (2 * i + h + 1) * M)
            out_ref[:, lanes] = (near_ref[:, lanes] + both[h * N : (h + 1) * N]).astype(jnp.bfloat16)


def downward(place, low, own, high, counts, coupling, links, basis, near, tops):
    classes = counts.shape[0]
    height = counts.shape[2] // 2
    return pl.pallas_call(
        down_kernel,
        name="downward",
        out_shape=jax.ShapeDtypeStruct((N, B * M), jnp.bfloat16),
        in_specs=[pl.BlockSpec(memory_space=pltpu.SMEM)] + [vmem()] * (8 + len(tops)),
        out_specs=vmem(),
        scratch_shapes=[
            pltpu.VMEM((N * height, 2 * K), jnp.float32),
            pltpu.VMEM((2 * height, N * K), jnp.bfloat16),
            pltpu.VMEM((classes * 4 * K, 4 * K), jnp.bfloat16),
            pltpu.VMEM((N // 2 * PAIRS, classes * 4 * K), jnp.bfloat16),
            pltpu.VMEM((N * PAIRS, 2 * K), jnp.float32),
        ],
        compiler_params=pltpu.CompilerParams(vmem_limit_bytes=40 << 20),
        cost_estimate=pl.CostEstimate(
            flops=4_000_000_000, bytes_accessed=6_000_000, transcendentals=0
        ),
    )(place, low, own, high, counts, coupling, links, basis, near, *tops)


def per_device(
    values, coords, basis, transfer, coupling, near_src, far_src, far_cls, top_src, top_cls
):
    position = lax.axis_index("leaf")
    subtrees = lax.axis_size("leaf")
    class_count = coupling.shape[0]
    height = -(-(PAIRS + 2 * RIM + subtrees) // 64) * 64

    whole_basis = lax.all_gather(basis, "vec", axis=0, tiled=True)

    place = jnp.full((1,), 0, jnp.int32) + position
    middle = (ROW / 2, B // ROW / 2, position.astype(jnp.float32) + 0.5)
    centre = jnp.stack([jnp.asarray(x, jnp.float32) for x in middle])
    packed, for_high, for_low, targets = pack(centre, values, coords)

    links, coupling_t = relay(transfer, coupling)
    forward = [(i, i + 1) for i in range(subtrees - 1)]
    backward = [(i + 1, i) for i in range(subtrees - 1)]
    from_low = lax.ppermute(for_high, "leaf", forward)
    from_high = lax.ppermute(for_low, "leaf", backward)
    counts = class_counts(place, far_src, far_cls, top_src, top_cls, class_count, 2 * height)

    basis_pairs = whole_basis.reshape(B // 2, 2 * K, M)
    coefs, first, last, root = upward(values, basis_pairs, links)
    low = lax.ppermute(last, "leaf", forward)
    high = lax.ppermute(first, "leaf", backward)
    packed, coefs = lax.optimization_barrier((packed, coefs))
    near = near_field(1, near_src, packed, targets)

    is_even = position % 2 == 0
    other = jnp.where(is_even, high[N, :N], low[N, :N])
    duo = jnp.where(is_even, jnp.stack([root, other]), jnp.stack([other, root]))
    tops = [duo]
    layers = [(0, from_low), (2, from_high)]
    step = 2
    while step < subtrees:
        known = jnp.concatenate(tops, axis=0) if len(tops) > 1 else duo
        known, near = lax.optimization_barrier((known, near))
        tops.append(lax.ppermute(known, "leaf", [(i, i ^ step) for i in range(subtrees)]))
        if layers:
            layer, source = layers.pop(0)
            near = near_field(layer, near_src, source, targets, near)
        step *= 2
    for layer, source in layers:
        near = near_field(layer, near_src, source, targets, near)
    return downward(
        place, low, coefs, high, counts, coupling_t, links, basis_pairs, near, tops
    )


def solution(mesh):
    in_specs = (
        P("vec", "leaf"),
        P(None, "leaf"),
        P(("leaf", "vec"), None, None),
        P("leaf", None),
        P(),
        P("leaf", None),
        P("leaf", None),
        P("leaf", None),
        P(),
        P(),
    )
    out_specs = P("vec", "leaf")
    return jax.shard_map(
        per_device, mesh=mesh, in_specs=in_specs, out_specs=out_specs, check_vma=False
    )
```
